128 devices in a mesh: batch: 8 (over x, core), proto: 16 (over y, z).
Axes of the slice: x: 4, y: 4, z: 4, core: 2. Of those that a mesh axis runs over, the one named last changes fastest.
Arguments:
- student_feats: bfloat16 [4096, 384], P('batch'), may hold values from -6 to 6
- teacher_feats: bfloat16 [4096, 384], P('batch'), may hold values from -9 to 9
- student_protos: bfloat16 [131072, 384], P('proto'), may hold values from -1 to 1
- teacher_protos: bfloat16 [131072, 384], P('proto'), may hold values from -9 to 9
Outputs:
- grad_proto: bfloat16 [131072, 384], P('proto')
- grad_student: bfloat16 [4096, 384], P('batch')
The draws below stay inside these ranges and needn't reach their ends.
All inputs are finite; a program needn't handle non-finite values.
Results may differ from the reference program's by a relative error of at most 0.0076.
Values may be sent and summed in bfloat16 or wider, within the bound.
A program may use at most 128 MiB of HBM per device.

```python
import jax
import jax.numpy as jnp
from jax import lax

D = 384
PROTO_DEV = 8192
ITERS = 3
TOKENS = 4096
PROTOS = 131072


cluster_count = 64


drawn_spread = 2.0


def shared_centers(key):
    return jax.random.truncated_normal(jax.random.fold_in(key, 101), -3.0, 3.0, (cluster_count, D), jnp.float32)


def draw_teacher_feats(key, part):
    centers = shared_centers(key)
    key = jax.random.fold_in(key, 3)
    ceiling = jax.random.randint(jax.random.fold_in(key, 1), (TOKENS,), 1, cluster_count + 1)
    groups = jax.random.randint(jax.random.fold_in(key, 2), (TOKENS,), 0, ceiling)
    jitter = drawn_spread * jax.random.truncated_normal(jax.random.fold_in(key, 4), -3.0, 3.0, (TOKENS, D), jnp.float32)
    return (centers[groups] + jitter).astype(jnp.bfloat16)


def draw_teacher_protos(key, part):
    centers = shared_centers(key)
    key = jax.random.fold_in(key, 7)
    groups = jnp.arange(PROTOS, dtype=jnp.int32) * cluster_count // PROTOS
    jitter = drawn_spread * jax.random.truncated_normal(jax.random.fold_in(key, 4), -3.0, 3.0, (PROTOS, D), jnp.float32)
    return (centers[groups] + jitter).astype(jnp.bfloat16)


def draw_student_protos(key, part):
    key = jax.random.fold_in(key, 11)
    shard_count = PROTOS // PROTO_DEV
    heading = jax.random.truncated_normal(jax.random.fold_in(key, 1), -3.0, 3.0, (shard_count, D), jnp.float32)
    strength = jax.random.uniform(jax.random.fold_in(key, 2), (shard_count,), jnp.float32, 0.5, 2.0)
    jitter = jax.random.truncated_normal(jax.random.fold_in(key, 3), -3.0, 3.0, (PROTOS, D), jnp.float32)
    owner = jnp.arange(PROTOS) // PROTO_DEV
    rows = (strength[:, None] * heading)[owner] + jitter
    return jnp.clip(rows * D ** (-0.5), -1.0, 1.0).astype(jnp.bfloat16)


def shard_levels(own_key, shape, shards, least, high):
    gain, own = 1.0, jax.random.fold_in(own_key, 6)
    for dim, blocks in shards:
        steps = jnp.exp(jax.random.uniform(jax.random.fold_in(own, dim), (blocks,), jnp.float32, least / len(shards), high / len(shards)))
        gain = gain * jnp.repeat(steps, shape[dim] // blocks).reshape([-1 if axis == dim else 1 for axis in range(len(shape))])
    return gain


def normal_values(key, dims, scale, most, cuts=(), held_as=jnp.bfloat16):
    loudness = shard_levels(key, dims, cuts, -0.22, 0.18) if cuts else 1.0
    values = jax.random.normal(key, dims, jnp.float32) * scale * loudness
    return jnp.minimum(jnp.maximum(values, -most), most).astype(held_as)


def setup_inputs(seed: int = 0) -> dict:
    streams_of = jax.random.split(jax.random.key(seed), 5)
    return {
        "student_feats": normal_values(streams_of[0], (TOKENS, D), 1.0, 6.0, ((0, 8),)),
        "teacher_feats": draw_teacher_feats(jax.random.fold_in(streams_of[4], 71), 0),
        "student_protos": draw_student_protos(jax.random.fold_in(streams_of[4], 71), 0),
        "teacher_protos": draw_teacher_protos(jax.random.fold_in(streams_of[4], 71), 0),
    }


eps = 1e-06
teacher_temp = 0.04
student_temp = 0.1

def unit_rows(matrix):
    values = matrix.astype(jnp.float32)
    scale = lax.rsqrt(lax.optimization_barrier(jnp.sum(values * values, axis=1, keepdims=True)) + eps)
    return (values * scale, scale)

def similar(left, right):
    return lax.dot_general(left, right, (((1,), (1,)), ((), ())), preferred_element_type=jnp.float32)

def back_norm(grad, unit, scale):
    return scale * (grad - unit * lax.optimization_barrier(jnp.sum(grad * unit, axis=1, keepdims=True)))

def reference(student_feats, teacher_feats, student_protos, teacher_protos):
    stud_float, stud_scale = unit_rows(student_feats)
    teach_float, teach_scale = unit_rows(teacher_feats)
    proto_float, proto_scale = unit_rows(student_protos)
    anchor_float, anchor_scale = unit_rows(teacher_protos)
    stud_unit = stud_float.astype(jnp.bfloat16)
    teach_unit = teach_float.astype(jnp.bfloat16)
    proto_unit = proto_float.astype(jnp.bfloat16)
    anchor_unit = anchor_float.astype(jnp.bfloat16)
    tok_all = student_feats.shape[0]
    proto_all = student_protos.shape[0]
    teach_exp = jnp.exp(similar(teach_unit, anchor_unit) / teacher_temp)
    row_weight = jnp.ones((tok_all,), jnp.float32)
    col_weight = jnp.ones((proto_all,), jnp.float32)
    for sweep in range(ITERS):
        col_weight = 1.0 / (proto_all * lax.optimization_barrier(jnp.sum(teach_exp * row_weight[:, None], axis=0)))
        row_weight = 1.0 / (tok_all * lax.optimization_barrier(jnp.sum(teach_exp * col_weight[None, :], axis=1)))
    targets = tok_all * teach_exp * row_weight[:, None] * col_weight[None, :]
    logits = similar(stud_unit, proto_unit) / student_temp
    exp_logits = jnp.exp(logits)
    total = lax.optimization_barrier(jnp.sum(exp_logits, axis=1))
    delta = ((exp_logits / total[:, None] - targets) / (student_temp * tok_all)).astype(jnp.bfloat16)
    proto_back = lax.dot_general(delta, stud_unit, (((0,), (0,)), ((), ())), preferred_element_type=jnp.float32)
    grad_proto = back_norm(proto_back, proto_float, proto_scale).astype(jnp.bfloat16)
    feat_back = jnp.dot(delta, proto_unit, preferred_element_type=jnp.float32)
    grad_student = back_norm(feat_back, stud_float, stud_scale).astype(jnp.bfloat16)
    return (grad_proto, grad_student)
```

```python
import jax
import jax.numpy as jnp
from jax import lax
from jax.sharding import PartitionSpec as P

ITERS = 3


eps = 1e-06
teacher_temp = 0.04
student_temp = 0.1


def unit_rows(matrix):
    values = matrix.astype(jnp.float32)
    scale = lax.rsqrt(jnp.sum(values * values, axis=1, keepdims=True) + eps)
    return (values * scale, scale)


def similar(left, right):
    return lax.dot_general(
        left, right, (((1,), (1,)), ((), ())), preferred_element_type=jnp.float32
    )


def back_norm(grad, unit, scale):
    return scale * (grad - unit * jnp.sum(grad * unit, axis=1, keepdims=True))


def on_device(student_feats, teacher_feats, student_protos, teacher_protos):
    parts = lax.axis_size("batch")
    tok_all = student_feats.shape[0] * parts
    proto_all = student_protos.shape[0] * lax.axis_size("proto")
    mine = student_protos.shape[0] // parts
    start = lax.axis_index("batch") * mine
    student_protos = lax.dynamic_slice_in_dim(student_protos, start, mine)
    teacher_protos = lax.dynamic_slice_in_dim(teacher_protos, start, mine)
    stud_float, stud_scale = unit_rows(student_feats)
    teach_float, _ = unit_rows(teacher_feats)
    proto_float, proto_scale = unit_rows(student_protos)
    anchor_float, _ = unit_rows(teacher_protos)
    teach_unit = lax.all_gather(teach_float.astype(jnp.bfloat16), "batch", tiled=True)
    stud_unit = lax.all_gather(stud_float.astype(jnp.bfloat16), "batch", tiled=True)
    proto_unit = proto_float.astype(jnp.bfloat16)
    anchor_unit = anchor_float.astype(jnp.bfloat16)
    teach_exp = jnp.exp(similar(anchor_unit, teach_unit) / teacher_temp)
    exp_logits = jnp.exp(similar(proto_unit, stud_unit) / student_temp)
    row_weight = jnp.ones((tok_all,), jnp.float32)
    for sweep in range(ITERS):
        col_sum = jnp.sum(teach_exp * row_weight[None, :], axis=1)
        col_weight = 1.0 / (proto_all * col_sum)
        row_part = jnp.sum(teach_exp * col_weight[:, None], axis=0)
        if sweep == ITERS - 1:
            row_part = jnp.stack([row_part, jnp.sum(exp_logits, axis=0)])
            row_part, total = lax.psum(row_part, ("batch", "proto"))
        else:
            row_part = lax.psum(row_part, ("batch", "proto"))
        row_weight = 1.0 / (tok_all * row_part)
    targets = tok_all * teach_exp * row_weight[None, :] * col_weight[:, None]
    delta = ((exp_logits / total[None, :] - targets) / (student_temp * tok_all)).astype(
        jnp.bfloat16
    )
    proto_back = jnp.dot(delta, stud_unit, preferred_element_type=jnp.float32)
    grad_proto = back_norm(proto_back, proto_float, proto_scale).astype(jnp.bfloat16)
    grad_proto = lax.all_gather(grad_proto, "batch", tiled=True)
    feat_back = lax.dot_general(
        delta, proto_unit, (((0,), (0,)), ((), ())), preferred_element_type=jnp.float32
    )
    feat_back = lax.psum_scatter(feat_back, "batch", tiled=True)
    feat_back = lax.psum(feat_back, "proto")
    grad_student = back_norm(feat_back, stud_float, stud_scale).astype(jnp.bfloat16)
    return (grad_proto, grad_student)


def solution(mesh):
    in_specs = (P("batch", None), P("batch", None), P("proto", None), P("proto", None))
    out_specs = (P("proto", None), P("batch", None))
    return jax.shard_map(
        on_device, mesh=mesh, in_specs=in_specs, out_specs=out_specs, check_vma=False
    )
```

```python
import functools

import jax
import jax.numpy as jnp
from jax import lax
from jax.experimental import pallas as pl
from jax.experimental.pallas import tpu as pltpu
from jax.sharding import PartitionSpec as P

ITERS = 3
eps = 1e-06
teacher_temp = 0.04
student_temp = 0.1
LOG2E = 1.4426950408889634
F32 = jnp.float32
BF = jnp.bfloat16
MESH = pl.DeviceIdType.MESH
CH = 128


def nt(left, right):
    return lax.dot_general(
        left, right, (((1,), (1,)), ((), ())), preferred_element_type=F32
    )


def nn(left, right):
    return jnp.dot(left, right, preferred_element_type=F32)


def tn(left, right):
    return lax.dot_general(
        left, right, (((0,), (0,)), ((), ())), preferred_element_type=F32
    )


def loop(count, body):
    def step(i, carry):
        body(i)
        return carry

    lax.fori_loop(0, count, step, 0)


def rows(start, size):
    return pl.ds(pl.multiple_of(start, size), size)


def unit_rows(values):
    values = values.astype(F32)
    scale = lax.rsqrt(jnp.sum(values * values, axis=1, keepdims=True) + eps)
    return values * scale, scale


def back_norm(grad, unit, scale):
    return scale * (grad - unit * jnp.sum(grad * unit, axis=1, keepdims=True))


def kernel(
    nb, nq,
    sf, tf, sp_hbm, tp_hbm,
    gp_out, gs_out,
    t_all, s_all, sp, anchor, pu, e, s, cs, tot, fa, fb, fbb, st, sr, gpb, ccol,
    r16, c16, w_src, w_mid, w_g1, w_g2, w_out, cx, yzr, sumf, xs, xr, gsb,
    lsem, t_s, t_r, tf_s, tf_r, s_s, s_r, sf_s, sf_r,
    a1_s, a1_r, a2_s, a2_r, g_s, g_r, f_s, f_r, sib_s, sib_r, own_s,
    cx_s, cx_r, yz_s, yz_r, xr_s, xr_r, gs_s, gs_r,
):
    nx = nb // 2
    tl, depth = sf.shape
    tokens = tl * nb
    pl_rows = sp.shape[0]
    protos = pl_rows * nb * nq
    chunks = pl_rows // CH
    wide = tokens // 128
    piece = tl // nq
    plane = 2 * tl
    b, p = lax.axis_index("batch"), lax.axis_index("proto")
    x, c = b // 2, lax.rem(b, 2)

    def bat(dx, dc):
        return lax.rem(x + dx, nx) * 2 + lax.rem(c + dc, 2)

    def remote(src, dst, ss, rs, to):
        return pltpu.make_async_remote_copy(
            src, dst, ss, rs, device_id=to, device_id_type=MESH
        )

    sibling = (bat(0, 1), p)

    barrier = pltpu.get_barrier_semaphore()
    for j in range(1, nb):
        pl.semaphore_signal(
            barrier, inc=1, device_id=(lax.rem(b + j, nb), p), device_id_type=MESH
        )
    for j in range(1, nq):
        pl.semaphore_signal(
            barrier, inc=1, device_id=(b, lax.rem(p + j, nq)), device_id_type=MESH
        )
    load_t = pltpu.make_async_copy(tp_hbm.at[rows(b * pl_rows, pl_rows)], anchor, lsem.at[0])
    load_s = pltpu.make_async_copy(sp_hbm.at[rows(b * pl_rows, pl_rows)], sp, lsem.at[1])
    load_t.start()
    load_s.start()

    def norm_into(src, dst, start, count):
        def body(i):
            unit, _ = unit_rows(src[rows(i * 128, 128), :])
            dst[rows(start + i * 128, 128), :] = unit.astype(BF)

        loop(count // 128, body)

    norm_into(tf, t_all, b * tl, tl)
    pl.semaphore_wait(barrier, nb + nq - 2)

    def sends(buf, ss, rs):
        mine = buf.at[rows(b * tl, tl)]
        out = [remote(mine, mine, ss.at[0], rs.at[0], sibling)]
        for dx in range(1, nx):
            out.append(remote(mine, mine, ss.at[dx], rs.at[dx], (bat(dx, 0), p)))
        return out

    def forward(buf, ss, rs, dx):
        block = buf.at[rows(bat(nx - dx, 0) * tl, tl)]
        return remote(block, block, ss.at[dx], rs.at[dx], sibling)

    order = [0, 1, nx - 1] + list(range(2, nx - 1))
    order = order[:1] + [d for i, d in enumerate(order[1:]) if d not in order[1:][:i]]
    t_sends = sends(t_all, t_s, t_r)
    for dx in order:
        t_sends[dx].start()
    norm_into(sf, s_all, b * tl, tl)
    load_t.wait()
    norm_into(anchor, anchor, 0, pl_rows)
    load_s.wait()
    norm_into(sp, pu, 0, pl_rows)

    def exp_plane(left, right, out, dx, factor, accumulate):
        off = lax.rem(x + nx - dx, nx) * plane
        cols = rows(off, plane)

        def body(i):
            sl = rows(i * 256, 256)
            value = jnp.exp2(nt(left[sl, :], right[cols, :]) * factor)
            out[sl, cols] = value.astype(BF)
            accumulate(value, sl, cols, dx)

        loop(pl_rows // 256, body)

    def col_acc(value, sl, cols, dx):
        acc = value[:, 0:128]
        for q in range(1, plane // 128):
            acc = acc + value[:, q * 128 : (q + 1) * 128]
        if dx == 0:
            cs[sl, :] = acc
        else:
            cs[sl, :] += acc

    def row_acc(value, sl, cols, dx):
        tot[:, cols] += jnp.sum(value.reshape(32, 8, plane), axis=0)

    def arrive(buf, ds, ss, rs, fs, fr, dx):
        if dx == 0:
            ds[0].wait_recv()
        else:
            ds[dx].wait_recv()
            forward(buf, fs, fr, dx).start()

    def arrived(buf, fs, fr, dx):
        if dx:
            forward(buf, fs, fr, dx).wait_recv()

    for dx in order:
        arrive(t_all, t_sends, t_s, t_r, tf_s, tf_r, dx)
        arrived(t_all, tf_s, tf_r, dx)
        exp_plane(anchor, t_all, e, dx, LOG2E / teacher_temp, col_acc)
    s_sends = sends(s_all, s_s, s_r)
    for dx in order:
        s_sends[dx].start()

    half = lax.broadcasted_iota(jnp.int32, (16, 128), 0) < 8

    def split_into(dst, j, row):
        high = row.astype(BF).astype(F32)
        dst[:, j * 128 : (j + 1) * 128] = jnp.where(half, high, row - high).astype(BF)

    def reduce_start(n, height):
        h = slice(0, height)
        ds = [
            remote(w_src.at[n, h], w_g1.at[n, j - 1, h], a1_s.at[n, j - 1],
                   a1_r.at[n, j - 1], (lax.rem(b + j, nb), p))
            for j in range(1, nb)
        ]
        for d in ds:
            d.start()
        return ds

    def reduce_middle(n, height, ds):
        h = slice(0, height)
        for d in ds:
            d.wait_recv()
        value = w_src[n, h]
        for j in range(nb - 1):
            value = value + w_g1[n, j, h]
        w_mid[n, h] = value
        out = [
            remote(w_mid.at[n, h], w_g2.at[n, j - 1, h], a2_s.at[n, j - 1],
                   a2_r.at[n, j - 1], (b, lax.rem(p + j, nq)))
            for j in range(1, nq)
        ]
        for d in out:
            d.start()
        return out

    def reduce_end(n, height, ds):
        h = slice(0, height)
        for d in ds:
            d.wait_recv()
        value = w_mid[n, h]
        for j in range(nq - 1):
            value = value + w_g2[n, j, h]
        return value

    def col_weights(j, sums):
        return 1.0 / (protos * sums)

    def row_pass(n):
        out = nn(c16[...], e[...])
        line = out[0:1, :] + out[8:9, :]
        for j in range(wide):
            w_src[n, j : j + 1, :] = line[:, j * 128 : (j + 1) * 128]

    def col_pass(weights):
        for j in range(wide):
            split_into(r16, j, weights[j : j + 1, :])
        out = nt(r16[...], e[...])
        line = 1.0 / (protos * (out[0:1, :] + out[8:9, :]))
        return [line[:, j * 128 : (j + 1) * 128] for j in range(pl_rows // 128)]

    tot[...] = jnp.zeros_like(tot)

    def student_plane(dx):
        arrived(s_all, sf_s, sf_r, dx)
        exp_plane(pu, s_all, s, dx, LOG2E / student_temp, row_acc)

    pending = []
    for j in range(pl_rows // 128):
        sums = jnp.sum(cs[j * 128 : (j + 1) * 128, :].T, axis=0, keepdims=True)
        split_into(c16, j, 1.0 / (protos * sums))
    row_pass(0)
    ds = reduce_start(0, wide)
    pending += ds
    arrive(s_all, s_sends, s_s, s_r, sf_s, sf_r, 0)
    student_plane(0)
    ds = reduce_middle(0, wide, ds)
    pending += ds
    weights = 1.0 / (tokens * reduce_end(0, wide, ds))
    for dx in order[1:]:
        arrive(s_all, s_sends, s_s, s_r, sf_s, sf_r, dx)
    for j, line in enumerate(col_pass(weights)):
        split_into(c16, j, line)
    row_pass(1)
    ds = reduce_start(1, wide)
    pending += ds
    for dx in order[1:3]:
        student_plane(dx)
    ds = reduce_middle(1, wide, ds)
    pending += ds
    for dx in order[3:]:
        student_plane(dx)
    weights = 1.0 / (tokens * reduce_end(1, wide, ds))
    lines = col_pass(weights)
    for j, line in enumerate(lines):
        split_into(c16, j, line)
    row_pass(2)
    line = jnp.sum(tot[...], axis=0, keepdims=True)
    for j in range(wide):
        w_src[2, wide + j : wide + j + 1, :] = line[:, j * 128 : (j + 1) * 128]
    ds = reduce_start(2, 2 * wide)
    pending += ds
    for j, line in enumerate(lines):
        ccol[j * 128 : (j + 1) * 128, :] = jnp.broadcast_to(line, (128, 128)).T

    def feat_part(left, right, out):
        def body(j):
            cols = rows(j * 512, 512)
            out[cols, :] = tn(left[:, cols], right[...])

        loop(tokens // 512, body)

    feat_part(s, pu, fa)
    ds = reduce_middle(2, 2 * wide, ds)
    pending += ds

    def scale_protos(j):
        sl = rows(j * 128, 128)
        anchor[sl, :] = (ccol[sl, 0:1] * pu[sl, :].astype(F32)).astype(BF)

    loop(pl_rows // 128, scale_protos)
    feat_part(e, anchor, fb)
    value = reduce_end(2, 2 * wide, ds)
    w_out[0:wide, :] = (1.0 / student_temp) / (tokens * value[0:wide])
    w_out[wide : 2 * wide, :] = 1.0 / (student_temp * tokens * value[wide : 2 * wide])

    def apply_weights(j):
        sl = rows(j * 128, 128)
        rcol = jnp.broadcast_to(w_out[pl.ds(j, 1), :], (128, 128)).T[:, 0:1]
        tcol = jnp.broadcast_to(w_out[pl.ds(wide + j, 1), :], (128, 128)).T[:, 0:1]
        stud = s_all[sl, :].astype(F32)
        sr[sl, :] = (stud * rcol).astype(BF)
        st[sl, :] = (stud * tcol).astype(BF)
        fbb[sl, :] = (fa[sl, :] * tcol - fb[sl, :] * rcol).astype(BF)

    loop(wide, apply_weights)

    cx_d = []
    for xx in range(nx):
        d = remote(
            fbb.at[rows((xx * 2 + 1 - c) * tl, tl)], cx.at[xx],
            cx_s.at[xx], cx_r.at[xx], sibling,
        )
        d.start()
        cx_d.append(d)

    def block_rows(block, q):
        return rows(block * pl_rows + q * CH, CH)

    def half_rows(block, q, k):
        return rows(block * pl_rows + q * CH + k * (CH // 2), CH // 2)

    def own_copy(q):
        return pltpu.make_async_copy(
            gpb.at[rows(q * CH, CH)], gp_out.at[block_rows(b, q)], own_s.at[q]
        )

    def chunk_send(q, k):
        to = (bat(1, 0), p) if k == 0 else (bat(nx - 1, 0), p)
        return remote(
            gpb.at[rows(q * CH, CH)], gp_out.at[block_rows(b, q)],
            g_s.at[k, q], g_r.at[k, q], to,
        )

    def chunk_forward(q, k):
        block = bat(nx - 1, 0) if k == 0 else bat(1, 0)
        to = (bat(1, 0), p) if k == 0 else (bat(nx - 1, 0), p)
        part = gp_out.at[half_rows(block, q, k)]
        return remote(part, part, f_s.at[k, q], f_r.at[k, q], to)

    def chunk_sibling(q, k):
        block = bat((0, nx - 1, 1, 2)[k], 0)
        part = gp_out.at[block_rows(block, q)]
        src = gpb.at[rows(q * CH, CH)] if k == 0 else part
        return remote(src, part, sib_s.at[k, q], sib_r.at[k, q], sibling)

    def chunk_compute(q):
        sl = rows(q * CH, CH)
        back = nn(s[sl, :], st[...]) - ccol[sl, 0:1] * nn(e[sl, :], sr[...])
        unit, scale = unit_rows(sp[sl, :])
        gpb[sl, :] = back_norm(back, unit, scale).astype(BF)
        chunk_send(q, 0).start()
        chunk_send(q, 1).start()
        chunk_sibling(q, 0).start()
        own_copy(q).start()

    def chunk_recv(q):
        for k in range(2):
            chunk_send(q, k).wait_recv()
            chunk_forward(q, k).start()
            chunk_sibling(q, 1 + k).start()

    def chunk_last(q):
        for k in range(2):
            chunk_forward(q, k).wait_recv()
        chunk_sibling(q, 3).start()

    loop(3, chunk_compute)

    for d in cx_d:
        d.wait_recv()
    for xx in range(nx):
        def add_sibling(i, xx=xx):
            sl = rows(i * 128, 128)
            mine = fbb[rows((xx * 2 + c) * tl + i * 128, 128), :].astype(F32)
            cx[xx, sl, :] = (mine + cx[xx, sl, :].astype(F32)).astype(BF)

        loop(tl // 128, add_sibling)
    yz_d = []
    for j in range(1, nq):
        d = remote(
            cx.at[:, rows(lax.rem(p + j, nq) * piece, piece), :], yzr.at[j - 1],
            yz_s.at[j - 1], yz_r.at[j - 1], (b, lax.rem(p + j, nq)),
        )
        d.start()
        yz_d.append(d)

    loop(chunks - 3, lambda i: chunk_compute(i + 3))
    loop(chunks, chunk_recv)
    for d in yz_d:
        d.wait_recv()
    value = cx[:, rows(p * piece, piece), :].astype(F32)
    for j in range(nq - 1):
        value = value + yzr[j].astype(F32)
    sumf[...] = value
    xs[...] = value.astype(BF)
    xr_d = []
    for dx in range(1, nx):
        d = remote(
            xs.at[lax.rem(x + dx, nx)], xr.at[dx - 1],
            xr_s.at[dx - 1], xr_r.at[dx - 1], (bat(dx, 0), p),
        )
        d.start()
        xr_d.append(d)
    loop(chunks, chunk_last)
    for d in xr_d:
        d.wait_recv()
    value = sumf[x]
    for dx in range(nx - 1):
        value = value + xr[dx].astype(F32)
    own = rows(p * piece, piece)
    unit, scale = unit_rows(sf[own, :])
    gsb[...] = back_norm(value, unit, scale).astype(BF)
    gs_out[own, :] = gsb[...]
    gs_d = []
    for j in range(1, nq):
        d = remote(
            gsb, gs_out.at[own], gs_s.at[j - 1], gs_r.at[j - 1], (b, lax.rem(p + j, nq))
        )
        d.start()
        gs_d.append(d)

    for d in t_sends + s_sends + pending + cx_d + yz_d + xr_d + gs_d:
        d.wait_send()
    for dx in range(1, nx):
        forward(t_all, tf_s, tf_r, dx).wait_send()
        forward(s_all, sf_s, sf_r, dx).wait_send()

    def drain(q):
        own_copy(q).wait()
        for k in range(2):
            chunk_send(q, k).wait_send()
            chunk_forward(q, k).wait_send()
        for k in range(4):
            chunk_sibling(q, k).wait()

    loop(chunks, drain)
    for d in gs_d:
        d.wait_recv()


def on_device(nb, nq, student_feats, teacher_feats, student_protos, teacher_protos):
    tl, depth = student_feats.shape
    pl_rows = student_protos.shape[0] // nb
    tokens = tl * nb
    chunks = pl_rows // CH
    wide = tokens // 128
    nx = nb // 2
    piece = tl // nq
    vm = pltpu.VMEM
    dma = pltpu.SemaphoreType.DMA
    scratch = [
        vm((tokens, depth), BF),
        vm((tokens, depth), BF),
        vm((pl_rows, depth), BF),
        vm((pl_rows, depth), BF),
        vm((pl_rows, depth), BF),
        vm((pl_rows, tokens), BF),
        vm((pl_rows, tokens), BF),
        vm((pl_rows, 128), F32),
        vm((8, tokens), F32),
        vm((tokens, depth), F32),
        vm((tokens, depth), F32),
        vm((tokens, depth), BF),
        vm((tokens, depth), BF),
        vm((tokens, depth), BF),
        vm((pl_rows, depth), BF),
        vm((pl_rows, 128), F32),
        vm((16, tokens), BF),
        vm((16, pl_rows), BF),
        vm((ITERS, 2 * wide, 128), F32),
        vm((ITERS, 2 * wide, 128), F32),
        vm((ITERS, nb - 1, 2 * wide, 128), F32),
        vm((ITERS, nq - 1, 2 * wide, 128), F32),
        vm((2 * wide, 128), F32),
        vm((nx, tl, depth), BF),
        vm((nq - 1, nx, piece, depth), BF),
        vm((nx, piece, depth), F32),
        vm((nx, piece, depth), BF),
        vm((nx - 1, piece, depth), BF),
        vm((piece, depth), BF),
        dma((2,)),
        dma((nx,)), dma((nx,)), dma((nx,)), dma((nx,)),
        dma((nx,)), dma((nx,)), dma((nx,)), dma((nx,)),
        dma((ITERS, nb - 1)), dma((ITERS, nb - 1)),
        dma((ITERS, nq - 1)), dma((ITERS, nq - 1)),
        dma((2, chunks)), dma((2, chunks)), dma((2, chunks)), dma((2, chunks)),
        dma((4, chunks)), dma((4, chunks)), dma((chunks,)),
        dma((nx,)), dma((nx,)),
        dma((nq - 1,)), dma((nq - 1,)),
        dma((nx - 1,)), dma((nx - 1,)),
        dma((nq - 1,)), dma((nq - 1,)),
    ]
    in_vmem = pl.BlockSpec(memory_space=pltpu.VMEM)
    anywhere = pl.BlockSpec(memory_space=pl.ANY)
    return pl.pallas_call(
        functools.partial(kernel, nb, nq),
        out_shape=[
            jax.ShapeDtypeStruct(student_protos.shape, BF),
            jax.ShapeDtypeStruct(student_feats.shape, BF),
        ],
        in_specs=[in_vmem, in_vmem, anywhere, anywhere],
        out_specs=[anywhere, in_vmem],
        scratch_shapes=scratch,
        compiler_params=pltpu.CompilerParams(
            collective_id=0, has_side_effects=True, vmem_limit_bytes=62 << 20
        ),
        name="prototype_head",
    )(student_feats, teacher_feats, student_protos, teacher_protos)


def solution(mesh):
    nb, nq = mesh.shape["batch"], mesh.shape["proto"]
    in_specs = (P("batch", None), P("batch", None), P("proto", None), P("proto", None))
    out_specs = (P("proto", None), P("batch", None))
    return jax.shard_map(
        functools.partial(on_device, nb, nq),
        mesh=mesh, in_specs=in_specs, out_specs=out_specs, check_vma=False,
    )
```

```python
import functools

import jax
import jax.numpy as jnp
from jax import lax
from jax.experimental import pallas as pl
from jax.experimental.pallas import tpu as pltpu
from jax.sharding import PartitionSpec as P

ITERS = 3
eps = 1e-06
teacher_temp = 0.04
student_temp = 0.1
LOG2E = 1.4426950408889634
F32 = jnp.float32
BF = jnp.bfloat16
MESH = pl.DeviceIdType.MESH
CH = 128


def nt(left, right):
    return lax.dot_general(
        left, right, (((1,), (1,)), ((), ())), preferred_element_type=F32
    )


def nn(left, right):
    return jnp.dot(left, right, preferred_element_type=F32)


def tn(left, right):
    return lax.dot_general(
        left, right, (((0,), (0,)), ((), ())), preferred_element_type=F32
    )


def loop(count, body):
    def step(i, carry):
        body(i)
        return carry

    lax.fori_loop(0, count, step, 0)


def rows(start, size):
    return pl.ds(pl.multiple_of(start, size), size)


def unit_rows(values):
    values = values.astype(F32)
    scale = lax.rsqrt(jnp.sum(values * values, axis=1, keepdims=True) + eps)
    return values * scale, scale


def back_norm(grad, unit, scale):
    return scale * (grad - unit * jnp.sum(grad * unit, axis=1, keepdims=True))


def kernel(
    nb, nq,
    sf_hbm, tf_hbm, sp_hbm, tp_hbm,
    gp_out, gs_out,
    sf, tf, t_all, s_all, sp, anchor, pu, e, s, cs, tot, fa, fb, ra, rb, st, ccol,
    r16, c16, w_src, w_mid, w_g1, w_g2, w_out, cx, yzr, sumf, xs, xr,
    lsem, tok_s, tok_r, fwd_s, fwd_r, spr_s, spr_r,
    a1_s, a1_r, a2_s, a2_r, g_s, g_r, f_s, f_r, sib_s, sib_r,
    ra_s, ra_r, rb_s, rb_r, yz_s, yz_r, xr_s, xr_r, gs_s, gs_r,
):
    nx = nb // 2
    far_dx = nx // 2
    tl, depth = sf.shape
    tokens = tl * nb
    pl_rows = sp.shape[0]
    protos = pl_rows * nb * nq
    chunks = pl_rows // CH
    wide = tokens // 128
    piece = tl // nq
    plane = 2 * tl
    b, p = lax.axis_index("batch"), lax.axis_index("proto")
    x, c = b // 2, lax.rem(b, 2)

    def bat(dx, dc):
        return lax.rem(x + dx, nx) * 2 + lax.rem(c + dc, 2)

    def peer(j):
        return (b, lax.rem(p + j, nq))

    def remote(src, dst, ss, rs, to):
        return pltpu.make_async_remote_copy(
            src, dst, ss, rs, device_id=to, device_id_type=MESH
        )

    sibling = (bat(0, 1), p)

    barrier = pltpu.get_barrier_semaphore()
    for j in range(1, nb):
        pl.semaphore_signal(
            barrier, inc=1, device_id=(lax.rem(b + j, nb), p), device_id_type=MESH
        )
    for j in range(1, nq):
        pl.semaphore_signal(barrier, inc=1, device_id=peer(j), device_id_type=MESH)
    mine = rows(b * pl_rows, pl_rows)
    loads = [
        pltpu.make_async_copy(tf_hbm, tf, lsem.at[0]),
        pltpu.make_async_copy(sf_hbm, sf, lsem.at[1]),
        pltpu.make_async_copy(tp_hbm.at[mine], anchor, lsem.at[2]),
        pltpu.make_async_copy(sp_hbm.at[mine], sp, lsem.at[3]),
    ]
    for d in loads:
        d.start()

    def norm_into(src, dst, start, count):
        def body(i):
            unit, _ = unit_rows(src[rows(i * 128, 128), :])
            dst[rows(start + i * 128, 128), :] = unit.astype(BF)

        loop(count // 128, body)

    loads[0].wait()
    norm_into(tf, t_all, b * tl, tl)
    pl.semaphore_wait(barrier, nb + nq - 2)

    feats = (t_all, s_all)

    def token_copy(f, dx):
        start, size = b * tl, tl
        if dx == far_dx:
            start, size = b * tl + p * piece, piece
        part = feats[f].at[rows(start, size)]
        to = sibling if dx == 0 else (bat(dx, 0), p)
        return remote(part, part, tok_s.at[f, dx], tok_r.at[f, dx], to)

    def spread(f, j):
        part = feats[f].at[rows(bat(nx - far_dx, 0) * tl + p * piece, piece)]
        return remote(part, part, spr_s.at[f, j - 1], spr_r.at[f, j - 1], peer(j))

    def forward(f, dx):
        block = feats[f].at[rows(bat(nx - dx, 0) * tl, tl)]
        return remote(block, block, fwd_s.at[f, dx], fwd_r.at[f, dx], sibling)

    near = (1, nx - 1)

    def tokens_send(f):
        for dx in (far_dx, 0) + near:
            token_copy(f, dx).start()

    def spread_start(f):
        token_copy(f, far_dx).wait_recv()
        for j in range(1, nq):
            spread(f, j).start()

    def spread_end(f):
        for j in range(1, nq):
            spread(f, j).wait_recv()
        forward(f, far_dx).start()

    def near_end(f):
        for dx in near:
            token_copy(f, dx).wait_recv()
            forward(f, dx).start()

    def tokens_drain(f):
        for dx in (far_dx, 0) + (() if f == 0 else near):
            token_copy(f, dx).wait_send()
        for dx in range(1, nx):
            forward(f, dx).wait_send()
        for j in range(1, nq):
            spread(f, j).wait_send()

    tokens_send(0)
    loads[2].wait()
    norm_into(anchor, anchor, 0, pl_rows)

    def exp_plane(left, right, out, dx, factor, accumulate):
        cols = rows(lax.rem(x + nx - dx, nx) * plane, plane)

        def body(i):
            sl = rows(i * 256, 256)
            value = jnp.exp2(nt(left[sl, :], right[cols, :]) * factor)
            out[sl, cols] = value.astype(BF)
            accumulate(value, sl, cols, dx)

        loop(pl_rows // 256, body)

    def col_acc(value, sl, cols, dx):
        acc = value[:, 0:128]
        for q in range(1, plane // 128):
            acc = acc + value[:, q * 128 : (q + 1) * 128]
        if dx == 0:
            cs[sl, :] = acc
        else:
            cs[sl, :] += acc

    def row_acc(value, sl, cols, dx):
        tot[:, cols] += jnp.sum(value.reshape(32, 8, plane), axis=0)

    def teacher_plane(dx):
        if dx:
            forward(0, dx).wait_recv()
        else:
            token_copy(0, 0).wait_recv()
        exp_plane(anchor, t_all, e, dx, LOG2E / teacher_temp, col_acc)

    def student_plane(dx):
        if dx:
            forward(1, dx).wait_recv()
        else:
            token_copy(1, 0).wait_recv()
        exp_plane(pu, s_all, s, dx, LOG2E / student_temp, row_acc)

    loads[1].wait()
    norm_into(sf, s_all, b * tl, tl)
    teacher_plane(0)
    spread_start(0)
    loads[3].wait()
    norm_into(sp, pu, 0, pl_rows)
    tot[...] = jnp.zeros_like(tot)
    for dx in near:
        token_copy(0, dx).wait_send()
    tokens_send(1)
    spread_end(0)
    near_end(0)
    teacher_plane(far_dx)
    teacher_plane(near[0])
    spread_start(1)
    teacher_plane(near[1])
    half = lax.broadcasted_iota(jnp.int32, (16, 128), 0) < 8

    def split_into(dst, j, row):
        high = row.astype(BF).astype(F32)
        dst[:, j * 128 : (j + 1) * 128] = jnp.where(half, high, row - high).astype(BF)

    def reduce_start(n, height):
        h = slice(0, height)
        ds = [
            remote(w_src.at[n, h], w_g1.at[n, j - 1, h], a1_s.at[n, j - 1],
                   a1_r.at[n, j - 1], (lax.rem(b + j, nb), p))
            for j in range(1, nb)
        ]
        for d in ds:
            d.start()
        return ds

    def reduce_middle(n, height, ds):
        h = slice(0, height)
        for d in ds:
            d.wait_recv()
        value = w_src[n, h]
        for j in range(nb - 1):
            value = value + w_g1[n, j, h]
        w_mid[n, h] = value
        out = [
            remote(w_mid.at[n, h], w_g2.at[n, j - 1, h], a2_s.at[n, j - 1],
                   a2_r.at[n, j - 1], peer(j))
            for j in range(1, nq)
        ]
        for d in out:
            d.start()
        return out

    def reduce_end(n, height, ds):
        h = slice(0, height)
        for d in ds:
            d.wait_recv()
        value = w_mid[n, h]
        for j in range(nq - 1):
            value = value + w_g2[n, j, h]
        return value

    def row_pass(n):
        out = nn(c16[...], e[...])
        line = out[0:1, :] + out[8:9, :]
        for j in range(wide):
            w_src[n, j : j + 1, :] = line[:, j * 128 : (j + 1) * 128]

    def col_pass(weights):
        for j in range(wide):
            split_into(r16, j, weights[j : j + 1, :])
        out = nt(r16[...], e[...])
        line = 1.0 / (protos * (out[0:1, :] + out[8:9, :]))
        return [line[:, j * 128 : (j + 1) * 128] for j in range(pl_rows // 128)]

    def feat_out(left, right, buf, base, to, ss, rs):
        def body(xx):
            cols = rows((xx * 2 + 1 - c) * tl, tl)
            sl = rows(base + xx * tl, tl)
            buf[sl, :] = tn(left[:, cols], right[...]).astype(BF)
            feat_copy(buf, base, to, ss, rs, xx).start()

        loop(nx, body)

    def feat_copy(buf, base, to, ss, rs, xx):
        return remote(
            buf.at[rows(base + xx * tl, tl)], to.at[rows(xx * tl, tl)],
            ss.at[xx], rs.at[xx], sibling,
        )

    def feat_own(left, right, out):
        def body(xx):
            cols = rows((xx * 2 + c) * tl, tl)
            out[rows(xx * tl, tl), :] = tn(left[:, cols], right[...])

        loop(nx, body)

    pending = []
    for j in range(pl_rows // 128):
        sums = jnp.sum(cs[j * 128 : (j + 1) * 128, :].T, axis=0, keepdims=True)
        split_into(c16, j, 1.0 / (protos * sums))
    row_pass(0)
    ds = reduce_start(0, wide)
    pending += ds
    student_plane(0)
    spread_end(1)
    ds = reduce_middle(0, wide, ds)
    pending += ds
    student_plane(far_dx)
    near_end(1)
    student_plane(near[0])
    student_plane(near[1])
    tokens_drain(0)
    weights = 1.0 / (tokens * reduce_end(0, wide, ds))
    for j, line in enumerate(col_pass(weights)):
        split_into(c16, j, line)
    row_pass(1)
    line = jnp.sum(tot[...], axis=0, keepdims=True)
    for j in range(wide):
        w_src[1, wide + j : wide + j + 1, :] = line[:, j * 128 : (j + 1) * 128]
    ds = reduce_start(1, 2 * wide)
    pending += ds
    feat_out(s, pu, t_all, 0, ra, ra_s, ra_r)
    ds = reduce_middle(1, 2 * wide, ds)
    pending += ds
    feat_own(s, pu, fa)
    value = reduce_end(1, 2 * wide, ds)
    weights = 1.0 / (tokens * value[0:wide])
    w_out[wide : 2 * wide, :] = 1.0 / (student_temp * tokens * value[wide : 2 * wide])
    lines = col_pass(weights)
    for j, line in enumerate(lines):
        split_into(c16, j, line)
    row_pass(2)
    ds = reduce_start(2, wide)
    pending += ds
    for j, line in enumerate(lines):
        ccol[j * 128 : (j + 1) * 128, :] = jnp.broadcast_to(line, (128, 128)).T

    def scale_protos(j):
        sl = rows(j * 128, 128)
        anchor[sl, :] = (ccol[sl, 0:1] * pu[sl, :].astype(F32)).astype(BF)

    loop(pl_rows // 128, scale_protos)
    feat_out(e, anchor, t_all, nx * tl, rb, rb_s, rb_r)
    ds = reduce_middle(2, wide, ds)
    pending += ds
    feat_own(e, anchor, fb)

    def column(j):
        return jnp.broadcast_to(w_out[pl.ds(j, 1), :], (128, 128)).T[:, 0:1]

    def student_weights(j):
        sl = rows(j * 128, 128)
        st[sl, :] = (s_all[sl, :].astype(F32) * column(wide + j)).astype(BF)

    loop(wide, student_weights)
    tokens_drain(1)
    for xx in range(nx):
        feat_copy(t_all, 0, ra, ra_s, ra_r, xx).wait()
        feat_copy(t_all, nx * tl, rb, rb_s, rb_r, xx).wait()
    w_out[0:wide, :] = (1.0 / student_temp) / (tokens * reduce_end(2, wide, ds))

    group = tl // 128

    def combine(i):
        sl = rows(i * 128, 128)
        j = ((i // group) * 2 + c) * group + lax.rem(i, group)
        value = (fa[sl, :] + ra[sl, :].astype(F32)) * column(wide + j)
        value = value - (fb[sl, :] + rb[sl, :].astype(F32)) * column(j)
        cx[i // group, rows(lax.rem(i, group) * 128, 128), :] = value.astype(BF)

    loop(nx * group, combine)
    yz_d = []
    for j in range(1, nq):
        d = remote(
            cx.at[:, rows(lax.rem(p + j, nq) * piece, piece), :], yzr.at[j - 1],
            yz_s.at[j - 1], yz_r.at[j - 1], peer(j),
        )
        d.start()
        yz_d.append(d)

    def teacher_weights(j):
        sl = rows(j * 128, 128)
        s_all[sl, :] = (s_all[sl, :].astype(F32) * column(j)).astype(BF)

    loop(wide, teacher_weights)

    def chunk_part(block, q):
        return gp_out.at[rows(block * pl_rows + q * CH, CH)]

    def chunk_send(q, k):
        to = (bat(1, 0), p) if k == 0 else (bat(nx - 1, 0), p)
        part = chunk_part(b, q)
        return remote(part, part, g_s.at[k, q], g_r.at[k, q], to)

    def chunk_forward(q, k):
        block = bat(nx - 1, 0) if k == 0 else bat(1, 0)
        to = (bat(1, 0), p) if k == 0 else (bat(nx - 1, 0), p)
        size = CH // 2
        part = gp_out.at[rows(block * pl_rows + q * CH + k * size, size)]
        return remote(part, part, f_s.at[k, q], f_r.at[k, q], to)

    def chunk_sibling(q, k):
        part = chunk_part(bat((0, nx - 1, 1, 2)[k], 0), q)
        return remote(part, part, sib_s.at[k, q], sib_r.at[k, q], sibling)

    def chunk_compute(q):
        sl = rows(q * CH, CH)
        back = nn(s[sl, :], st[...]) - ccol[sl, 0:1] * nn(e[sl, :], s_all[...])
        unit, scale = unit_rows(sp[sl, :])
        value = back_norm(back, unit, scale).astype(BF)
        gp_out[rows(b * pl_rows + q * CH, CH), :] = value
        chunk_send(q, 0).start()
        chunk_send(q, 1).start()
        chunk_sibling(q, 0).start()

    def chunk_recv(q):
        for k in range(2):
            chunk_send(q, k).wait_recv()
            chunk_forward(q, k).start()
            chunk_sibling(q, 1 + k).start()

    def chunk_last(q):
        for k in range(2):
            chunk_forward(q, k).wait_recv()
        chunk_sibling(q, 3).start()

    lag = 3
    loop(lag, chunk_compute)

    def chunk_both(q):
        chunk_compute(q + lag)
        chunk_recv(q)

    loop(chunks - lag, chunk_both)
    loop(lag, lambda q: chunk_recv(q + chunks - lag))
    for d in yz_d:
        d.wait_recv()
    value = cx[:, rows(p * piece, piece), :].astype(F32)
    for j in range(nq - 1):
        value = value + yzr[j].astype(F32)
    sumf[...] = value
    xs[...] = value.astype(BF)
    xr_d = []
    for dx in range(1, nx):
        d = remote(
            xs.at[lax.rem(x + dx, nx)], xr.at[dx - 1],
            xr_s.at[dx - 1], xr_r.at[dx - 1], (bat(dx, 0), p),
        )
        d.start()
        xr_d.append(d)
    loop(chunks, chunk_last)
    for d in xr_d:
        d.wait_recv()
    value = sumf[x]
    for dx in range(nx - 1):
        value = value + xr[dx].astype(F32)
    own = rows(p * piece, piece)
    unit, scale = unit_rows(sf[own, :])
    gs_out[own, :] = back_norm(value, unit, scale).astype(BF)
    gs_d = []
    for j in range(1, nq):
        part = gs_out.at[own]
        d = remote(part, part, gs_s.at[j - 1], gs_r.at[j - 1], peer(j))
        d.start()
        gs_d.append(d)

    for d in pending + yz_d + xr_d + gs_d:
        d.wait_send()

    def drain(q):
        for k in range(2):
            chunk_send(q, k).wait_send()
            chunk_forward(q, k).wait_send()
        for k in range(4):
            chunk_sibling(q, k).wait()

    loop(chunks, drain)
    for d in gs_d:
        d.wait_recv()


def on_device(nb, nq, student_feats, teacher_feats, student_protos, teacher_protos):
    tl, depth = student_feats.shape
    pl_rows = student_protos.shape[0] // nb
    tokens = tl * nb
    chunks = pl_rows // CH
    wide = tokens // 128
    nx = nb // 2
    piece = tl // nq
    vm = pltpu.VMEM
    dma = pltpu.SemaphoreType.DMA
    half = tokens // 2
    scratch = [
        vm((tl, depth), BF),
        vm((tl, depth), BF),
        vm((tokens, depth), BF),
        vm((tokens, depth), BF),
        vm((pl_rows, depth), BF),
        vm((pl_rows, depth), BF),
        vm((pl_rows, depth), BF),
        vm((pl_rows, tokens), BF),
        vm((pl_rows, tokens), BF),
        vm((pl_rows, 128), F32),
        vm((8, tokens), F32),
        vm((half, depth), F32),
        vm((half, depth), F32),
        vm((half, depth), BF),
        vm((half, depth), BF),
        vm((tokens, depth), BF),
        vm((pl_rows, 128), F32),
        vm((16, tokens), BF),
        vm((16, pl_rows), BF),
        vm((ITERS, 2 * wide, 128), F32),
        vm((ITERS, 2 * wide, 128), F32),
        vm((ITERS, nb - 1, 2 * wide, 128), F32),
        vm((ITERS, nq - 1, 2 * wide, 128), F32),
        vm((2 * wide, 128), F32),
        vm((nx, tl, depth), BF),
        vm((nq - 1, nx, piece, depth), BF),
        vm((nx, piece, depth), F32),
        vm((nx, piece, depth), BF),
        vm((nx - 1, piece, depth), BF),
        dma((4,)),
        dma((2, nx)), dma((2, nx)), dma((2, nx)), dma((2, nx)),
        dma((2, nq - 1)), dma((2, nq - 1)),
        dma((ITERS, nb - 1)), dma((ITERS, nb - 1)),
        dma((ITERS, nq - 1)), dma((ITERS, nq - 1)),
        dma((2, chunks)), dma((2, chunks)), dma((2, chunks)), dma((2, chunks)),
        dma((4, chunks)), dma((4, chunks)),
        dma((nx,)), dma((nx,)), dma((nx,)), dma((nx,)),
        dma((nq - 1,)), dma((nq - 1,)),
        dma((nx - 1,)), dma((nx - 1,)),
        dma((nq - 1,)), dma((nq - 1,)),
    ]
    in_vmem = pl.BlockSpec(memory_space=pltpu.VMEM)
    anywhere = pl.BlockSpec(memory_space=pl.ANY)
    return pl.pallas_call(
        functools.partial(kernel, nb, nq),
        out_shape=[
            pltpu.VMEM(student_protos.shape, BF),
            pltpu.VMEM(student_feats.shape, BF),
        ],
        in_specs=[anywhere] * 4,
        out_specs=[in_vmem, in_vmem],
        scratch_shapes=scratch,
        compiler_params=pltpu.CompilerParams(
            collective_id=0, has_side_effects=True, vmem_limit_bytes=54 << 20
        ),
        name="prototype_head",
    )(student_feats, teacher_feats, student_protos, teacher_protos)


def solution(mesh):
    nb, nq = mesh.shape["batch"], mesh.shape["proto"]
    in_specs = (P("batch", None), P("batch", None), P("proto", None), P("proto", None))
    out_specs = (P("proto", None), P("batch", None))
    return jax.shard_map(
        functools.partial(on_device, nb, nq),
        mesh=mesh, in_specs=in_specs, out_specs=out_specs, check_vma=False,
    )
```

```python
import functools

import jax
import jax.numpy as jnp
from jax import lax
from jax.experimental import pallas as pl
from jax.experimental.pallas import tpu as pltpu
from jax.sharding import PartitionSpec as P

ITERS = 3
eps = 1e-06
teacher_temp = 0.04
student_temp = 0.1
LOG2E = 1.4426950408889634
F32 = jnp.float32
BF = jnp.bfloat16
MESH = pl.DeviceIdType.MESH
CH = 128
NZ = 4


def nt(left, right):
    return lax.dot_general(
        left, right, (((1,), (1,)), ((), ())), preferred_element_type=F32
    )


def nn(left, right):
    return jnp.dot(left, right, preferred_element_type=F32)


def tn(left, right):
    return lax.dot_general(
        left, right, (((0,), (0,)), ((), ())), preferred_element_type=F32
    )


def loop(count, body):
    def step(i, carry):
        body(i)
        return carry

    lax.fori_loop(0, count, step, 0)


def rows(start, size):
    return pl.ds(pl.multiple_of(start, size), size)


def unit_rows(values):
    values = values.astype(F32)
    scale = lax.rsqrt(jnp.sum(values * values, axis=1, keepdims=True) + eps)
    return values * scale, scale


def back_norm(grad, unit, scale):
    return scale * (grad - unit * jnp.sum(grad * unit, axis=1, keepdims=True))


def kernel(
    nb, nq,
    sf_hbm, tf_hbm, sp_hbm, tp_hbm,
    gp_out, gs_out,
    sf, tf, t_all, s_all, sp, anchor, pu, e, s, cs, tot, fa, fb, ra, rb, st, ccol,
    r16, c16, w_src, w_mid, w_g1, w_g2, w_out, cx, b1y, b1z, c2y, c2z, b2y, b2z, sumf, xs, xr,
    lsem, tok_s, tok_r, fwd_s, fwd_r, spr_s, spr_r,
    a1_s, a1_r, a2_s, a2_r, g_s, g_r, f_s, f_r, sib_s, sib_r,
    ra_s, ra_r, rb_s, rb_r, y1_s, y1_r, z1_s, z1_r, y2_s, y2_r, z2_s, z2_r, xr_s, xr_r, gs_s, gs_r,
):
    nx = nb // 2
    far_dx = nx // 2
    hx = nx // 2
    nz = NZ
    ny = nq // nz
    tl, depth = sf.shape
    tokens = tl * nb
    pl_rows = sp.shape[0]
    protos = pl_rows * nb * nq
    chunks = pl_rows // CH
    wide = tokens // 128
    piece = tl // nq
    plane = 2 * tl
    b, p = lax.axis_index("batch"), lax.axis_index("proto")
    x, c = b // 2, lax.rem(b, 2)
    y, z = p // nz, lax.rem(p, nz)

    def bat(dx, dc):
        return lax.rem(x + dx, nx) * 2 + lax.rem(c + dc, 2)

    def peer(j):
        return (b, lax.rem(p + j, nq))

    def remote(src, dst, ss, rs, to):
        return pltpu.make_async_remote_copy(
            src, dst, ss, rs, device_id=to, device_id_type=MESH
        )

    sibling = (bat(0, 1), p)

    barrier = pltpu.get_barrier_semaphore()
    for j in range(1, nb):
        pl.semaphore_signal(
            barrier, inc=1, device_id=(lax.rem(b + j, nb), p), device_id_type=MESH
        )
    for j in range(1, nq):
        pl.semaphore_signal(barrier, inc=1, device_id=peer(j), device_id_type=MESH)
    mine = rows(b * pl_rows, pl_rows)
    loads = [
        pltpu.make_async_copy(tf_hbm, tf, lsem.at[0]),
        pltpu.make_async_copy(sf_hbm, sf, lsem.at[1]),
        pltpu.make_async_copy(tp_hbm.at[mine], anchor, lsem.at[2]),
        pltpu.make_async_copy(sp_hbm.at[mine], sp, lsem.at[3]),
    ]
    for d in loads:
        d.start()

    def norm_into(src, dst, start, count):
        def body(i):
            unit, _ = unit_rows(src[rows(i * 128, 128), :])
            dst[rows(start + i * 128, 128), :] = unit.astype(BF)

        loop(count // 128, body)

    loads[0].wait()
    norm_into(tf, t_all, b * tl, tl)
    pl.semaphore_wait(barrier, nb + nq - 2)

    feats = (t_all, s_all)

    def token_copy(f, dx):
        start, size = b * tl, tl
        if dx == far_dx:
            start, size = b * tl + p * piece, piece
        part = feats[f].at[rows(start, size)]
        to = sibling if dx == 0 else (bat(dx, 0), p)
        return remote(part, part, tok_s.at[f, dx], tok_r.at[f, dx], to)

    def spread(f, j):
        part = feats[f].at[rows(bat(nx - far_dx, 0) * tl + p * piece, piece)]
        return remote(part, part, spr_s.at[f, j - 1], spr_r.at[f, j - 1], peer(j))

    def forward(f, dx):
        block = feats[f].at[rows(bat(nx - dx, 0) * tl, tl)]
        return remote(block, block, fwd_s.at[f, dx], fwd_r.at[f, dx], sibling)

    near = (1, nx - 1)

    def tokens_send(f):
        for dx in (far_dx, 0) + near:
            token_copy(f, dx).start()

    def spread_start(f):
        token_copy(f, far_dx).wait_recv()
        for j in range(1, nq):
            spread(f, j).start()

    def spread_end(f):
        for j in range(1, nq):
            spread(f, j).wait_recv()
        forward(f, far_dx).start()

    def near_end(f):
        for dx in near:
            token_copy(f, dx).wait_recv()
            forward(f, dx).start()

    def tokens_drain(f):
        for dx in (far_dx, 0) + (() if f == 0 else near):
            token_copy(f, dx).wait_send()
        for dx in range(1, nx):
            forward(f, dx).wait_send()
        for j in range(1, nq):
            spread(f, j).wait_send()

    tokens_send(0)
    loads[2].wait()
    norm_into(anchor, anchor, 0, pl_rows)

    def exp_plane(left, right, out, dx, factor, accumulate):
        cols = rows(lax.rem(x + nx - dx, nx) * plane, plane)

        def body(i):
            sl = rows(i * 256, 256)
            value = jnp.exp2(nt(left[sl, :], right[cols, :]) * factor)
            out[sl, cols] = value.astype(BF)
            accumulate(value, sl, cols, dx)

        loop(pl_rows // 256, body)

    def col_acc(value, sl, cols, dx):
        acc = value[:, 0:128]
        for q in range(1, plane // 128):
            acc = acc + value[:, q * 128 : (q + 1) * 128]
        if dx == 0:
            cs[sl, :] = acc
        else:
            cs[sl, :] += acc

    def row_acc(value, sl, cols, dx):
        tot[:, cols] += jnp.sum(value.reshape(32, 8, plane), axis=0)

    def teacher_plane(dx):
        if dx:
            forward(0, dx).wait_recv()
        else:
            token_copy(0, 0).wait_recv()
        exp_plane(anchor, t_all, e, dx, LOG2E / teacher_temp, col_acc)

    def student_plane(dx):
        if dx:
            forward(1, dx).wait_recv()
        else:
            token_copy(1, 0).wait_recv()
        exp_plane(pu, s_all, s, dx, LOG2E / student_temp, row_acc)

    loads[1].wait()
    norm_into(sf, s_all, b * tl, tl)
    teacher_plane(0)
    spread_start(0)
    loads[3].wait()
    norm_into(sp, pu, 0, pl_rows)
    tot[...] = jnp.zeros_like(tot)
    for dx in near:
        token_copy(0, dx).wait_send()
    tokens_send(1)
    spread_end(0)
    near_end(0)
    teacher_plane(far_dx)
    teacher_plane(near[0])
    spread_start(1)
    teacher_plane(near[1])
    half = lax.broadcasted_iota(jnp.int32, (16, 128), 0) < 8

    def split_into(dst, j, row):
        high = row.astype(BF).astype(F32)
        dst[:, j * 128 : (j + 1) * 128] = jnp.where(half, high, row - high).astype(BF)

    def reduce_start(n):
        ds = [
            remote(w_src.at[n], w_g1.at[n, j - 1], a1_s.at[n, j - 1],
                   a1_r.at[n, j - 1], (lax.rem(b + j, nb), p))
            for j in range(1, nb)
        ]
        for d in ds:
            d.start()
        pending.extend(ds)
        return ds

    def reduce_middle(n, ds):
        for d in ds:
            d.wait_recv()
        value = w_src[n]
        for j in range(nb - 1):
            value = value + w_g1[n, j]
        w_mid[n] = value.astype(BF)
        ds = [
            remote(w_mid.at[n], w_g2.at[n, j - 1], a2_s.at[n, j - 1],
                   a2_r.at[n, j - 1], peer(j))
            for j in range(1, nq)
        ]
        for d in ds:
            d.start()
        pending.extend(ds)
        return ds

    def reduce_end(n, ds):
        for d in ds:
            d.wait_recv()
        value = w_mid[n].astype(F32)
        for j in range(nq - 1):
            value = value + w_g2[n, j].astype(F32)
        return value

    def row_pass(n):
        out = nn(c16[...], e[...])
        line = out[0:1, :] + out[8:9, :]
        for j in range(wide):
            w_src[n, j : j + 1, :] = line[:, j * 128 : (j + 1) * 128]

    def col_pass(weights):
        for j in range(wide):
            split_into(r16, j, weights[j : j + 1, :])
        out = nt(r16[...], e[...])
        line = 1.0 / (protos * (out[0:1, :] + out[8:9, :]))
        return [line[:, j * 128 : (j + 1) * 128] for j in range(pl_rows // 128)]

    def feat_out(left, right, buf, base, to, ss, rs):
        def body(xx):
            cols = rows((xx * 2 + 1 - c) * tl, tl)
            sl = rows(base + xx * tl, tl)
            buf[sl, :] = tn(left[:, cols], right[...]).astype(BF)
            feat_copy(buf, base, to, ss, rs, xx).start()

        loop(nx, body)

    def feat_copy(buf, base, to, ss, rs, xx):
        return remote(
            buf.at[rows(base + xx * tl, tl)], to.at[rows(xx * tl, tl)],
            ss.at[xx], rs.at[xx], sibling,
        )

    def feat_own(left, right, out):
        def body(xx):
            cols = rows((xx * 2 + c) * tl, tl)
            out[rows(xx * tl, tl), :] = tn(left[:, cols], right[...])

        loop(nx, body)

    pending = []
    for j in range(pl_rows // 128):
        sums = jnp.sum(cs[j * 128 : (j + 1) * 128, :].T, axis=0, keepdims=True)
        split_into(c16, j, 1.0 / (protos * sums))
    row_pass(0)
    ds = reduce_start(0)
    student_plane(0)
    spread_end(1)
    ds = reduce_middle(0, ds)
    student_plane(far_dx)
    near_end(1)
    student_plane(near[0])
    student_plane(near[1])
    tokens_drain(0)
    weights = 1.0 / (tokens * reduce_end(0, ds))
    for j, line in enumerate(col_pass(weights)):
        split_into(c16, j, line)
    row_pass(1)
    ds = reduce_start(1)
    line = jnp.sum(tot[...], axis=0, keepdims=True)
    for j in range(wide):
        w_src[ITERS, j : j + 1, :] = line[:, j * 128 : (j + 1) * 128]
    dt = reduce_start(ITERS)
    feat_out(s, pu, t_all, 0, ra, ra_s, ra_r)
    ds = reduce_middle(1, ds)
    dt = reduce_middle(ITERS, dt)
    feat_own(s, pu, fa)
    weights = 1.0 / (tokens * reduce_end(1, ds))
    lines = col_pass(weights)
    for j, line in enumerate(lines):
        split_into(c16, j, line)
    row_pass(2)
    ds = reduce_start(2)
    for j, line in enumerate(lines):
        ccol[j * 128 : (j + 1) * 128, :] = jnp.broadcast_to(line, (128, 128)).T

    def scale_protos(j):
        sl = rows(j * 128, 128)
        anchor[sl, :] = (ccol[sl, 0:1] * pu[sl, :].astype(F32)).astype(BF)

    loop(pl_rows // 128, scale_protos)
    feat_out(e, anchor, t_all, nx * tl, rb, rb_s, rb_r)
    ds = reduce_middle(2, ds)
    w_out[wide : 2 * wide, :] = 1.0 / (student_temp * tokens * reduce_end(ITERS, dt))
    feat_own(e, anchor, fb)

    def column(j):
        return jnp.broadcast_to(w_out[pl.ds(j, 1), :], (128, 128)).T[:, 0:1]

    def student_weights(j):
        sl = rows(j * 128, 128)
        st[sl, :] = (s_all[sl, :].astype(F32) * column(wide + j)).astype(BF)

    loop(wide, student_weights)
    tokens_drain(1)
    for xx in range(nx):
        feat_copy(t_all, 0, ra, ra_s, ra_r, xx).wait()
        feat_copy(t_all, nx * tl, rb, rb_s, rb_r, xx).wait()
    w_out[0:wide, :] = (1.0 / student_temp) / (tokens * reduce_end(2, ds))

    group = tl // 128

    def combine(i):
        sl = rows(i * 128, 128)
        j = ((i // group) * 2 + c) * group + lax.rem(i, group)
        value = (fa[sl, :] + ra[sl, :].astype(F32)) * column(wide + j)
        value = value - (fb[sl, :] + rb[sl, :].astype(F32)) * column(j)
        cx[i // group, lax.rem(i, group)] = value.astype(BF).reshape(nz, piece, depth)

    loop(nx * group, combine)
    feat_d = []

    def feat_send(src, dst, ss, rs, to):
        d = remote(src, dst, ss, rs, to)
        d.start()
        feat_d.append(d)
        return d

    def along_y(d):
        return lax.rem(y + d, ny)

    def along_z(d):
        return lax.rem(z + d, nz)

    first = [
        feat_send(cx.at[0:hx, along_y(d)], b1y.at[d - 1], y1_s.at[d - 1],
                  y1_r.at[d - 1], (b, along_y(d) * nz + z))
        for d in range(1, ny)
    ] + [
        feat_send(cx.at[hx:nx, :, along_z(d)], b1z.at[d - 1], z1_s.at[d - 1],
                  z1_r.at[d - 1], (b, y * nz + along_z(d)))
        for d in range(1, nz)
    ]

    def feat_middle():
        for d in first:
            d.wait_recv()
        for h in range(hx):
            value = cx[h, y].astype(F32)
            for d in range(ny - 1):
                value = value + b1y[d, h].astype(F32)
            c2y[h] = value.astype(BF)
            value = cx[hx + h, :, z].astype(F32)
            for d in range(nz - 1):
                value = value + b1z[d, h].astype(F32)
            c2z[h] = value.astype(BF)
        return [
            feat_send(c2y.at[:, along_z(d)], b2y.at[d - 1], z2_s.at[d - 1],
                      z2_r.at[d - 1], (b, y * nz + along_z(d)))
            for d in range(1, nz)
        ] + [
            feat_send(c2z.at[:, along_y(d)], b2z.at[d - 1], y2_s.at[d - 1],
                      y2_r.at[d - 1], (b, along_y(d) * nz + z))
            for d in range(1, ny)
        ]

    def feat_x(second):
        for d in second:
            d.wait_recv()
        value = c2y[:, z].astype(F32)
        for d in range(nz - 1):
            value = value + b2y[d].astype(F32)
        sumf[0:hx] = value
        xs[0:hx] = value.astype(BF)
        value = c2z[:, y].astype(F32)
        for d in range(ny - 1):
            value = value + b2z[d].astype(F32)
        sumf[hx:nx] = value
        xs[hx:nx] = value.astype(BF)
        return [
            feat_send(xs.at[lax.rem(x + dx, nx)], xr.at[dx - 1],
                      xr_s.at[dx - 1], xr_r.at[dx - 1], (bat(dx, 0), p))
            for dx in range(1, nx)
        ]

    def feat_last(third):
        for d in third:
            d.wait_recv()
        value = sumf[x]
        for dx in range(nx - 1):
            value = value + xr[dx].astype(F32)
        own = rows(p * piece, piece)
        unit, scale = unit_rows(sf[own, :])
        gs_out[own, :] = back_norm(value, unit, scale).astype(BF)
        part = gs_out.at[own]
        return [
            feat_send(part, part, gs_s.at[j - 1], gs_r.at[j - 1], peer(j))
            for j in range(1, nq)
        ]

    def teacher_weights(j):
        sl = rows(j * 128, 128)
        s_all[sl, :] = (s_all[sl, :].astype(F32) * column(j)).astype(BF)

    loop(wide, teacher_weights)

    def chunk_part(block, q):
        return gp_out.at[rows(block * pl_rows + q * CH, CH)]

    def chunk_send(q, k):
        to = (bat(1, 0), p) if k == 0 else (bat(nx - 1, 0), p)
        part = chunk_part(b, q)
        return remote(part, part, g_s.at[k, q], g_r.at[k, q], to)

    def chunk_forward(q, k):
        block = bat(nx - 1, 0) if k == 0 else bat(1, 0)
        to = (bat(1, 0), p) if k == 0 else (bat(nx - 1, 0), p)
        size = CH // 2
        part = gp_out.at[rows(block * pl_rows + q * CH + k * size, size)]
        return remote(part, part, f_s.at[k, q], f_r.at[k, q], to)

    def chunk_sibling(q, k):
        part = chunk_part(bat((0, nx - 1, 1, 2)[k], 0), q)
        return remote(part, part, sib_s.at[k, q], sib_r.at[k, q], sibling)

    def chunk_compute(q):
        sl = rows(q * CH, CH)
        back = nn(s[sl, :], st[...]) - ccol[sl, 0:1] * nn(e[sl, :], s_all[...])
        unit, scale = unit_rows(sp[sl, :])
        value = back_norm(back, unit, scale).astype(BF)
        gp_out[rows(b * pl_rows + q * CH, CH), :] = value
        chunk_send(q, 0).start()
        chunk_send(q, 1).start()
        chunk_sibling(q, 0).start()

    def chunk_recv(q):
        for k in range(2):
            chunk_send(q, k).wait_recv()
            chunk_forward(q, k).start()
            chunk_sibling(q, 1 + k).start()

    def chunk_last(q):
        for k in range(2):
            chunk_forward(q, k).wait_recv()
        chunk_sibling(q, 3).start()

    lag = 3
    loop(lag, chunk_compute)

    def chunk_both(q):
        chunk_compute(q + lag)
        chunk_recv(q)

    loop(2, chunk_both)
    second = feat_middle()
    loop(chunks - lag - 2, lambda q: chunk_both(q + 2))
    third = feat_x(second)
    chunk_recv(chunks - lag)
    final = feat_last(third)
    loop(lag - 1, lambda q: chunk_recv(q + chunks - lag + 1))
    loop(chunks, chunk_last)

    for d in pending + feat_d:
        d.wait_send()

    def drain(q):
        for k in range(2):
            chunk_send(q, k).wait_send()
            chunk_forward(q, k).wait_send()
        for k in range(4):
            chunk_sibling(q, k).wait()

    loop(chunks, drain)
    for d in final:
        d.wait_recv()


def on_device(nb, nq, student_feats, teacher_feats, student_protos, teacher_protos):
    tl, depth = student_feats.shape
    pl_rows = student_protos.shape[0] // nb
    tokens = tl * nb
    chunks = pl_rows // CH
    wide = tokens // 128
    nx = nb // 2
    piece = tl // nq
    vm = pltpu.VMEM
    dma = pltpu.SemaphoreType.DMA
    half = tokens // 2
    hx, nz = nx // 2, NZ
    ny = nq // nz
    scratch = [
        vm((tl, depth), BF),
        vm((tl, depth), BF),
        vm((tokens, depth), BF),
        vm((tokens, depth), BF),
        vm((pl_rows, depth), BF),
        vm((pl_rows, depth), BF),
        vm((pl_rows, depth), BF),
        vm((pl_rows, tokens), BF),
        vm((pl_rows, tokens), BF),
        vm((pl_rows, 128), F32),
        vm((8, tokens), F32),
        vm((half, depth), F32),
        vm((half, depth), F32),
        vm((half, depth), BF),
        vm((half, depth), BF),
        vm((tokens, depth), BF),
        vm((pl_rows, 128), F32),
        vm((16, tokens), BF),
        vm((16, pl_rows), BF),
        vm((ITERS + 1, wide, 128), F32),
        vm((ITERS + 1, wide, 128), BF),
        vm((ITERS + 1, nb - 1, wide, 128), F32),
        vm((ITERS + 1, nq - 1, wide, 128), BF),
        vm((2 * wide, 128), F32),
        vm((nx, ny, nz, piece, depth), BF),
        vm((ny - 1, hx, nz, piece, depth), BF),
        vm((nz - 1, hx, ny, piece, depth), BF),
        vm((hx, nz, piece, depth), BF),
        vm((hx, ny, piece, depth), BF),
        vm((nz - 1, hx, piece, depth), BF),
        vm((ny - 1, hx, piece, depth), BF),
        vm((nx, piece, depth), F32),
        vm((nx, piece, depth), BF),
        vm((nx - 1, piece, depth), BF),
        dma((4,)),
        dma((2, nx)), dma((2, nx)), dma((2, nx)), dma((2, nx)),
        dma((2, nq - 1)), dma((2, nq - 1)),
        dma((ITERS + 1, nb - 1)), dma((ITERS + 1, nb - 1)),
        dma((ITERS + 1, nq - 1)), dma((ITERS + 1, nq - 1)),
        dma((2, chunks)), dma((2, chunks)), dma((2, chunks)), dma((2, chunks)),
        dma((4, chunks)), dma((4, chunks)),
        dma((nx,)), dma((nx,)), dma((nx,)), dma((nx,)),
        dma((ny - 1,)), dma((ny - 1,)), dma((nz - 1,)), dma((nz - 1,)),
        dma((ny - 1,)), dma((ny - 1,)), dma((nz - 1,)), dma((nz - 1,)),
        dma((nx - 1,)), dma((nx - 1,)),
        dma((nq - 1,)), dma((nq - 1,)),
    ]
    in_vmem = pl.BlockSpec(memory_space=pltpu.VMEM)
    anywhere = pl.BlockSpec(memory_space=pl.ANY)
    return pl.pallas_call(
        functools.partial(kernel, nb, nq),
        out_shape=[
            pltpu.VMEM(student_protos.shape, BF),
            pltpu.VMEM(student_feats.shape, BF),
        ],
        in_specs=[anywhere] * 4,
        out_specs=[in_vmem, in_vmem],
        scratch_shapes=scratch,
        compiler_params=pltpu.CompilerParams(
            collective_id=0, has_side_effects=True, vmem_limit_bytes=54 << 20
        ),
        name="prototype_head",
    )(student_feats, teacher_feats, student_protos, teacher_protos)


def solution(mesh):
    nb, nq = mesh.shape["batch"], mesh.shape["proto"]
    in_specs = (P("batch", None), P("batch", None), P("proto", None), P("proto", None))
    out_specs = (P("proto", None), P("batch", None))
    return jax.shard_map(
        functools.partial(on_device, nb, nq),
        mesh=mesh, in_specs=in_specs, out_specs=out_specs, check_vma=False,
    )
```

```python
import functools

import jax
import jax.numpy as jnp
from jax import lax
from jax.experimental import pallas as pl
from jax.experimental.pallas import tpu as pltpu
from jax.sharding import PartitionSpec as P

ITERS = 3
eps = 1e-06
teacher_temp = 0.04
student_temp = 0.1
LOG2E = 1.4426950408889634
F32 = jnp.float32
BF = jnp.bfloat16
MESH = pl.DeviceIdType.MESH
CH = 128
NZ = 4


def nt(left, right):
    return lax.dot_general(
        left, right, (((1,), (1,)), ((), ())), preferred_element_type=F32
    )


def nn(left, right):
    return jnp.dot(left, right, preferred_element_type=F32)


def tn(left, right):
    return lax.dot_general(
        left, right, (((0,), (0,)), ((), ())), preferred_element_type=F32
    )


def loop(count, body):
    def step(i, carry):
        body(i)
        return carry

    lax.fori_loop(0, count, step, 0)


def rows(start, size):
    return pl.ds(pl.multiple_of(start, size), size)


def unit_rows(values):
    values = values.astype(F32)
    scale = lax.rsqrt(jnp.sum(values * values, axis=1, keepdims=True) + eps)
    return values * scale, scale


def back_norm(grad, unit, scale):
    return scale * (grad - unit * jnp.sum(grad * unit, axis=1, keepdims=True))


def kernel(
    nb, nq,
    sf_hbm, tf_hbm, sp_hbm, tp_hbm,
    gp_out, gs_out,
    sf, tf, t_all, s_all, sp, anchor, pu, e, s, cs, tot, fa, fb, ra, rb, oa, ob, put, anct, ccol,
    r16, c16, w_src, w_mid, w_g1, w_g2, w_out, cx, b1y, b1z, c2y, c2z, b2y, b2z, sumf, xs, xr,
    lsem, near_s, near_r, nfwd_s, nfwd_r, tok_s, tok_r, fwd_s, fwd_r, spr_s, spr_r,
    a1_s, a1_r, a2_s, a2_r, g_s, g_r, f_s, f_r, sib_s, sib_r,
    ra_s, ra_r, rb_s, rb_r, y1_s, y1_r, z1_s, z1_r, y2_s, y2_r, z2_s, z2_r, xr_s, xr_r, gs_s, gs_r,
):
    nx = nb // 2
    far_dx = nx // 2
    hx = nx // 2
    nz = NZ
    ny = nq // nz
    tl, depth = sf.shape
    tokens = tl * nb
    pl_rows = sp.shape[0]
    protos = pl_rows * nb * nq
    chunks = pl_rows // CH
    wide = tokens // 128
    piece = tl // nq
    plane = 2 * tl
    b, p = lax.axis_index("batch"), lax.axis_index("proto")
    x, c = b // 2, lax.rem(b, 2)
    y, z = p // nz, lax.rem(p, nz)

    def bat(dx, dc):
        return lax.rem(x + dx, nx) * 2 + lax.rem(c + dc, 2)

    def peer(j):
        return (b, lax.rem(p + j, nq))

    def remote(src, dst, ss, rs, to):
        return pltpu.make_async_remote_copy(
            src, dst, ss, rs, device_id=to, device_id_type=MESH
        )

    sibling = (bat(0, 1), p)

    barrier = pltpu.get_barrier_semaphore()
    for j in range(1, nb):
        pl.semaphore_signal(
            barrier, inc=1, device_id=(lax.rem(b + j, nb), p), device_id_type=MESH
        )
    for j in range(1, nq):
        pl.semaphore_signal(barrier, inc=1, device_id=peer(j), device_id_type=MESH)
    mine = rows(b * pl_rows, pl_rows)
    loads = [
        pltpu.make_async_copy(tf_hbm, tf, lsem.at[0]),
        pltpu.make_async_copy(sf_hbm, sf, lsem.at[1]),
        pltpu.make_async_copy(tp_hbm.at[mine], anchor, lsem.at[2]),
        pltpu.make_async_copy(sp_hbm.at[mine], sp, lsem.at[3]),
    ]
    for d in loads:
        d.start()

    def norm_into(src, dst, start, count):
        def body(i):
            unit, _ = unit_rows(src[rows(i * 128, 128), :])
            dst[rows(start + i * 128, 128), :] = unit.astype(BF)

        loop(count // 128, body)

    loads[0].wait()
    norm_into(tf, t_all, b * tl, tl)
    pl.semaphore_wait(barrier, nb + nq - 2)

    feats = (t_all, s_all)

    def near_copy(f, dx, h):
        part = feats[f].at[rows(b * tl + h * (tl // 2), tl // 2)]
        return remote(
            part, part, near_s.at[f, dx, h], near_r.at[f, dx, h], (bat(dx, 0), p)
        )

    def near_forward(f, dx, h):
        part = feats[f].at[rows(bat(nx - dx, 0) * tl + h * (tl // 2), tl // 2)]
        return remote(
            part, part, nfwd_s.at[f, dx, h], nfwd_r.at[f, dx, h], sibling
        )

    def token_copy(f, dx):
        start, size = b * tl, tl
        if dx == far_dx:
            start, size = b * tl + p * piece, piece
        part = feats[f].at[rows(start, size)]
        to = sibling if dx == 0 else (bat(dx, 0), p)
        return remote(part, part, tok_s.at[f, dx], tok_r.at[f, dx], to)

    def spread(f, j):
        part = feats[f].at[rows(bat(nx - far_dx, 0) * tl + p * piece, piece)]
        return remote(part, part, spr_s.at[f, j - 1], spr_r.at[f, j - 1], peer(j))

    def forward(f, dx):
        block = feats[f].at[rows(bat(nx - dx, 0) * tl, tl)]
        return remote(block, block, fwd_s.at[f, dx], fwd_r.at[f, dx], sibling)

    near = (1, nx - 1)

    def tokens_send(f):
        token_copy(f, far_dx).start()
        token_copy(f, 0).start()
        for h in range(2):
            for dx in near:
                near_copy(f, dx, h).start()

    def spread_start(f):
        token_copy(f, far_dx).wait_recv()
        for j in range(1, nq):
            spread(f, j).start()

    def spread_end(f):
        for j in range(1, nq):
            spread(f, j).wait_recv()
        forward(f, far_dx).start()

    def near_end(f):
        for h in range(2):
            for dx in near:
                near_copy(f, dx, h).wait_recv()
                near_forward(f, dx, h).start()

    def tokens_drain(f):
        token_copy(f, far_dx).wait_send()
        token_copy(f, 0).wait_send()
        forward(f, far_dx).wait_send()
        for h in range(2):
            for dx in near:
                if f:
                    near_copy(f, dx, h).wait_send()
                near_forward(f, dx, h).wait_send()
        for j in range(1, nq):
            spread(f, j).wait_send()

    tokens_send(0)
    loads[2].wait()
    norm_into(anchor, anchor, 0, pl_rows)

    def exp_plane(left, right, out, dx, factor, accumulate):
        cols = rows(lax.rem(x + nx - dx, nx) * plane, plane)

        def body(i):
            sl = rows(i * 256, 256)
            value = jnp.exp2(nt(left[sl, :], right[cols, :]) * factor)
            out[sl, cols] = value.astype(BF)
            accumulate(value, sl, cols, dx)

        loop(pl_rows // 256, body)

    def col_acc(value, sl, cols, dx):
        acc = value[:, 0:128]
        for q in range(1, plane // 128):
            acc = acc + value[:, q * 128 : (q + 1) * 128]
        if dx == 0:
            cs[sl, :] = acc
        else:
            cs[sl, :] += acc

    def row_acc(value, sl, cols, dx):
        tot[:, cols] += jnp.sum(value.reshape(32, 8, plane), axis=0)

    def teacher_plane(dx):
        if dx == far_dx:
            forward(0, dx).wait_recv()
        elif dx:
            for h in range(2):
                near_forward(0, dx, h).wait_recv()
        else:
            token_copy(0, 0).wait_recv()
        exp_plane(anchor, t_all, e, dx, LOG2E / teacher_temp, col_acc)

    def student_plane(dx):
        if dx == far_dx:
            forward(1, dx).wait_recv()
        elif dx:
            for h in range(2):
                near_forward(1, dx, h).wait_recv()
        else:
            token_copy(1, 0).wait_recv()
        exp_plane(pu, s_all, s, dx, LOG2E / student_temp, row_acc)

    loads[1].wait()
    norm_into(sf, s_all, b * tl, tl)
    teacher_plane(0)
    spread_start(0)
    loads[3].wait()

    def norm_protos(i):
        sl = rows(i * 128, 128)
        unit, _ = unit_rows(sp[sl, :])
        pu[sl, :] = unit.astype(BF)
        put[:, sl] = unit.T.astype(BF)

    loop(pl_rows // 128, norm_protos)
    tot[...] = jnp.zeros_like(tot)
    for h in range(2):
        for dx in near:
            near_copy(0, dx, h).wait_send()
    tokens_send(1)
    spread_end(0)
    near_end(0)
    teacher_plane(far_dx)
    teacher_plane(near[0])
    spread_start(1)
    teacher_plane(near[1])
    half = lax.broadcasted_iota(jnp.int32, (16, 128), 0) < 8

    def split_into(dst, j, row):
        high = row.astype(BF).astype(F32)
        dst[:, j * 128 : (j + 1) * 128] = jnp.where(half, high, row - high).astype(BF)

    def reduce_start(n):
        ds = [
            remote(w_src.at[n], w_g1.at[n, j - 1], a1_s.at[n, j - 1],
                   a1_r.at[n, j - 1], (lax.rem(b + j, nb), p))
            for j in range(1, nb)
        ]
        for d in ds:
            d.start()
        pending.extend(ds)
        return ds

    def reduce_middle(n, ds):
        for d in ds:
            d.wait_recv()
        value = w_src[n]
        for j in range(nb - 1):
            value = value + w_g1[n, j]
        w_mid[n] = value.astype(BF)
        ds = [
            remote(w_mid.at[n], w_g2.at[n, j - 1], a2_s.at[n, j - 1],
                   a2_r.at[n, j - 1], peer(j))
            for j in range(1, nq)
        ]
        for d in ds:
            d.start()
        pending.extend(ds)
        return ds

    def reduce_end(n, ds):
        for d in ds:
            d.wait_recv()
        value = w_mid[n].astype(F32)
        for j in range(nq - 1):
            value = value + w_g2[n, j].astype(F32)
        return value

    def row_pass(n):
        out = nn(c16[...], e[...])
        line = out[0:1, :] + out[8:9, :]
        for j in range(wide):
            w_src[n, j : j + 1, :] = line[:, j * 128 : (j + 1) * 128]

    def col_pass(weights):
        for j in range(wide):
            split_into(r16, j, weights[j : j + 1, :])
        out = nt(r16[...], e[...])
        line = 1.0 / (protos * (out[0:1, :] + out[8:9, :]))
        return [line[:, j * 128 : (j + 1) * 128] for j in range(pl_rows // 128)]

    def feat_copy(buf, to, ss, rs, xx):
        return remote(buf.at[xx], to.at[xx], ss.at[xx], rs.at[xx], sibling)

    def feat_out(left, right, buf, to, ss, rs):
        def body(xx):
            cols = rows((xx * 2 + 1 - c) * tl, tl)
            buf[xx] = nn(left[...], right[:, cols]).astype(BF)
            feat_copy(buf, to, ss, rs, xx).start()

        loop(nx, body)

    def feat_own(left, right, out):
        def body(xx):
            cols = rows((xx * 2 + c) * tl, tl)
            out[xx] = nn(left[...], right[:, cols])

        loop(nx, body)

    pending = []
    for j in range(pl_rows // 128):
        sums = jnp.sum(cs[j * 128 : (j + 1) * 128, :].T, axis=0, keepdims=True)
        split_into(c16, j, 1.0 / (protos * sums))
    row_pass(0)
    ds = reduce_start(0)
    student_plane(0)
    spread_end(1)
    ds = reduce_middle(0, ds)
    student_plane(far_dx)
    near_end(1)
    student_plane(near[0])
    student_plane(near[1])
    tokens_drain(0)
    weights = 1.0 / (tokens * reduce_end(0, ds))
    for j, line in enumerate(col_pass(weights)):
        split_into(c16, j, line)
    row_pass(1)
    ds = reduce_start(1)
    line = jnp.sum(tot[...], axis=0, keepdims=True)
    for j in range(wide):
        w_src[ITERS, j : j + 1, :] = line[:, j * 128 : (j + 1) * 128]
    dt = reduce_start(ITERS)
    feat_out(put, s, oa, ra, ra_s, ra_r)
    ds = reduce_middle(1, ds)
    dt = reduce_middle(ITERS, dt)
    feat_own(put, s, fa)
    weights = 1.0 / (tokens * reduce_end(1, ds))
    lines = col_pass(weights)
    for j, line in enumerate(lines):
        split_into(c16, j, line)
    row_pass(2)
    ds = reduce_start(2)
    for j, line in enumerate(lines):
        sl = slice(j * 128, (j + 1) * 128)
        anct[:, sl] = (put[:, sl].astype(F32) * line).astype(BF)
    feat_out(anct, e, ob, rb, rb_s, rb_r)
    ds = reduce_middle(2, ds)
    w_out[wide : 2 * wide, :] = 1.0 / (student_temp * tokens * reduce_end(ITERS, dt))
    feat_own(anct, e, fb)
    for j, line in enumerate(lines):
        ccol[j * 128 : (j + 1) * 128, :] = jnp.broadcast_to(line, (128, 128)).T

    def column(j):
        return jnp.broadcast_to(w_out[pl.ds(j, 1), :], (128, 128)).T[:, 0:1]

    def student_weights(j):
        sl = rows(j * 128, 128)
        t_all[sl, :] = (s_all[sl, :].astype(F32) * column(wide + j)).astype(BF)

    loop(wide, student_weights)
    tokens_drain(1)
    for xx in range(nx):
        feat_copy(oa, ra, ra_s, ra_r, xx).wait()
        feat_copy(ob, rb, rb_s, rb_r, xx).wait()
    w_out[0:wide, :] = (1.0 / student_temp) / (tokens * reduce_end(2, ds))

    def teacher_weights(j):
        sl = rows(j * 128, 128)
        s_all[sl, :] = (s_all[sl, :].astype(F32) * column(j)).astype(BF)

    loop(wide, teacher_weights)

    def chunk_part(block, q):
        return gp_out.at[rows(block * pl_rows + q * CH, CH)]

    def chunk_send(q, k):
        to = (bat(1, 0), p) if k == 0 else (bat(nx - 1, 0), p)
        part = chunk_part(b, q)
        return remote(part, part, g_s.at[k, q], g_r.at[k, q], to)

    def chunk_forward(q, k):
        block = bat(nx - 1, 0) if k == 0 else bat(1, 0)
        to = (bat(1, 0), p) if k == 0 else (bat(nx - 1, 0), p)
        size = CH // 2
        part = gp_out.at[rows(block * pl_rows + q * CH + k * size, size)]
        return remote(part, part, f_s.at[k, q], f_r.at[k, q], to)

    def chunk_sibling(q, k):
        part = chunk_part(bat((0, nx - 1, 1, 2)[k], 0), q)
        return remote(part, part, sib_s.at[k, q], sib_r.at[k, q], sibling)

    def chunk_compute(q):
        sl = rows(q * CH, CH)
        back = nn(s[sl, :], t_all[...]) - ccol[sl, 0:1] * nn(e[sl, :], s_all[...])
        unit, scale = unit_rows(sp[sl, :])
        value = back_norm(back, unit, scale).astype(BF)
        gp_out[rows(b * pl_rows + q * CH, CH), :] = value
        chunk_send(q, 0).start()
        chunk_send(q, 1).start()
        chunk_sibling(q, 0).start()

    def chunk_recv(q):
        for k in range(2):
            chunk_send(q, k).wait_recv()
            chunk_forward(q, k).start()
            chunk_sibling(q, 1 + k).start()

    def chunk_last(q):
        for k in range(2):
            chunk_forward(q, k).wait_recv()
        chunk_sibling(q, 3).start()

    loop(2, chunk_compute)

    group = tl // 128

    def combine(i):
        xx, g = i // group, lax.rem(i, group)
        sl = rows(g * 128, 128)
        j = (xx * 2 + c) * group + g
        value = (fa[xx, :, sl] + ra[xx, :, sl].astype(F32)) * w_out[pl.ds(wide + j, 1), :]
        value = value - (fb[xx, :, sl] + rb[xx, :, sl].astype(F32)) * w_out[pl.ds(j, 1), :]
        cx[xx, g] = value.T.astype(BF).reshape(nz, piece, depth)

    loop(nx * group, combine)
    feat_d = []

    def feat_send(src, dst, ss, rs, to):
        d = remote(src, dst, ss, rs, to)
        d.start()
        feat_d.append(d)
        return d

    def along_y(d):
        return lax.rem(y + d, ny)

    def along_z(d):
        return lax.rem(z + d, nz)

    first = [
        feat_send(cx.at[0:hx, along_y(d)], b1y.at[d - 1], y1_s.at[d - 1],
                  y1_r.at[d - 1], (b, along_y(d) * nz + z))
        for d in range(1, ny)
    ] + [
        feat_send(cx.at[hx:nx, :, along_z(d)], b1z.at[d - 1], z1_s.at[d - 1],
                  z1_r.at[d - 1], (b, y * nz + along_z(d)))
        for d in range(1, nz)
    ]

    def feat_middle():
        for d in first:
            d.wait_recv()
        for h in range(hx):
            value = cx[h, y].astype(F32)
            for d in range(ny - 1):
                value = value + b1y[d, h].astype(F32)
            c2y[h] = value.astype(BF)
            value = cx[hx + h, :, z].astype(F32)
            for d in range(nz - 1):
                value = value + b1z[d, h].astype(F32)
            c2z[h] = value.astype(BF)
        return [
            feat_send(c2y.at[:, along_z(d)], b2y.at[d - 1], z2_s.at[d - 1],
                      z2_r.at[d - 1], (b, y * nz + along_z(d)))
            for d in range(1, nz)
        ] + [
            feat_send(c2z.at[:, along_y(d)], b2z.at[d - 1], y2_s.at[d - 1],
                      y2_r.at[d - 1], (b, along_y(d) * nz + z))
            for d in range(1, ny)
        ]

    def feat_x(second):
        for d in second:
            d.wait_recv()
        value = c2y[:, z].astype(F32)
        for d in range(nz - 1):
            value = value + b2y[d].astype(F32)
        sumf[0:hx] = value
        xs[0:hx] = value.astype(BF)
        value = c2z[:, y].astype(F32)
        for d in range(ny - 1):
            value = value + b2z[d].astype(F32)
        sumf[hx:nx] = value
        xs[hx:nx] = value.astype(BF)
        return [
            feat_send(xs.at[lax.rem(x + dx, nx)], xr.at[dx - 1],
                      xr_s.at[dx - 1], xr_r.at[dx - 1], (bat(dx, 0), p))
            for dx in range(1, nx)
        ]

    def feat_last(third):
        for d in third:
            d.wait_recv()
        value = sumf[x]
        for dx in range(nx - 1):
            value = value + xr[dx].astype(F32)
        own = rows(p * piece, piece)
        unit, scale = unit_rows(sf[own, :])
        gs_out[own, :] = back_norm(value, unit, scale).astype(BF)
        part = gs_out.at[own]
        return [
            feat_send(part, part, gs_s.at[j - 1], gs_r.at[j - 1], peer(j))
            for j in range(1, nq)
        ]

    loop(3, lambda q: chunk_compute(q + 2))
    second = feat_middle()
    loop(chunks - 5, lambda q: chunk_compute(q + 5))
    third = feat_x(second)
    loop(chunks - 3, chunk_recv)
    final = feat_last(third)
    loop(3, lambda q: chunk_recv(q + chunks - 3))
    loop(chunks, chunk_last)

    for d in pending + feat_d:
        d.wait_send()

    def drain(q):
        for k in range(2):
            chunk_send(q, k).wait_send()
            chunk_forward(q, k).wait_send()
        for k in range(4):
            chunk_sibling(q, k).wait()

    loop(chunks, drain)
    for d in final:
        d.wait_recv()


def on_device(nb, nq, student_feats, teacher_feats, student_protos, teacher_protos):
    tl, depth = student_feats.shape
    pl_rows = student_protos.shape[0] // nb
    tokens = tl * nb
    chunks = pl_rows // CH
    wide = tokens // 128
    nx = nb // 2
    piece = tl // nq
    vm = pltpu.VMEM
    dma = pltpu.SemaphoreType.DMA
    hx, nz = nx // 2, NZ
    ny = nq // nz
    scratch = [
        vm((tl, depth), BF),
        vm((tl, depth), BF),
        vm((tokens, depth), BF),
        vm((tokens, depth), BF),
        vm((pl_rows, depth), BF),
        vm((pl_rows, depth), BF),
        vm((pl_rows, depth), BF),
        vm((pl_rows, tokens), BF),
        vm((pl_rows, tokens), BF),
        vm((pl_rows, 128), F32),
        vm((8, tokens), F32),
        vm((nx, depth, tl), F32),
        vm((nx, depth, tl), F32),
        vm((nx, depth, tl), BF),
        vm((nx, depth, tl), BF),
        vm((nx, depth, tl), BF),
        vm((nx, depth, tl), BF),
        vm((depth, pl_rows), BF),
        vm((depth, pl_rows), BF),
        vm((pl_rows, 128), F32),
        vm((16, tokens), BF),
        vm((16, pl_rows), BF),
        vm((ITERS + 1, wide, 128), F32),
        vm((ITERS + 1, wide, 128), BF),
        vm((ITERS + 1, nb - 1, wide, 128), F32),
        vm((ITERS + 1, nq - 1, wide, 128), BF),
        vm((2 * wide, 128), F32),
        vm((nx, ny, nz, piece, depth), BF),
        vm((ny - 1, hx, nz, piece, depth), BF),
        vm((nz - 1, hx, ny, piece, depth), BF),
        vm((hx, nz, piece, depth), BF),
        vm((hx, ny, piece, depth), BF),
        vm((nz - 1, hx, piece, depth), BF),
        vm((ny - 1, hx, piece, depth), BF),
        vm((nx, piece, depth), F32),
        vm((nx, piece, depth), BF),
        vm((nx - 1, piece, depth), BF),
        dma((4,)),
        dma((2, nx, 2)), dma((2, nx, 2)), dma((2, nx, 2)), dma((2, nx, 2)),
        dma((2, nx)), dma((2, nx)), dma((2, nx)), dma((2, nx)),
        dma((2, nq - 1)), dma((2, nq - 1)),
        dma((ITERS + 1, nb - 1)), dma((ITERS + 1, nb - 1)),
        dma((ITERS + 1, nq - 1)), dma((ITERS + 1, nq - 1)),
        dma((2, chunks)), dma((2, chunks)), dma((2, chunks)), dma((2, chunks)),
        dma((4, chunks)), dma((4, chunks)),
        dma((nx,)), dma((nx,)), dma((nx,)), dma((nx,)),
        dma((ny - 1,)), dma((ny - 1,)), dma((nz - 1,)), dma((nz - 1,)),
        dma((ny - 1,)), dma((ny - 1,)), dma((nz - 1,)), dma((nz - 1,)),
        dma((nx - 1,)), dma((nx - 1,)),
        dma((nq - 1,)), dma((nq - 1,)),
    ]
    in_vmem = pl.BlockSpec(memory_space=pltpu.VMEM)
    anywhere = pl.BlockSpec(memory_space=pl.ANY)
    return pl.pallas_call(
        functools.partial(kernel, nb, nq),
        out_shape=[
            pltpu.VMEM(student_protos.shape, BF),
            pltpu.VMEM(student_feats.shape, BF),
        ],
        in_specs=[anywhere] * 4,
        out_specs=[in_vmem, in_vmem],
        scratch_shapes=scratch,
        compiler_params=pltpu.CompilerParams(
            collective_id=0, has_side_effects=True, vmem_limit_bytes=54 << 20
        ),
        name="prototype_head",
    )(student_feats, teacher_feats, student_protos, teacher_protos)


def solution(mesh):
    nb, nq = mesh.shape["batch"], mesh.shape["proto"]
    in_specs = (P("batch", None), P("batch", None), P("proto", None), P("proto", None))
    out_specs = (P("proto", None), P("batch", None))
    return jax.shard_map(
        functools.partial(on_device, nb, nq),
        mesh=mesh, in_specs=in_specs, out_specs=out_specs, check_vma=False,
    )
```

```python
import functools

import jax
import jax.numpy as jnp
from jax import lax
from jax.experimental import pallas as pl
from jax.experimental.pallas import tpu as pltpu
from jax.sharding import PartitionSpec as P

ITERS = 3
eps = 1e-06
teacher_temp = 0.04
student_temp = 0.1
LOG2E = 1.4426950408889634
F32 = jnp.float32
BF = jnp.bfloat16
MESH = pl.DeviceIdType.MESH
CH = 128
NZ = 4


def nt(left, right):
    return lax.dot_general(
        left, right, (((1,), (1,)), ((), ())), preferred_element_type=F32
    )


def nn(left, right):
    return jnp.dot(left, right, preferred_element_type=F32)


def tn(left, right):
    return lax.dot_general(
        left, right, (((0,), (0,)), ((), ())), preferred_element_type=F32
    )


def loop(count, body):
    def step(i, carry):
        body(i)
        return carry

    lax.fori_loop(0, count, step, 0)


def rows(start, size):
    return pl.ds(pl.multiple_of(start, size), size)


def unit_rows(values):
    values = values.astype(F32)
    scale = lax.rsqrt(jnp.sum(values * values, axis=1, keepdims=True) + eps)
    return values * scale, scale


def back_norm(grad, unit, scale):
    return scale * (grad - unit * jnp.sum(grad * unit, axis=1, keepdims=True))


def kernel(
    nb, nq,
    sf_hbm, tf_hbm, sp_hbm, tp_hbm,
    gp_out, gs_out,
    sf, tf, t_all, s_all, sp, anchor, pu, e, s, cs, tot, fa, fb, ra, rb, oa, ob, put, anct, ccol,
    r16, c16, w_src, w_mid, w_g1, w_g2, w_out, cx, b1y, b1z, c2y, c2z, b2y, b2z, sumf, xs, xr,
    lsem, near_s, near_r, nfwd_s, nfwd_r, tok_s, tok_r, fwd_s, fwd_r, spr_s, spr_r,
    a1_s, a1_r, a2_s, a2_r, out_s, g_r, f_r, sib_r,
    ra_s, ra_r, rb_s, rb_r, y1_s, y1_r, z1_s, z1_r, y2_s, y2_r, z2_s, z2_r, xr_s, xr_r, gs_s, gs_r,
):
    nx = nb // 2
    far_dx = nx // 2
    hx = nx // 2
    nz = NZ
    ny = nq // nz
    tl, depth = sf.shape
    tokens = tl * nb
    pl_rows = sp.shape[0]
    protos = pl_rows * nb * nq
    chunks = pl_rows // CH
    wide = tokens // 128
    piece = tl // nq
    plane = 2 * tl
    b, p = lax.axis_index("batch"), lax.axis_index("proto")
    x, c = b // 2, lax.rem(b, 2)
    y, z = p // nz, lax.rem(p, nz)

    def bat(dx, dc):
        return lax.rem(x + dx, nx) * 2 + lax.rem(c + dc, 2)

    def peer(j):
        return (b, lax.rem(p + j, nq))

    def remote(src, dst, ss, rs, to):
        return pltpu.make_async_remote_copy(
            src, dst, ss, rs, device_id=to, device_id_type=MESH
        )

    sibling = (bat(0, 1), p)

    barrier = pltpu.get_barrier_semaphore()
    for j in range(1, nb):
        pl.semaphore_signal(
            barrier, inc=1, device_id=(lax.rem(b + j, nb), p), device_id_type=MESH
        )
    for j in range(1, nq):
        pl.semaphore_signal(barrier, inc=1, device_id=peer(j), device_id_type=MESH)
    mine = rows(b * pl_rows, pl_rows)
    loads = [
        pltpu.make_async_copy(tf_hbm, tf, lsem.at[0]),
        pltpu.make_async_copy(sf_hbm, sf, lsem.at[1]),
        pltpu.make_async_copy(tp_hbm.at[mine], anchor, lsem.at[2]),
        pltpu.make_async_copy(sp_hbm.at[mine], sp, lsem.at[3]),
    ]
    for d in loads:
        d.start()

    def norm_into(src, dst, start, count):
        def body(i):
            unit, _ = unit_rows(src[rows(i * 128, 128), :])
            dst[rows(start + i * 128, 128), :] = unit.astype(BF)

        loop(count // 128, body)

    loads[0].wait()
    norm_into(tf, t_all, b * tl, tl)
    pl.semaphore_wait(barrier, nb + nq - 2)

    feats = (t_all, s_all)

    def near_copy(f, dx, h):
        part = feats[f].at[rows(b * tl + h * (tl // 2), tl // 2)]
        return remote(
            part, part, near_s.at[f, dx, h], near_r.at[f, dx, h], (bat(dx, 0), p)
        )

    def near_forward(f, dx, h):
        part = feats[f].at[rows(bat(nx - dx, 0) * tl + h * (tl // 2), tl // 2)]
        return remote(
            part, part, nfwd_s.at[f, dx, h], nfwd_r.at[f, dx, h], sibling
        )

    def token_copy(f, dx):
        start, size = b * tl, tl
        if dx == far_dx:
            start, size = b * tl + p * piece, piece
        part = feats[f].at[rows(start, size)]
        to = sibling if dx == 0 else (bat(dx, 0), p)
        return remote(part, part, tok_s.at[f, dx], tok_r.at[f, dx], to)

    def spread(f, j):
        part = feats[f].at[rows(bat(nx - far_dx, 0) * tl + p * piece, piece)]
        return remote(part, part, spr_s.at[f], spr_r.at[f], peer(j))

    def spread_all(f):
        part = feats[f].at[0 : tl - piece]
        return remote(part, part, spr_s.at[f], spr_r.at[f], sibling)

    def forward(f, dx):
        block = feats[f].at[rows(bat(nx - dx, 0) * tl, tl)]
        return remote(block, block, fwd_s.at[f, dx], fwd_r.at[f, dx], sibling)

    near = (1, nx - 1)

    def tokens_send(f):
        token_copy(f, far_dx).start()
        token_copy(f, 0).start()
        for h in range(2):
            for dx in near:
                near_copy(f, dx, h).start()

    def spread_start(f):
        token_copy(f, far_dx).wait_recv()
        for j in range(1, nq):
            spread(f, j).start()

    def spread_end(f):
        spread_all(f).wait_recv()
        forward(f, far_dx).start()

    def near_part(f, h):
        for dx in near:
            near_copy(f, dx, h).wait_recv()
            near_forward(f, dx, h).start()

    def tokens_drain(f):
        token_copy(f, far_dx).wait_send()
        token_copy(f, 0).wait_send()
        forward(f, far_dx).wait_send()
        for h in range(2):
            for dx in near:
                if f:
                    near_copy(f, dx, h).wait_send()
                near_forward(f, dx, h).wait_send()
        spread_all(f).wait_send()

    tokens_send(0)
    loads[2].wait()
    norm_into(anchor, anchor, 0, pl_rows)

    def exp_block(left, right, out, block, width, factor, accumulate, first):
        cols = pl.ds(pl.multiple_of(block * tl, width), width)

        def body(i):
            sl = rows(i * 256, 256)
            value = jnp.exp2(nt(left[sl, :], right[cols, :]) * factor)
            out[sl, cols] = value.astype(BF)
            accumulate(value, sl, cols, width, first)

        loop(pl_rows // 256, body)

    def col_acc(value, sl, cols, width, first):
        acc = value[:, 0:128]
        for q in range(1, width // 128):
            acc = acc + value[:, q * 128 : (q + 1) * 128]
        if first:
            cs[sl, :] = acc
        else:
            cs[sl, :] += acc

    def row_acc(value, sl, cols, width, first):
        tot[:, cols] += jnp.sum(value.reshape(32, 8, width), axis=0)

    def chip_block(dx):
        return lax.rem(x + nx - dx, nx) * 2

    def teacher_block(block, width, first=False):
        exp_block(anchor, t_all, e, block, width, LOG2E / teacher_temp, col_acc, first)

    def student_plane(dx):
        if dx == far_dx:
            forward(1, dx).wait_recv()
        elif dx:
            for h in range(2):
                near_forward(1, dx, h).wait_recv()
        else:
            token_copy(1, 0).wait_recv()
        exp_block(
            pu, s_all, s, chip_block(dx), plane, LOG2E / student_temp, row_acc, False
        )

    loads[1].wait()
    norm_into(sf, s_all, b * tl, tl)
    token_copy(0, 0).wait_recv()
    teacher_block(chip_block(0), plane, True)
    spread_start(0)
    loads[3].wait()

    def norm_protos(i):
        sl = rows(i * 128, 128)
        unit, _ = unit_rows(sp[sl, :])
        pu[sl, :] = unit.astype(BF)
        put[:, sl] = unit.T.astype(BF)

    loop(pl_rows // 128, norm_protos)
    tot[...] = jnp.zeros_like(tot)
    for h in range(2):
        for dx in near:
            near_copy(0, dx, h).wait_send()
    tokens_send(1)
    spread_end(0)
    near_part(0, 0)
    forward(0, far_dx).wait_recv()
    teacher_block(chip_block(far_dx), plane)
    near_part(0, 1)
    for dx in near:
        teacher_block(chip_block(dx) + c, tl)
    spread_start(1)
    for dx in near:
        for h in range(2):
            near_forward(0, dx, h).wait_recv()
        teacher_block(chip_block(dx) + 1 - c, tl)
    half = lax.broadcasted_iota(jnp.int32, (16, 128), 0) < 8

    def split_into(dst, j, row):
        high = row.astype(BF).astype(F32)
        dst[:, j * 128 : (j + 1) * 128] = jnp.where(half, high, row - high).astype(BF)

    def first_step(n, j=1):
        return remote(w_src.at[n], w_g1.at[n, j - 1], a1_s.at[n], a1_r.at[n],
                      (lax.rem(b + j, nb), p))

    def second_step(n, j=1):
        return remote(w_mid.at[n], w_g2.at[n, j - 1], a2_s.at[n], a2_r.at[n], peer(j))

    def first_all(n):
        return remote(w_g1.at[n], w_g1.at[n], a1_s.at[n], a1_r.at[n], sibling)

    def second_all(n):
        return remote(w_g2.at[n], w_g2.at[n], a2_s.at[n], a2_r.at[n], sibling)

    def reduce_start(n):
        for j in range(1, nb):
            first_step(n, j).start()

    def reduce_middle(n):
        first_all(n).wait_recv()
        value = w_src[n]
        for j in range(nb - 1):
            value = value + w_g1[n, j]
        w_mid[n] = value.astype(BF)
        for j in range(1, nq):
            second_step(n, j).start()

    def reduce_end(n):
        second_all(n).wait_recv()
        value = w_mid[n].astype(F32)
        for j in range(nq - 1):
            value = value + w_g2[n, j].astype(F32)
        return value

    def row_pass(n):
        out = nn(c16[...], e[...])
        line = out[0:1, :] + out[8:9, :]
        for j in range(wide):
            w_src[n, j : j + 1, :] = line[:, j * 128 : (j + 1) * 128]

    def col_pass(weights):
        for j in range(wide):
            split_into(r16, j, weights[j : j + 1, :])
        out = nt(r16[...], e[...])
        line = 1.0 / (protos * (out[0:1, :] + out[8:9, :]))
        return [line[:, j * 128 : (j + 1) * 128] for j in range(pl_rows // 128)]

    def feat_copy(buf, to, ss, rs, xx):
        return remote(buf.at[xx], to.at[xx], ss.at[xx], rs.at[xx], sibling)

    def feat_out(left, right, buf, to, ss, rs):
        def body(xx):
            cols = rows((xx * 2 + 1 - c) * tl, tl)
            buf[xx] = nn(left[...], right[:, cols]).astype(BF)
            feat_copy(buf, to, ss, rs, xx).start()

        loop(nx, body)

    def feat_own(left, right, out):
        def body(xx):
            cols = rows((xx * 2 + c) * tl, tl)
            out[xx] = nn(left[...], right[:, cols])

        loop(nx, body)

    for j in range(pl_rows // 128):
        sums = jnp.sum(cs[j * 128 : (j + 1) * 128, :].T, axis=0, keepdims=True)
        split_into(c16, j, 1.0 / (protos * sums))
    row_pass(0)
    reduce_start(0)
    student_plane(0)
    spread_end(1)
    reduce_middle(0)
    student_plane(far_dx)
    near_part(1, 0)
    near_part(1, 1)
    student_plane(near[0])
    student_plane(near[1])
    tokens_drain(0)
    weights = 1.0 / (tokens * reduce_end(0))
    for j, line in enumerate(col_pass(weights)):
        split_into(c16, j, line)
    row_pass(1)
    reduce_start(1)
    feat_out(put, s, oa, ra, ra_s, ra_r)
    reduce_middle(1)
    line = jnp.sum(tot[...], axis=0, keepdims=True)
    for j in range(wide):
        w_src[ITERS, j : j + 1, :] = line[:, j * 128 : (j + 1) * 128]
    reduce_start(ITERS)
    feat_own(put, s, fa)
    weights = 1.0 / (tokens * reduce_end(1))
    lines = col_pass(weights)
    for j, line in enumerate(lines):
        split_into(c16, j, line)
    row_pass(2)
    reduce_start(2)
    reduce_middle(ITERS)
    for j, line in enumerate(lines):
        sl = slice(j * 128, (j + 1) * 128)
        anct[:, sl] = (put[:, sl].astype(F32) * line).astype(BF)
    feat_out(anct, e, ob, rb, rb_s, rb_r)
    reduce_middle(2)
    feat_own(anct, e, fb)
    w_out[wide : 2 * wide, :] = 1.0 / (student_temp * tokens * reduce_end(ITERS))
    for j, line in enumerate(lines):
        ccol[j * 128 : (j + 1) * 128, :] = jnp.broadcast_to(line, (128, 128)).T

    def column(j):
        return jnp.broadcast_to(w_out[pl.ds(j, 1), :], (128, 128)).T[:, 0:1]

    def student_weights(j):
        sl = rows(j * 128, 128)
        t_all[sl, :] = (s_all[sl, :].astype(F32) * column(wide + j)).astype(BF)

    loop(wide, student_weights)
    tokens_drain(1)
    for xx in range(nx):
        feat_copy(oa, ra, ra_s, ra_r, xx).wait()
        feat_copy(ob, rb, rb_s, rb_r, xx).wait()
    w_out[0:wide, :] = (1.0 / student_temp) / (tokens * reduce_end(2))

    def teacher_weights(j):
        sl = rows(j * 128, 128)
        s_all[sl, :] = (s_all[sl, :].astype(F32) * column(j)).astype(BF)

    loop(wide, teacher_weights)

    span = 2 * CH
    groups = pl_rows // span

    def chunk_send(q, k):
        to = (bat(1, 0), p) if k == 0 else (bat(nx - 1, 0), p)
        part = gp_out.at[rows(b * pl_rows + q * CH, CH)]
        return remote(part, part, out_s.at[0], g_r.at[k, q], to)

    def group_forward(g, k):
        block = bat(nx - 1, 0) if k == 0 else bat(1, 0)
        to = (bat(1, 0), p) if k == 0 else (bat(nx - 1, 0), p)
        part = gp_out.at[rows(block * pl_rows + g * span + k * CH, CH)]
        return remote(part, part, out_s.at[0], f_r.at[k, g], to)

    def group_sibling(g, k):
        block = bat((nx - 1, 1, 2)[k], 0)
        part = gp_out.at[rows(block * pl_rows + g * span, span)]
        return remote(part, part, out_s.at[0], sib_r.at[0], sibling)

    def own_sibling():
        part = gp_out.at[rows(b * pl_rows, pl_rows)]
        return remote(part, part, out_s.at[0], sib_r.at[0], sibling)

    def chunk_compute(q):
        sl = rows(q * CH, CH)
        back = nn(s[sl, :], t_all[...]) - ccol[sl, 0:1] * nn(e[sl, :], s_all[...])
        unit, scale = unit_rows(sp[sl, :])
        value = back_norm(back, unit, scale).astype(BF)
        gp_out[rows(b * pl_rows + q * CH, CH), :] = value
        chunk_send(q, 0).start()
        chunk_send(q, 1).start()

    def group_recv(g):
        for k in range(2):
            chunk_send(2 * g, k).wait_recv()
            chunk_send(2 * g + 1, k).wait_recv()
            group_forward(g, k).start()
            group_sibling(g, k).start()

    def group_last(g):
        for k in range(2):
            group_forward(g, k).wait_recv()
        group_sibling(g, 2).start()

    loop(2, chunk_compute)

    group = tl // 128

    def combine(i):
        xx, g = i // group, lax.rem(i, group)
        sl = rows(g * 128, 128)
        j = (xx * 2 + c) * group + g
        value = (fa[xx, :, sl] + ra[xx, :, sl].astype(F32)) * w_out[pl.ds(wide + j, 1), :]
        value = value - (fb[xx, :, sl] + rb[xx, :, sl].astype(F32)) * w_out[pl.ds(j, 1), :]
        cx[xx, g] = value.T.astype(BF).reshape(nz, piece, depth)

    loop(nx * group, combine)
    def feat_send(src, dst, ss, rs, to):
        remote(src, dst, ss, rs, to).start()

    def whole(buf, ss, rs):
        return remote(buf, buf, ss.at[0], rs.at[0], sibling)

    first = [whole(b1y, y1_s, y1_r), whole(b1z, z1_s, z1_r)]
    second = [whole(b2y, z2_s, z2_r), whole(b2z, y2_s, y2_r)]
    third = whole(xr, xr_s, xr_r)
    final = remote(
        gs_out.at[0 : tl - piece], gs_out.at[0 : tl - piece],
        gs_s.at[0], gs_r.at[0], sibling,
    )

    def along_y(d):
        return lax.rem(y + d, ny)

    def along_z(d):
        return lax.rem(z + d, nz)

    for d in range(1, ny):
        feat_send(cx.at[0:hx, along_y(d)], b1y.at[d - 1], y1_s.at[0],
                  y1_r.at[0], (b, along_y(d) * nz + z))
    for d in range(1, nz):
        feat_send(cx.at[hx:nx, :, along_z(d)], b1z.at[d - 1], z1_s.at[0],
                  z1_r.at[0], (b, y * nz + along_z(d)))

    def feat_middle():
        for d in first:
            d.wait_recv()
        for h in range(hx):
            value = cx[h, y].astype(F32)
            for d in range(ny - 1):
                value = value + b1y[d, h].astype(F32)
            c2y[h] = value.astype(BF)
            value = cx[hx + h, :, z].astype(F32)
            for d in range(nz - 1):
                value = value + b1z[d, h].astype(F32)
            c2z[h] = value.astype(BF)
        for d in range(1, nz):
            feat_send(c2y.at[:, along_z(d)], b2y.at[d - 1], z2_s.at[0],
                      z2_r.at[0], (b, y * nz + along_z(d)))
        for d in range(1, ny):
            feat_send(c2z.at[:, along_y(d)], b2z.at[d - 1], y2_s.at[0],
                      y2_r.at[0], (b, along_y(d) * nz + z))

    def feat_x():
        for d in second:
            d.wait_recv()
        value = c2y[:, z].astype(F32)
        for d in range(nz - 1):
            value = value + b2y[d].astype(F32)
        sumf[0:hx] = value
        xs[0:hx] = value.astype(BF)
        value = c2z[:, y].astype(F32)
        for d in range(ny - 1):
            value = value + b2z[d].astype(F32)
        sumf[hx:nx] = value
        xs[hx:nx] = value.astype(BF)
        for dx in range(1, nx):
            feat_send(xs.at[lax.rem(x + dx, nx)], xr.at[dx - 1],
                      xr_s.at[0], xr_r.at[0], (bat(dx, 0), p))

    def feat_last():
        third.wait_recv()
        value = sumf[x]
        for dx in range(nx - 1):
            value = value + xr[dx].astype(F32)
        own = rows(p * piece, piece)
        unit, scale = unit_rows(sf[own, :])
        gs_out[own, :] = back_norm(value, unit, scale).astype(BF)
        part = gs_out.at[own]
        for j in range(1, nq):
            feat_send(part, part, gs_s.at[0], gs_r.at[0], peer(j))

    loop(chunks - 2, lambda q: chunk_compute(q + 2))
    own_sibling().start()
    feat_middle()
    loop(groups, group_recv)
    feat_x()
    loop(groups // 2, group_last)
    feat_last()
    loop(groups // 2, lambda g: group_last(g + groups // 2))

    for n in range(ITERS + 1):
        first_all(n).wait_send()
        second_all(n).wait_send()
    for d in first + second + [third, final]:
        d.wait_send()
    sent = gp_out.at[0 : pl_rows * (nx + 3)]
    remote(sent, sent, out_s.at[0], sib_r.at[0], sibling).wait_send()
    held = gp_out.at[0 : pl_rows * nx]
    remote(held, held, out_s.at[0], sib_r.at[0], sibling).wait_recv()
    final.wait_recv()


def on_device(nb, nq, student_feats, teacher_feats, student_protos, teacher_protos):
    tl, depth = student_feats.shape
    pl_rows = student_protos.shape[0] // nb
    tokens = tl * nb
    chunks = pl_rows // CH
    wide = tokens // 128
    nx = nb // 2
    piece = tl // nq
    vm = pltpu.VMEM
    dma = pltpu.SemaphoreType.DMA
    hx, nz = nx // 2, NZ
    ny = nq // nz
    scratch = [
        vm((tl, depth), BF),
        vm((tl, depth), BF),
        vm((tokens, depth), BF),
        vm((tokens, depth), BF),
        vm((pl_rows, depth), BF),
        vm((pl_rows, depth), BF),
        vm((pl_rows, depth), BF),
        vm((pl_rows, tokens), BF),
        vm((pl_rows, tokens), BF),
        vm((pl_rows, 128), F32),
        vm((8, tokens), F32),
        vm((nx, depth, tl), F32),
        vm((nx, depth, tl), F32),
        vm((nx, depth, tl), BF),
        vm((nx, depth, tl), BF),
        vm((nx, depth, tl), BF),
        vm((nx, depth, tl), BF),
        vm((depth, pl_rows), BF),
        vm((depth, pl_rows), BF),
        vm((pl_rows, 128), F32),
        vm((16, tokens), BF),
        vm((16, pl_rows), BF),
        vm((ITERS + 1, wide, 128), F32),
        vm((ITERS + 1, wide, 128), BF),
        vm((ITERS + 1, nb - 1, wide, 128), F32),
        vm((ITERS + 1, nq - 1, wide, 128), BF),
        vm((2 * wide, 128), F32),
        vm((nx, ny, nz, piece, depth), BF),
        vm((ny - 1, hx, nz, piece, depth), BF),
        vm((nz - 1, hx, ny, piece, depth), BF),
        vm((hx, nz, piece, depth), BF),
        vm((hx, ny, piece, depth), BF),
        vm((nz - 1, hx, piece, depth), BF),
        vm((ny - 1, hx, piece, depth), BF),
        vm((nx, piece, depth), F32),
        vm((nx, piece, depth), BF),
        vm((nx - 1, piece, depth), BF),
        dma((4,)),
        dma((2, nx, 2)), dma((2, nx, 2)), dma((2, nx, 2)), dma((2, nx, 2)),
        dma((2, nx)), dma((2, nx)), dma((2, nx)), dma((2, nx)),
        dma((2,)), dma((2,)),
        dma((ITERS + 1,)), dma((ITERS + 1,)),
        dma((ITERS + 1,)), dma((ITERS + 1,)),
        dma((1,)), dma((2, chunks)), dma((2, chunks // 2)), dma((1,)),
        dma((nx,)), dma((nx,)), dma((nx,)), dma((nx,)),
        dma((1,)), dma((1,)), dma((1,)), dma((1,)), dma((1,)), dma((1,)),
        dma((1,)), dma((1,)), dma((1,)), dma((1,)), dma((1,)), dma((1,)),
    ]
    in_vmem = pl.BlockSpec(memory_space=pltpu.VMEM)
    anywhere = pl.BlockSpec(memory_space=pl.ANY)
    return pl.pallas_call(
        functools.partial(kernel, nb, nq),
        out_shape=[
            pltpu.VMEM(student_protos.shape, BF),
            pltpu.VMEM(student_feats.shape, BF),
        ],
        in_specs=[anywhere] * 4,
        out_specs=[in_vmem, in_vmem],
        scratch_shapes=scratch,
        compiler_params=pltpu.CompilerParams(
            collective_id=0, has_side_effects=True, vmem_limit_bytes=54 << 20
        ),
        name="prototype_head",
    )(student_feats, teacher_feats, student_protos, teacher_protos)


def solution(mesh):
    nb, nq = mesh.shape["batch"], mesh.shape["proto"]
    in_specs = (P("batch", None), P("batch", None), P("proto", None), P("proto", None))
    out_specs = (P("proto", None), P("batch", None))
    return jax.shard_map(
        functools.partial(on_device, nb, nq),
        mesh=mesh, in_specs=in_specs, out_specs=out_specs, check_vma=False,
    )
```

```python
import functools

import jax
import jax.numpy as jnp
from jax import lax
from jax.experimental import pallas as pl
from jax.experimental.pallas import tpu as pltpu
from jax.sharding import PartitionSpec as P

ITERS = 3
eps = 1e-06
teacher_temp = 0.04
student_temp = 0.1
LOG2E = 1.4426950408889634
F32 = jnp.float32
BF = jnp.bfloat16
MESH = pl.DeviceIdType.MESH
CH = 128
NZ = 4


def nt(left, right):
    return lax.dot_general(
        left, right, (((1,), (1,)), ((), ())), preferred_element_type=F32
    )


def nn(left, right):
    return jnp.dot(left, right, preferred_element_type=F32)


def tn(left, right):
    return lax.dot_general(
        left, right, (((0,), (0,)), ((), ())), preferred_element_type=F32
    )


def loop(count, body):
    def step(i, carry):
        body(i)
        return carry

    lax.fori_loop(0, count, step, 0)


def rows(start, size):
    return pl.ds(pl.multiple_of(start, size), size)


def unit_rows(values):
    values = values.astype(F32)
    scale = lax.rsqrt(jnp.sum(values * values, axis=1, keepdims=True) + eps)
    return values * scale, scale


def back_norm(grad, unit, scale):
    return scale * (grad - unit * jnp.sum(grad * unit, axis=1, keepdims=True))


def kernel(
    nb, nq,
    sf_hbm, tf_hbm, sp_hbm, tp_hbm,
    gp_out, gs_out,
    sf, tf, t_all, s_all, sp, anchor, pu, e, s, cs, tot, fa, fb, ra, rb, oa, ob, put, anct, ccol,
    r16, c16, w_src, w_mid, w_g1, w_g2, w_out, cx, b1y, b1z, c2y, c2z, b2y, b2z, sumf, xs, xr,
    lsem, near_s, near_r, nfwd_s, nfwd_r, tok_s, tok_r, fwd_s, fwd_r, spr_s, spr_r,
    a1_s, a1_r, a2_s, a2_r, out_s, g_r, f_r, sib_r,
    ra_s, ra_r, rb_s, rb_r, y1_s, y1_r, z1_s, z1_r, y2_s, y2_r, z2_s, z2_r, xr_s, xr_r, gs_s, gs_r,
):
    nx = nb // 2
    far_dx = nx // 2
    hx = nx // 2
    nz = NZ
    ny = nq // nz
    tl, depth = sf.shape
    tokens = tl * nb
    pl_rows = sp.shape[0]
    protos = pl_rows * nb * nq
    chunks = pl_rows // CH
    wide = tokens // 128
    piece = tl // nq
    plane = 2 * tl
    b, p = lax.axis_index("batch"), lax.axis_index("proto")
    x, c = b // 2, lax.rem(b, 2)
    y, z = p // nz, lax.rem(p, nz)

    def bat(dx, dc):
        return lax.rem(x + dx, nx) * 2 + lax.rem(c + dc, 2)

    def peer(j):
        return (b, lax.rem(p + j, nq))

    def remote(src, dst, ss, rs, to):
        return pltpu.make_async_remote_copy(
            src, dst, ss, rs, device_id=to, device_id_type=MESH
        )

    sibling = (bat(0, 1), p)

    barrier = pltpu.get_barrier_semaphore()
    for j in range(1, nb):
        pl.semaphore_signal(
            barrier, inc=1, device_id=(lax.rem(b + j, nb), p), device_id_type=MESH
        )
    for j in range(1, nq):
        pl.semaphore_signal(barrier, inc=1, device_id=peer(j), device_id_type=MESH)
    mine = rows(b * pl_rows, pl_rows)
    loads = [
        pltpu.make_async_copy(tf_hbm, tf, lsem.at[0]),
        pltpu.make_async_copy(sf_hbm, sf, lsem.at[1]),
        pltpu.make_async_copy(tp_hbm.at[mine], anchor, lsem.at[2]),
        pltpu.make_async_copy(sp_hbm.at[mine], sp, lsem.at[3]),
    ]
    for d in loads:
        d.start()

    def norm_into(src, dst, start, count):
        def body(i):
            unit, _ = unit_rows(src[rows(i * 128, 128), :])
            dst[rows(start + i * 128, 128), :] = unit.astype(BF)

        loop(count // 128, body)

    loads[0].wait()
    norm_into(tf, t_all, b * tl, tl)
    pl.semaphore_wait(barrier, nb + nq - 2)

    feats = (t_all, s_all)

    def near_copy(f, dx, h):
        part = feats[f].at[rows(b * tl + h * (tl // 2), tl // 2)]
        return remote(
            part, part, near_s.at[f, dx, h], near_r.at[f, dx, h], (bat(dx, 0), p)
        )

    def near_forward(f, dx, h):
        part = feats[f].at[rows(bat(nx - dx, 0) * tl + h * (tl // 2), tl // 2)]
        return remote(
            part, part, nfwd_s.at[f, dx, h], nfwd_r.at[f, dx, h], sibling
        )

    def token_copy(f, dx):
        start, size = b * tl, tl
        if dx == far_dx:
            start, size = b * tl + p * piece, piece
        part = feats[f].at[rows(start, size)]
        to = sibling if dx == 0 else (bat(dx, 0), p)
        return remote(part, part, tok_s.at[f, dx], tok_r.at[f, dx], to)

    def spread(f, j):
        part = feats[f].at[rows(bat(nx - far_dx, 0) * tl + p * piece, piece)]
        return remote(part, part, spr_s.at[f], spr_r.at[f], peer(j))

    def spread_all(f):
        part = feats[f].at[0 : tl - piece]
        return remote(part, part, spr_s.at[f], spr_r.at[f], sibling)

    def forward(f, dx):
        block = feats[f].at[rows(bat(nx - dx, 0) * tl, tl)]
        return remote(block, block, fwd_s.at[f, dx], fwd_r.at[f, dx], sibling)

    near = (1, nx - 1)

    def tokens_send(f):
        token_copy(f, far_dx).start()
        token_copy(f, 0).start()
        for h in range(2):
            for dx in near:
                near_copy(f, dx, h).start()

    def spread_start(f):
        token_copy(f, far_dx).wait_recv()
        for j in range(1, nq):
            spread(f, j).start()

    def spread_end(f):
        spread_all(f).wait_recv()
        forward(f, far_dx).start()

    def near_part(f, h):
        for dx in near:
            near_copy(f, dx, h).wait_recv()
            near_forward(f, dx, h).start()

    def tokens_drain(f):
        token_copy(f, far_dx).wait_send()
        token_copy(f, 0).wait_send()
        forward(f, far_dx).wait_send()
        for h in range(2):
            for dx in near:
                if f:
                    near_copy(f, dx, h).wait_send()
                near_forward(f, dx, h).wait_send()
        spread_all(f).wait_send()

    tokens_send(0)
    loads[2].wait()
    norm_into(anchor, anchor, 0, pl_rows)

    def exp_block(left, right, out, block, width, factor, accumulate, first):
        cols = pl.ds(pl.multiple_of(block * tl, width), width)

        def body(i):
            sl = rows(i * 256, 256)
            value = jnp.exp2(nt(left[sl, :], right[cols, :]) * factor)
            out[sl, cols] = value.astype(BF)
            accumulate(value, sl, cols, width, first)

        loop(pl_rows // 256, body)

    def col_acc(value, sl, cols, width, first):
        acc = value[:, 0:128]
        for q in range(1, width // 128):
            acc = acc + value[:, q * 128 : (q + 1) * 128]
        if first:
            cs[sl, :] = acc
        else:
            cs[sl, :] += acc

    def row_acc(value, sl, cols, width, first):
        tot[:, cols] += jnp.sum(value.reshape(32, 8, width), axis=0)

    def chip_block(dx):
        return lax.rem(x + nx - dx, nx) * 2

    def teacher_block(block, width, first=False):
        exp_block(anchor, t_all, e, block, width, LOG2E / teacher_temp, col_acc, first)

    def student_plane(dx):
        if dx == far_dx:
            forward(1, dx).wait_recv()
        elif dx:
            for h in range(2):
                near_forward(1, dx, h).wait_recv()
        else:
            token_copy(1, 0).wait_recv()
        exp_block(
            pu, s_all, s, chip_block(dx), plane, LOG2E / student_temp, row_acc, False
        )

    loads[1].wait()
    norm_into(sf, s_all, b * tl, tl)
    token_copy(0, 0).wait_recv()
    teacher_block(chip_block(0), plane, True)
    spread_start(0)
    loads[3].wait()

    def norm_protos(i):
        sl = rows(i * 128, 128)
        unit, _ = unit_rows(sp[sl, :])
        pu[sl, :] = unit.astype(BF)
        put[:, sl] = unit.T.astype(BF)

    loop(pl_rows // 128, norm_protos)
    tot[...] = jnp.zeros_like(tot)
    for h in range(2):
        for dx in near:
            near_copy(0, dx, h).wait_send()
    tokens_send(1)
    spread_end(0)
    near_part(0, 0)
    forward(0, far_dx).wait_recv()
    teacher_block(chip_block(far_dx), plane)
    near_part(0, 1)
    for dx in near:
        teacher_block(chip_block(dx) + c, tl)
    spread_start(1)
    for dx in near:
        for h in range(2):
            near_forward(0, dx, h).wait_recv()
        teacher_block(chip_block(dx) + 1 - c, tl)
    half = lax.broadcasted_iota(jnp.int32, (16, 128), 0) < 8

    def split_into(dst, j, row):
        high = row.astype(BF).astype(F32)
        dst[:, j * 128 : (j + 1) * 128] = jnp.where(half, high, row - high).astype(BF)

    def first_step(n, j=1):
        return remote(w_src.at[n], w_g1.at[n, j - 1], a1_s.at[n], a1_r.at[n],
                      (lax.rem(b + j, nb), p))

    def second_step(n, j=1):
        return remote(w_mid.at[n], w_g2.at[n, j - 1], a2_s.at[n], a2_r.at[n], peer(j))

    def first_all(n):
        return remote(w_g1.at[n], w_g1.at[n], a1_s.at[n], a1_r.at[n], sibling)

    def second_all(n):
        return remote(w_g2.at[n], w_g2.at[n], a2_s.at[n], a2_r.at[n], sibling)

    def reduce_start(n):
        for j in range(1, nb):
            first_step(n, j).start()

    def reduce_middle(n):
        first_all(n).wait_recv()
        value = w_src[n]
        for j in range(nb - 1):
            value = value + w_g1[n, j]
        w_mid[n] = value.astype(BF)
        for j in range(1, nq):
            second_step(n, j).start()

    def reduce_end(n):
        second_all(n).wait_recv()
        value = w_mid[n].astype(F32)
        for j in range(nq - 1):
            value = value + w_g2[n, j].astype(F32)
        return value

    def row_pass(n):
        out = nn(c16[...], e[...])
        line = out[0:1, :] + out[8:9, :]
        for j in range(wide):
            w_src[n, j : j + 1, :] = line[:, j * 128 : (j + 1) * 128]

    def col_pass(weights):
        for j in range(wide):
            split_into(r16, j, weights[j : j + 1, :])
        out = nt(r16[...], e[...])
        line = 1.0 / (protos * (out[0:1, :] + out[8:9, :]))
        return [line[:, j * 128 : (j + 1) * 128] for j in range(pl_rows // 128)]

    def feat_copy(buf, to, ss, rs, xx):
        return remote(buf.at[xx], to.at[xx], ss.at[xx], rs.at[xx], sibling)

    def feat_out(left, right, buf, to, ss, rs):
        def body(xx):
            cols = rows((xx * 2 + 1 - c) * tl, tl)
            buf[xx] = nn(left[...], right[:, cols]).astype(BF)
            feat_copy(buf, to, ss, rs, xx).start()

        loop(nx, body)

    def feat_own(left, right, out):
        def body(xx):
            cols = rows((xx * 2 + c) * tl, tl)
            out[xx] = nn(left[...], right[:, cols])

        loop(nx, body)

    for j in range(pl_rows // 128):
        sums = jnp.sum(cs[j * 128 : (j + 1) * 128, :].T, axis=0, keepdims=True)
        split_into(c16, j, 1.0 / (protos * sums))
    row_pass(0)
    reduce_start(0)
    student_plane(0)
    spread_end(1)
    reduce_middle(0)
    student_plane(far_dx)
    near_part(1, 0)
    near_part(1, 1)
    student_plane(near[0])
    student_plane(near[1])
    tokens_drain(0)
    weights = 1.0 / (tokens * reduce_end(0))
    for j, line in enumerate(col_pass(weights)):
        split_into(c16, j, line)
    row_pass(1)
    reduce_start(1)
    feat_out(put, s, oa, ra, ra_s, ra_r)
    reduce_middle(1)
    line = jnp.sum(tot[...], axis=0, keepdims=True)
    for j in range(wide):
        w_src[ITERS, j : j + 1, :] = line[:, j * 128 : (j + 1) * 128]
    reduce_start(ITERS)
    feat_own(put, s, fa)
    weights = 1.0 / (tokens * reduce_end(1))
    lines = col_pass(weights)
    for j, line in enumerate(lines):
        split_into(c16, j, line)
    row_pass(2)
    reduce_start(2)
    reduce_middle(ITERS)
    for j, line in enumerate(lines):
        sl = slice(j * 128, (j + 1) * 128)
        anct[:, sl] = (put[:, sl].astype(F32) * line).astype(BF)
    feat_out(anct, e, ob, rb, rb_s, rb_r)
    reduce_middle(2)
    feat_own(anct, e, fb)
    w_out[wide : 2 * wide, :] = 1.0 / (student_temp * tokens * reduce_end(ITERS))
    for j, line in enumerate(lines):
        ccol[j * 128 : (j + 1) * 128, :] = jnp.broadcast_to(line, (128, 128)).T

    def column(j):
        return jnp.broadcast_to(w_out[pl.ds(j, 1), :], (128, 128)).T[:, 0:1]

    def student_weights(j):
        sl = rows(j * 128, 128)
        t_all[sl, :] = (s_all[sl, :].astype(F32) * column(wide + j)).astype(BF)

    loop(wide, student_weights)
    tokens_drain(1)
    for xx in range(nx):
        feat_copy(oa, ra, ra_s, ra_r, xx).wait()
        feat_copy(ob, rb, rb_s, rb_r, xx).wait()
    w_out[0:wide, :] = (1.0 / student_temp) / (tokens * reduce_end(2))

    group = tl // 128

    def combine(i):
        xx, g = i // group, lax.rem(i, group)
        sl = rows(g * 128, 128)
        j = (xx * 2 + c) * group + g
        value = (fa[xx, :, sl] + ra[xx, :, sl].astype(F32)) * w_out[pl.ds(wide + j, 1), :]
        value = value - (fb[xx, :, sl] + rb[xx, :, sl].astype(F32)) * w_out[pl.ds(j, 1), :]
        cx[xx, g] = value.T.astype(BF).reshape(nz, piece, depth)

    loop(nx * group, combine)
    def feat_send(src, dst, ss, rs, to):
        remote(src, dst, ss, rs, to).start()

    def whole(buf, ss, rs):
        return remote(buf, buf, ss.at[0], rs.at[0], sibling)

    first = [whole(b1y, y1_s, y1_r), whole(b1z, z1_s, z1_r)]
    second = [whole(b2y, z2_s, z2_r), whole(b2z, y2_s, y2_r)]
    third = whole(xr, xr_s, xr_r)
    final = remote(
        gs_out.at[0 : tl - piece], gs_out.at[0 : tl - piece],
        gs_s.at[0], gs_r.at[0], sibling,
    )

    def along_y(d):
        return lax.rem(y + d, ny)

    def along_z(d):
        return lax.rem(z + d, nz)

    for d in range(1, ny):
        feat_send(cx.at[0:hx, along_y(d)], b1y.at[d - 1], y1_s.at[0],
                  y1_r.at[0], (b, along_y(d) * nz + z))
    for d in range(1, nz):
        feat_send(cx.at[hx:nx, :, along_z(d)], b1z.at[d - 1], z1_s.at[0],
                  z1_r.at[0], (b, y * nz + along_z(d)))

    def feat_middle():
        for d in first:
            d.wait_recv()
        for h in range(hx):
            value = cx[h, y].astype(F32)
            for d in range(ny - 1):
                value = value + b1y[d, h].astype(F32)
            c2y[h] = value.astype(BF)
            value = cx[hx + h, :, z].astype(F32)
            for d in range(nz - 1):
                value = value + b1z[d, h].astype(F32)
            c2z[h] = value.astype(BF)
        for d in range(1, nz):
            feat_send(c2y.at[:, along_z(d)], b2y.at[d - 1], z2_s.at[0],
                      z2_r.at[0], (b, y * nz + along_z(d)))
        for d in range(1, ny):
            feat_send(c2z.at[:, along_y(d)], b2z.at[d - 1], y2_s.at[0],
                      y2_r.at[0], (b, along_y(d) * nz + z))

    def feat_x():
        for d in second:
            d.wait_recv()
        value = c2y[:, z].astype(F32)
        for d in range(nz - 1):
            value = value + b2y[d].astype(F32)
        sumf[0:hx] = value
        xs[0:hx] = value.astype(BF)
        value = c2z[:, y].astype(F32)
        for d in range(ny - 1):
            value = value + b2z[d].astype(F32)
        sumf[hx:nx] = value
        xs[hx:nx] = value.astype(BF)
        for dx in range(1, nx):
            feat_send(xs.at[lax.rem(x + dx, nx)], xr.at[dx - 1],
                      xr_s.at[0], xr_r.at[0], (bat(dx, 0), p))

    def feat_last():
        third.wait_recv()
        value = sumf[x]
        for dx in range(nx - 1):
            value = value + xr[dx].astype(F32)
        own = rows(p * piece, piece)
        unit, scale = unit_rows(sf[own, :])
        gs_out[own, :] = back_norm(value, unit, scale).astype(BF)
        part = gs_out.at[own]
        for j in range(1, nq):
            feat_send(part, part, gs_s.at[0], gs_r.at[0], peer(j))

    def teacher_weights(j):
        sl = rows(j * 128, 128)
        s_all[sl, :] = (s_all[sl, :].astype(F32) * column(j)).astype(BF)

    loop(wide, teacher_weights)

    span = 2 * CH
    groups = pl_rows // span

    def chunk_send(q, k):
        to = (bat(1, 0), p) if k == 0 else (bat(nx - 1, 0), p)
        part = gp_out.at[rows(b * pl_rows + q * CH, CH)]
        return remote(part, part, out_s.at[0], g_r.at[k, q], to)

    def group_forward(g, k):
        block = bat(nx - 1, 0) if k == 0 else bat(1, 0)
        to = (bat(1, 0), p) if k == 0 else (bat(nx - 1, 0), p)
        part = gp_out.at[rows(block * pl_rows + g * span + k * CH, CH)]
        return remote(part, part, out_s.at[0], f_r.at[k, g], to)

    def group_sibling(g, k):
        block = bat((nx - 1, 1, 2)[k], 0)
        part = gp_out.at[rows(block * pl_rows + g * span, span)]
        return remote(part, part, out_s.at[0], sib_r.at[0], sibling)

    def own_sibling():
        part = gp_out.at[rows(b * pl_rows, pl_rows)]
        return remote(part, part, out_s.at[0], sib_r.at[0], sibling)

    def chunk_compute(q):
        sl = rows(q * CH, CH)
        back = nn(s[sl, :], t_all[...]) - ccol[sl, 0:1] * nn(e[sl, :], s_all[...])
        unit, scale = unit_rows(sp[sl, :])
        value = back_norm(back, unit, scale).astype(BF)
        gp_out[rows(b * pl_rows + q * CH, CH), :] = value
        chunk_send(q, 0).start()
        chunk_send(q, 1).start()

    def group_recv(g):
        for k in range(2):
            chunk_send(2 * g, k).wait_recv()
            chunk_send(2 * g + 1, k).wait_recv()
            group_forward(g, k).start()
            group_sibling(g, k).start()

    def group_last(g):
        for k in range(2):
            group_forward(g, k).wait_recv()
        group_sibling(g, 2).start()

    loop(5, chunk_compute)
    feat_middle()
    loop(chunks - 5, lambda q: chunk_compute(q + 5))
    own_sibling().start()
    feat_x()
    loop(groups - 1, group_recv)
    feat_last()
    group_recv(groups - 1)
    loop(groups, group_last)

    for n in range(ITERS + 1):
        first_all(n).wait_send()
        second_all(n).wait_send()
    for d in first + second + [third, final]:
        d.wait_send()
    sent = gp_out.at[0 : pl_rows * (nx + 3)]
    remote(sent, sent, out_s.at[0], sib_r.at[0], sibling).wait_send()
    held = gp_out.at[0 : pl_rows * nx]
    remote(held, held, out_s.at[0], sib_r.at[0], sibling).wait_recv()
    final.wait_recv()


def on_device(nb, nq, student_feats, teacher_feats, student_protos, teacher_protos):
    tl, depth = student_feats.shape
    pl_rows = student_protos.shape[0] // nb
    tokens = tl * nb
    chunks = pl_rows // CH
    wide = tokens // 128
    nx = nb // 2
    piece = tl // nq
    vm = pltpu.VMEM
    dma = pltpu.SemaphoreType.DMA
    hx, nz = nx // 2, NZ
    ny = nq // nz
    scratch = [
        vm((tl, depth), BF),
        vm((tl, depth), BF),
        vm((tokens, depth), BF),
        vm((tokens, depth), BF),
        vm((pl_rows, depth), BF),
        vm((pl_rows, depth), BF),
        vm((pl_rows, depth), BF),
        vm((pl_rows, tokens), BF),
        vm((pl_rows, tokens), BF),
        vm((pl_rows, 128), F32),
        vm((8, tokens), F32),
        vm((nx, depth, tl), F32),
        vm((nx, depth, tl), F32),
        vm((nx, depth, tl), BF),
        vm((nx, depth, tl), BF),
        vm((nx, depth, tl), BF),
        vm((nx, depth, tl), BF),
        vm((depth, pl_rows), BF),
        vm((depth, pl_rows), BF),
        vm((pl_rows, 128), F32),
        vm((16, tokens), BF),
        vm((16, pl_rows), BF),
        vm((ITERS + 1, wide, 128), F32),
        vm((ITERS + 1, wide, 128), BF),
        vm((ITERS + 1, nb - 1, wide, 128), F32),
        vm((ITERS + 1, nq - 1, wide, 128), BF),
        vm((2 * wide, 128), F32),
        vm((nx, ny, nz, piece, depth), BF),
        vm((ny - 1, hx, nz, piece, depth), BF),
        vm((nz - 1, hx, ny, piece, depth), BF),
        vm((hx, nz, piece, depth), BF),
        vm((hx, ny, piece, depth), BF),
        vm((nz - 1, hx, piece, depth), BF),
        vm((ny - 1, hx, piece, depth), BF),
        vm((nx, piece, depth), F32),
        vm((nx, piece, depth), BF),
        vm((nx - 1, piece, depth), BF),
        dma((4,)),
        dma((2, nx, 2)), dma((2, nx, 2)), dma((2, nx, 2)), dma((2, nx, 2)),
        dma((2, nx)), dma((2, nx)), dma((2, nx)), dma((2, nx)),
        dma((2,)), dma((2,)),
        dma((ITERS + 1,)), dma((ITERS + 1,)),
        dma((ITERS + 1,)), dma((ITERS + 1,)),
        dma((1,)), dma((2, chunks)), dma((2, chunks // 2)), dma((1,)),
        dma((nx,)), dma((nx,)), dma((nx,)), dma((nx,)),
        dma((1,)), dma((1,)), dma((1,)), dma((1,)), dma((1,)), dma((1,)),
        dma((1,)), dma((1,)), dma((1,)), dma((1,)), dma((1,)), dma((1,)),
    ]
    in_vmem = pl.BlockSpec(memory_space=pltpu.VMEM)
    anywhere = pl.BlockSpec(memory_space=pl.ANY)
    return pl.pallas_call(
        functools.partial(kernel, nb, nq),
        out_shape=[
            pltpu.VMEM(student_protos.shape, BF),
            pltpu.VMEM(student_feats.shape, BF),
        ],
        in_specs=[anywhere] * 4,
        out_specs=[in_vmem, in_vmem],
        scratch_shapes=scratch,
        compiler_params=pltpu.CompilerParams(
            collective_id=0, has_side_effects=True, vmem_limit_bytes=54 << 20
        ),
        name="prototype_head",
    )(student_feats, teacher_feats, student_protos, teacher_protos)


def solution(mesh):
    nb, nq = mesh.shape["batch"], mesh.shape["proto"]
    in_specs = (P("batch", None), P("batch", None), P("proto", None), P("proto", None))
    out_specs = (P("proto", None), P("batch", None))
    return jax.shard_map(
        functools.partial(on_device, nb, nq),
        mesh=mesh, in_specs=in_specs, out_specs=out_specs, check_vma=False,
    )
```

```python
import functools

import jax
import jax.numpy as jnp
from jax import lax
from jax.experimental import pallas as pl
from jax.experimental.pallas import tpu as pltpu
from jax.sharding import PartitionSpec as P

ITERS = 3
eps = 1e-06
teacher_temp = 0.04
student_temp = 0.1
LOG2E = 1.4426950408889634
F32 = jnp.float32
BF = jnp.bfloat16
MESH = pl.DeviceIdType.MESH
CH = 128
NZ = 4


def nt(left, right):
    return lax.dot_general(
        left, right, (((1,), (1,)), ((), ())), preferred_element_type=F32
    )


def nn(left, right):
    return jnp.dot(left, right, preferred_element_type=F32)


def tn(left, right):
    return lax.dot_general(
        left, right, (((0,), (0,)), ((), ())), preferred_element_type=F32
    )


def loop(count, body):
    def step(i, carry):
        body(i)
        return carry

    lax.fori_loop(0, count, step, 0)


def rows(start, size):
    return pl.ds(pl.multiple_of(start, size), size)


def unit_rows(values):
    values = values.astype(F32)
    scale = lax.rsqrt(jnp.sum(values * values, axis=1, keepdims=True) + eps)
    return values * scale, scale


def back_norm(grad, unit, scale):
    return scale * (grad - unit * jnp.sum(grad * unit, axis=1, keepdims=True))


def kernel(
    nb, nq,
    sf_hbm, tf_hbm, sp_hbm, tp_hbm,
    gp_out, gs_out,
    sf, tf, t_all, s_all, sp, anchor, pu, e, s, cs, tot, fa, fb, ra, rb, oa, ob, put, anct, ccol,
    r16, c16, w_src, w_mid, w_g1, w_g2, w_row, delta, cx, b1y, b1z, c2y, c2z, b2y, b2z, sumf, xs, xr,
    lsem, near_s, near_r, nfwd_s, nfwd_r, tok_s, tok_r, fwd_s, fwd_r, spr_s, spr_r,
    a1_s, a1_r, a2_s, a2_r, out_s, g_r, f_r, sib_r,
    ra_s, ra_r, rb_s, rb_r, y1_s, y1_r, z1_s, z1_r, y2_s, y2_r, z2_s, z2_r, xr_s, xr_r, gs_s, gs_r,
):
    nx = nb // 2
    far_dx = nx // 2
    hx = nx // 2
    nz = NZ
    ny = nq // nz
    tl, depth = sf.shape
    tokens = tl * nb
    pl_rows = sp.shape[0]
    protos = pl_rows * nb * nq
    chunks = pl_rows // CH
    wide = tokens // 128
    piece = tl // nq
    plane = 2 * tl
    b, p = lax.axis_index("batch"), lax.axis_index("proto")
    x, c = b // 2, lax.rem(b, 2)
    y, z = p // nz, lax.rem(p, nz)

    def bat(dx, dc):
        return lax.rem(x + dx, nx) * 2 + lax.rem(c + dc, 2)

    def peer(j):
        return (b, lax.rem(p + j, nq))

    def remote(src, dst, ss, rs, to):
        return pltpu.make_async_remote_copy(
            src, dst, ss, rs, device_id=to, device_id_type=MESH
        )

    sibling = (bat(0, 1), p)

    barrier = pltpu.get_barrier_semaphore()
    for j in range(1, nb):
        pl.semaphore_signal(
            barrier, inc=1, device_id=(lax.rem(b + j, nb), p), device_id_type=MESH
        )
    for j in range(1, nq):
        pl.semaphore_signal(barrier, inc=1, device_id=peer(j), device_id_type=MESH)
    mine = rows(b * pl_rows, pl_rows)
    loads = [
        pltpu.make_async_copy(tf_hbm, tf, lsem.at[0]),
        pltpu.make_async_copy(sf_hbm, sf, lsem.at[1]),
        pltpu.make_async_copy(tp_hbm.at[mine], anchor, lsem.at[2]),
        pltpu.make_async_copy(sp_hbm.at[mine], sp, lsem.at[3]),
    ]
    for d in loads:
        d.start()

    def norm_into(src, dst, start, count):
        def body(i):
            unit, _ = unit_rows(src[rows(i * 128, 128), :])
            dst[rows(start + i * 128, 128), :] = unit.astype(BF)

        loop(count // 128, body)

    loads[0].wait()
    norm_into(tf, t_all, b * tl, tl)
    pl.semaphore_wait(barrier, nb + nq - 2)

    feats = (t_all, s_all)

    def near_copy(f, dx, h):
        part = feats[f].at[rows(b * tl + h * (tl // 2), tl // 2)]
        return remote(
            part, part, near_s.at[f, dx, h], near_r.at[f, dx, h], (bat(dx, 0), p)
        )

    def near_forward(f, dx, h):
        part = feats[f].at[rows(bat(nx - dx, 0) * tl + h * (tl // 2), tl // 2)]
        return remote(
            part, part, nfwd_s.at[f, dx, h], nfwd_r.at[f, dx, h], sibling
        )

    def token_copy(f, dx):
        start, size = b * tl, tl
        if dx == far_dx:
            start, size = b * tl + p * piece, piece
        part = feats[f].at[rows(start, size)]
        to = sibling if dx == 0 else (bat(dx, 0), p)
        return remote(part, part, tok_s.at[f, dx], tok_r.at[f, dx], to)

    def spread(f, j):
        part = feats[f].at[rows(bat(nx - far_dx, 0) * tl + p * piece, piece)]
        return remote(part, part, spr_s.at[f], spr_r.at[f], peer(j))

    def spread_all(f):
        part = feats[f].at[0 : tl - piece]
        return remote(part, part, spr_s.at[f], spr_r.at[f], sibling)

    def forward(f, dx):
        block = feats[f].at[rows(bat(nx - dx, 0) * tl, tl)]
        return remote(block, block, fwd_s.at[f, dx], fwd_r.at[f, dx], sibling)

    near = (1, nx - 1)

    def tokens_send(f):
        token_copy(f, far_dx).start()
        token_copy(f, 0).start()
        for h in range(2):
            for dx in near:
                near_copy(f, dx, h).start()

    def spread_start(f):
        token_copy(f, far_dx).wait_recv()
        for j in range(1, nq):
            spread(f, j).start()

    def spread_end(f):
        spread_all(f).wait_recv()
        forward(f, far_dx).start()

    def near_part(f, h):
        for dx in near:
            near_copy(f, dx, h).wait_recv()
            near_forward(f, dx, h).start()

    def tokens_drain(f):
        token_copy(f, far_dx).wait_send()
        token_copy(f, 0).wait_send()
        forward(f, far_dx).wait_send()
        for h in range(2):
            for dx in near:
                if f:
                    near_copy(f, dx, h).wait_send()
                near_forward(f, dx, h).wait_send()
        spread_all(f).wait_send()

    tokens_send(0)
    loads[2].wait()
    norm_into(anchor, anchor, 0, pl_rows)

    def exp_block(left, right, out, block, width, factor, accumulate, first):
        cols = pl.ds(pl.multiple_of(block * tl, width), width)

        def body(i):
            sl = rows(i * 256, 256)
            value = jnp.exp2(nt(left[sl, :], right[cols, :]) * factor)
            out[sl, cols] = value.astype(BF)
            accumulate(value, sl, cols, width, first)

        loop(pl_rows // 256, body)

    def col_acc(value, sl, cols, width, first):
        acc = value[:, 0:128]
        for q in range(1, width // 128):
            acc = acc + value[:, q * 128 : (q + 1) * 128]
        if first:
            cs[sl, :] = acc
        else:
            cs[sl, :] += acc

    def row_acc(value, sl, cols, width, first):
        tot[:, cols] += jnp.sum(value.reshape(32, 8, width), axis=0)

    def chip_block(dx):
        return lax.rem(x + nx - dx, nx) * 2

    def teacher_block(block, width, first=False):
        exp_block(anchor, t_all, e, block, width, LOG2E / teacher_temp, col_acc, first)

    def student_plane(dx):
        if dx == far_dx:
            forward(1, dx).wait_recv()
        elif dx:
            for h in range(2):
                near_forward(1, dx, h).wait_recv()
        else:
            token_copy(1, 0).wait_recv()
        exp_block(
            pu, s_all, s, chip_block(dx), plane, LOG2E / student_temp, row_acc, False
        )

    loads[1].wait()
    norm_into(sf, s_all, b * tl, tl)
    token_copy(0, 0).wait_recv()
    teacher_block(chip_block(0), plane, True)
    spread_start(0)
    loads[3].wait()

    def norm_protos(i):
        sl = rows(i * 128, 128)
        unit, _ = unit_rows(sp[sl, :])
        pu[sl, :] = unit.astype(BF)
        put[:, sl] = unit.T.astype(BF)

    loop(pl_rows // 128, norm_protos)
    tot[...] = jnp.zeros_like(tot)
    for h in range(2):
        for dx in near:
            near_copy(0, dx, h).wait_send()
    tokens_send(1)
    spread_end(0)
    near_part(0, 0)
    forward(0, far_dx).wait_recv()
    teacher_block(chip_block(far_dx), plane)
    near_part(0, 1)
    for dx in near:
        teacher_block(chip_block(dx) + c, tl)
    spread_start(1)
    for dx in near:
        for h in range(2):
            near_forward(0, dx, h).wait_recv()
        teacher_block(chip_block(dx) + 1 - c, tl)
    half = lax.broadcasted_iota(jnp.int32, (16, 128), 0) < 8

    def split_into(dst, j, row):
        high = row.astype(BF).astype(F32)
        dst[:, j * 128 : (j + 1) * 128] = jnp.where(half, high, row - high).astype(BF)

    def first_step(n, j=1):
        return remote(w_src.at[n], w_g1.at[n, j - 1], a1_s.at[n], a1_r.at[n],
                      (lax.rem(b + j, nb), p))

    def second_step(n, j=1):
        return remote(w_mid.at[n], w_g2.at[n, j - 1], a2_s.at[n], a2_r.at[n], peer(j))

    def first_all(n):
        return remote(w_g1.at[n], w_g1.at[n], a1_s.at[n], a1_r.at[n], sibling)

    def second_all(n):
        return remote(w_g2.at[n], w_g2.at[n], a2_s.at[n], a2_r.at[n], sibling)

    def reduce_start(n):
        for j in range(1, nb):
            first_step(n, j).start()

    def reduce_middle(n):
        first_all(n).wait_recv()
        value = w_src[n]
        for j in range(nb - 1):
            value = value + w_g1[n, j]
        w_mid[n] = value.astype(BF)
        for j in range(1, nq):
            second_step(n, j).start()

    def reduce_end(n):
        second_all(n).wait_recv()
        value = w_mid[n].astype(F32)
        for j in range(nq - 1):
            value = value + w_g2[n, j].astype(F32)
        return value

    def spread_rows(k, weights):
        for j in range(wide):
            w_row[k, :, j * 128 : (j + 1) * 128] = jnp.broadcast_to(
                weights[j : j + 1, :], (8, 128)
            )

    def row_pass(n):
        out = nn(c16[...], e[...])
        line = out[0:1, :] + out[8:9, :]
        for j in range(wide):
            w_src[n, j : j + 1, :] = line[:, j * 128 : (j + 1) * 128]

    def col_pass(weights):
        for j in range(wide):
            split_into(r16, j, weights[j : j + 1, :])
        out = nt(r16[...], e[...])
        line = 1.0 / (protos * (out[0:1, :] + out[8:9, :]))
        return [line[:, j * 128 : (j + 1) * 128] for j in range(pl_rows // 128)]

    def feat_copy(buf, to, ss, rs, xx):
        return remote(buf.at[xx], to.at[xx], ss.at[xx], rs.at[xx], sibling)

    def feat_out(left, right, buf, to, ss, rs):
        def body(xx):
            cols = rows((xx * 2 + 1 - c) * tl, tl)
            buf[xx] = nn(left[...], right[:, cols]).astype(BF)
            feat_copy(buf, to, ss, rs, xx).start()

        loop(nx, body)

    def feat_own(left, right, out):
        def body(xx):
            cols = rows((xx * 2 + c) * tl, tl)
            out[xx] = nn(left[...], right[:, cols])

        loop(nx, body)

    for j in range(pl_rows // 128):
        sums = jnp.sum(cs[j * 128 : (j + 1) * 128, :].T, axis=0, keepdims=True)
        split_into(c16, j, 1.0 / (protos * sums))
    row_pass(0)
    reduce_start(0)
    student_plane(0)
    spread_end(1)
    reduce_middle(0)
    student_plane(far_dx)
    near_part(1, 0)
    near_part(1, 1)
    student_plane(near[0])
    student_plane(near[1])
    tokens_drain(0)
    weights = 1.0 / (tokens * reduce_end(0))
    for j, line in enumerate(col_pass(weights)):
        split_into(c16, j, line)
    row_pass(1)
    reduce_start(1)
    feat_out(put, s, oa, ra, ra_s, ra_r)
    reduce_middle(1)
    line = jnp.sum(tot[...], axis=0, keepdims=True)
    for j in range(wide):
        w_src[ITERS, j : j + 1, :] = line[:, j * 128 : (j + 1) * 128]
    reduce_start(ITERS)
    feat_own(put, s, fa)
    weights = 1.0 / (tokens * reduce_end(1))
    lines = col_pass(weights)
    for j, line in enumerate(lines):
        split_into(c16, j, line)
    row_pass(2)
    reduce_start(2)
    reduce_middle(ITERS)
    for j, line in enumerate(lines):
        sl = slice(j * 128, (j + 1) * 128)
        anct[:, sl] = (put[:, sl].astype(F32) * line).astype(BF)
    feat_out(anct, e, ob, rb, rb_s, rb_r)
    reduce_middle(2)
    feat_own(anct, e, fb)
    spread_rows(1, 1.0 / (student_temp * tokens * reduce_end(ITERS)))
    for j, line in enumerate(lines):
        ccol[j * 128 : (j + 1) * 128, :] = jnp.broadcast_to(line, (128, 128)).T


    tokens_drain(1)
    for xx in range(nx):
        feat_copy(oa, ra, ra_s, ra_r, xx).wait()
        feat_copy(ob, rb, rb_s, rb_r, xx).wait()
    spread_rows(0, (1.0 / student_temp) / (tokens * reduce_end(2)))

    group = tl // 128

    def combine(i):
        xx, g = i // group, lax.rem(i, group)
        sl = rows(g * 128, 128)
        at = rows(((xx * 2 + c) * group + g) * 128, 128)
        value = (fa[xx, :, sl] + ra[xx, :, sl].astype(F32)) * w_row[1, 0:1, at]
        value = value - (fb[xx, :, sl] + rb[xx, :, sl].astype(F32)) * w_row[0, 0:1, at]
        cx[xx, g] = value.T.astype(BF).reshape(nz, piece, depth)

    loop(nx * group, combine)
    def feat_send(src, dst, ss, rs, to):
        remote(src, dst, ss, rs, to).start()

    def whole(buf, ss, rs):
        return remote(buf, buf, ss.at[0], rs.at[0], sibling)

    first = [whole(b1y, y1_s, y1_r), whole(b1z, z1_s, z1_r)]
    second = [whole(b2y, z2_s, z2_r), whole(b2z, y2_s, y2_r)]
    third = whole(xr, xr_s, xr_r)
    final = remote(
        gs_out.at[0 : tl - piece], gs_out.at[0 : tl - piece],
        gs_s.at[0], gs_r.at[0], sibling,
    )

    def along_y(d):
        return lax.rem(y + d, ny)

    def along_z(d):
        return lax.rem(z + d, nz)

    for d in range(1, ny):
        feat_send(cx.at[0:hx, along_y(d)], b1y.at[d - 1], y1_s.at[0],
                  y1_r.at[0], (b, along_y(d) * nz + z))
    for d in range(1, nz):
        feat_send(cx.at[hx:nx, :, along_z(d)], b1z.at[d - 1], z1_s.at[0],
                  z1_r.at[0], (b, y * nz + along_z(d)))

    def feat_middle():
        for d in first:
            d.wait_recv()
        for h in range(hx):
            value = cx[h, y].astype(F32)
            for d in range(ny - 1):
                value = value + b1y[d, h].astype(F32)
            c2y[h] = value.astype(BF)
            value = cx[hx + h, :, z].astype(F32)
            for d in range(nz - 1):
                value = value + b1z[d, h].astype(F32)
            c2z[h] = value.astype(BF)
        for d in range(1, nz):
            feat_send(c2y.at[:, along_z(d)], b2y.at[d - 1], z2_s.at[0],
                      z2_r.at[0], (b, y * nz + along_z(d)))
        for d in range(1, ny):
            feat_send(c2z.at[:, along_y(d)], b2z.at[d - 1], y2_s.at[0],
                      y2_r.at[0], (b, along_y(d) * nz + z))

    def feat_x():
        for d in second:
            d.wait_recv()
        value = c2y[:, z].astype(F32)
        for d in range(nz - 1):
            value = value + b2y[d].astype(F32)
        sumf[0:hx] = value
        xs[0:hx] = value.astype(BF)
        value = c2z[:, y].astype(F32)
        for d in range(ny - 1):
            value = value + b2z[d].astype(F32)
        sumf[hx:nx] = value
        xs[hx:nx] = value.astype(BF)
        for dx in range(1, nx):
            feat_send(xs.at[lax.rem(x + dx, nx)], xr.at[dx - 1],
                      xr_s.at[0], xr_r.at[0], (bat(dx, 0), p))

    def feat_last():
        third.wait_recv()
        value = sumf[x]
        for dx in range(nx - 1):
            value = value + xr[dx].astype(F32)
        own = rows(p * piece, piece)
        unit, scale = unit_rows(sf[own, :])
        gs_out[own, :] = back_norm(value, unit, scale).astype(BF)
        part = gs_out.at[own]
        for j in range(1, nq):
            feat_send(part, part, gs_s.at[0], gs_r.at[0], peer(j))

    span = 2 * CH
    groups = pl_rows // span

    def chunk_send(q, k):
        to = (bat(1, 0), p) if k == 0 else (bat(nx - 1, 0), p)
        part = gp_out.at[rows(b * pl_rows + q * CH, CH)]
        return remote(part, part, out_s.at[0], g_r.at[k, q], to)

    def group_forward(g, k):
        block = bat(nx - 1, 0) if k == 0 else bat(1, 0)
        to = (bat(1, 0), p) if k == 0 else (bat(nx - 1, 0), p)
        part = gp_out.at[rows(block * pl_rows + g * span + k * CH, CH)]
        return remote(part, part, out_s.at[0], f_r.at[k, g], to)

    def group_sibling(g, k):
        block = bat((nx - 1, 1, 2)[k], 0)
        part = gp_out.at[rows(block * pl_rows + g * span, span)]
        return remote(part, part, out_s.at[0], sib_r.at[0], sibling)

    def own_sibling():
        part = gp_out.at[rows(b * pl_rows, pl_rows)]
        return remote(part, part, out_s.at[0], sib_r.at[0], sibling)

    def chunk_compute(q):
        sl = rows(q * CH, CH)
        weight = ccol[sl, 0:1]
        for j in range(tokens // 512):
            js = slice(j * 512, (j + 1) * 512)
            value = s[sl, js].astype(F32) * w_row[1, 0:1, js]
            value = value - e[sl, js].astype(F32) * (w_row[0, 0:1, js] * weight)
            delta[:, js] = value.astype(BF)
        back = nn(delta[...], s_all[...])
        unit, scale = unit_rows(sp[sl, :])
        value = back_norm(back, unit, scale).astype(BF)
        gp_out[rows(b * pl_rows + q * CH, CH), :] = value
        chunk_send(q, 0).start()
        chunk_send(q, 1).start()

    def group_recv(g):
        for k in range(2):
            chunk_send(2 * g, k).wait_recv()
            chunk_send(2 * g + 1, k).wait_recv()
            group_forward(g, k).start()
            group_sibling(g, k).start()

    def group_last(g):
        for k in range(2):
            group_forward(g, k).wait_recv()
        group_sibling(g, 2).start()

    loop(chunks, chunk_compute)
    own_sibling().start()
    feat_middle()
    feat_x()
    loop(groups - 1, group_recv)
    feat_last()
    group_recv(groups - 1)
    loop(groups, group_last)

    for n in range(ITERS + 1):
        first_all(n).wait_send()
        second_all(n).wait_send()
    for d in first + second + [third, final]:
        d.wait_send()
    sent = gp_out.at[0 : pl_rows * (nx + 3)]
    remote(sent, sent, out_s.at[0], sib_r.at[0], sibling).wait_send()
    held = gp_out.at[0 : pl_rows * nx]
    remote(held, held, out_s.at[0], sib_r.at[0], sibling).wait_recv()
    final.wait_recv()


def on_device(nb, nq, student_feats, teacher_feats, student_protos, teacher_protos):
    tl, depth = student_feats.shape
    pl_rows = student_protos.shape[0] // nb
    tokens = tl * nb
    chunks = pl_rows // CH
    wide = tokens // 128
    nx = nb // 2
    piece = tl // nq
    vm = pltpu.VMEM
    dma = pltpu.SemaphoreType.DMA
    hx, nz = nx // 2, NZ
    ny = nq // nz
    scratch = [
        vm((tl, depth), BF),
        vm((tl, depth), BF),
        vm((tokens, depth), BF),
        vm((tokens, depth), BF),
        vm((pl_rows, depth), BF),
        vm((pl_rows, depth), BF),
        vm((pl_rows, depth), BF),
        vm((pl_rows, tokens), BF),
        vm((pl_rows, tokens), BF),
        vm((pl_rows, 128), F32),
        vm((8, tokens), F32),
        vm((nx, depth, tl), F32),
        vm((nx, depth, tl), F32),
        vm((nx, depth, tl), BF),
        vm((nx, depth, tl), BF),
        vm((nx, depth, tl), BF),
        vm((nx, depth, tl), BF),
        vm((depth, pl_rows), BF),
        vm((depth, pl_rows), BF),
        vm((pl_rows, 128), F32),
        vm((16, tokens), BF),
        vm((16, pl_rows), BF),
        vm((ITERS + 1, wide, 128), F32),
        vm((ITERS + 1, wide, 128), BF),
        vm((ITERS + 1, nb - 1, wide, 128), F32),
        vm((ITERS + 1, nq - 1, wide, 128), BF),
        vm((2, 8, tokens), F32),
        vm((CH, tokens), BF),
        vm((nx, ny, nz, piece, depth), BF),
        vm((ny - 1, hx, nz, piece, depth), BF),
        vm((nz - 1, hx, ny, piece, depth), BF),
        vm((hx, nz, piece, depth), BF),
        vm((hx, ny, piece, depth), BF),
        vm((nz - 1, hx, piece, depth), BF),
        vm((ny - 1, hx, piece, depth), BF),
        vm((nx, piece, depth), F32),
        vm((nx, piece, depth), BF),
        vm((nx - 1, piece, depth), BF),
        dma((4,)),
        dma((2, nx, 2)), dma((2, nx, 2)), dma((2, nx, 2)), dma((2, nx, 2)),
        dma((2, nx)), dma((2, nx)), dma((2, nx)), dma((2, nx)),
        dma((2,)), dma((2,)),
        dma((ITERS + 1,)), dma((ITERS + 1,)),
        dma((ITERS + 1,)), dma((ITERS + 1,)),
        dma((1,)), dma((2, chunks)), dma((2, chunks // 2)), dma((1,)),
        dma((nx,)), dma((nx,)), dma((nx,)), dma((nx,)),
        dma((1,)), dma((1,)), dma((1,)), dma((1,)), dma((1,)), dma((1,)),
        dma((1,)), dma((1,)), dma((1,)), dma((1,)), dma((1,)), dma((1,)),
    ]
    in_vmem = pl.BlockSpec(memory_space=pltpu.VMEM)
    anywhere = pl.BlockSpec(memory_space=pl.ANY)
    return pl.pallas_call(
        functools.partial(kernel, nb, nq),
        out_shape=[
            pltpu.VMEM(student_protos.shape, BF),
            pltpu.VMEM(student_feats.shape, BF),
        ],
        in_specs=[anywhere] * 4,
        out_specs=[in_vmem, in_vmem],
        scratch_shapes=scratch,
        compiler_params=pltpu.CompilerParams(
            collective_id=0, has_side_effects=True, vmem_limit_bytes=54 << 20
        ),
        name="prototype_head",
    )(student_feats, teacher_feats, student_protos, teacher_protos)


def solution(mesh):
    nb, nq = mesh.shape["batch"], mesh.shape["proto"]
    in_specs = (P("batch", None), P("batch", None), P("proto", None), P("proto", None))
    out_specs = (P("proto", None), P("batch", None))
    return jax.shard_map(
        functools.partial(on_device, nb, nq),
        mesh=mesh, in_specs=in_specs, out_specs=out_specs, check_vma=False,
    )
```

```python
import functools

import jax
import jax.numpy as jnp
from jax import lax
from jax.experimental import pallas as pl
from jax.experimental.pallas import tpu as pltpu
from jax.sharding import PartitionSpec as P

ITERS = 3
eps = 1e-06
teacher_temp = 0.04
student_temp = 0.1
LOG2E = 1.4426950408889634
F32 = jnp.float32
BF = jnp.bfloat16
MESH = pl.DeviceIdType.MESH
CH = 128
NZ = 4


def nt(left, right):
    return lax.dot_general(
        left, right, (((1,), (1,)), ((), ())), preferred_element_type=F32
    )


def nn(left, right):
    return jnp.dot(left, right, preferred_element_type=F32)


def tn(left, right):
    return lax.dot_general(
        left, right, (((0,), (0,)), ((), ())), preferred_element_type=F32
    )


def loop(count, body):
    def step(i, carry):
        body(i)
        return carry

    lax.fori_loop(0, count, step, 0)


def rows(start, size):
    return pl.ds(pl.multiple_of(start, size), size)


def unit_rows(values):
    values = values.astype(F32)
    scale = lax.rsqrt(jnp.sum(values * values, axis=1, keepdims=True) + eps)
    return values * scale, scale


def back_norm(grad, unit, scale):
    return scale * (grad - unit * jnp.sum(grad * unit, axis=1, keepdims=True))


def kernel(
    nb, nq,
    sf_hbm, tf_hbm, sp_hbm, tp_hbm,
    gp_out, gs_out,
    sf, tf, t_all, s_all, sp, anchor, pu, e, s, cs, tot, fa, fb, ra, rb, oa, ob, put, anct, ccol,
    r16, c16, w_src, w_mid, w_g1, w_g2, w_row, delta, cx, b1y, b1z, c2y, c2z, b2y, b2z, sumf, xs, xr,
    lsem, near_s, near_r, nfwd_s, nfwd_r, tok_s, tok_r, fwd_s, fwd_r, spr_s, spr_r,
    a1_s, a1_r, a2_s, a2_r, out_s, g_r, f_r, sib_r,
    ra_s, ra_r, rb_s, rb_r, y1_s, y1_r, z1_s, z1_r, y2_s, y2_r, z2_s, z2_r, xr_s, xr_r, gs_s, gs_r,
):
    nx = nb // 2
    far_dx = nx // 2
    hx = nx // 2
    nz = NZ
    ny = nq // nz
    tl, depth = sf.shape
    tokens = tl * nb
    pl_rows = sp.shape[0]
    protos = pl_rows * nb * nq
    chunks = pl_rows // CH
    wide = tokens // 128
    piece = tl // nq
    plane = 2 * tl
    b, p = lax.axis_index("batch"), lax.axis_index("proto")
    x, c = b // 2, lax.rem(b, 2)
    y, z = p // nz, lax.rem(p, nz)

    def bat(dx, dc):
        return lax.rem(x + dx, nx) * 2 + lax.rem(c + dc, 2)

    def hops(d, n):
        return min(d, n - d)

    ys = [lax.rem(y + d, ny) for d in range(ny)]
    zs = [lax.rem(z + d, nz) for d in range(nz)]
    steps = [(dy, dz) for dy in range(ny) for dz in range(nz) if dy or dz]
    steps.sort(key=lambda d: -hops(d[0], ny) - hops(d[1], nz))
    proto_peers = [(dy * nz + dz - 1, (b, ys[dy] * nz + zs[dz])) for dy, dz in steps]
    steps = [(dx, dc) for dx in range(nx) for dc in range(2) if dx or dc]
    steps.sort(key=lambda d: -2 * hops(d[0], nx) - d[1])
    batch_peers = [(dx * 2 + dc - 1, (bat(dx, dc), p)) for dx, dc in steps]

    def remote(src, dst, ss, rs, to):
        return pltpu.make_async_remote_copy(
            src, dst, ss, rs, device_id=to, device_id_type=MESH
        )

    sibling = (bat(0, 1), p)

    barrier = pltpu.get_barrier_semaphore()
    for _, to in proto_peers + batch_peers:
        pl.semaphore_signal(barrier, inc=1, device_id=to, device_id_type=MESH)
    mine = rows(b * pl_rows, pl_rows)
    loads = [
        pltpu.make_async_copy(tf_hbm, tf, lsem.at[0]),
        pltpu.make_async_copy(sf_hbm, sf, lsem.at[1]),
        pltpu.make_async_copy(tp_hbm.at[mine], anchor, lsem.at[2]),
        pltpu.make_async_copy(sp_hbm.at[mine], sp, lsem.at[3]),
    ]
    for d in loads:
        d.start()

    def norm_into(src, dst, start, count):
        def body(i):
            unit, _ = unit_rows(src[rows(i * 128, 128), :])
            dst[rows(start + i * 128, 128), :] = unit.astype(BF)

        loop(count // 128, body)

    loads[0].wait()
    norm_into(tf, t_all, b * tl, tl)
    pl.semaphore_wait(barrier, nb + nq - 2)

    feats = (t_all, s_all)

    def near_copy(f, dx, h):
        part = feats[f].at[rows(b * tl + h * (tl // 2), tl // 2)]
        return remote(
            part, part, near_s.at[f, dx, h], near_r.at[f, dx, h], (bat(dx, 0), p)
        )

    def near_forward(f, dx, h):
        part = feats[f].at[rows(bat(nx - dx, 0) * tl + h * (tl // 2), tl // 2)]
        return remote(
            part, part, nfwd_s.at[f, dx, h], nfwd_r.at[f, dx, h], sibling
        )

    def token_copy(f, dx):
        start, size = b * tl, tl
        if dx == far_dx:
            start, size = b * tl + p * piece, piece
        part = feats[f].at[rows(start, size)]
        to = sibling if dx == 0 else (bat(dx, 0), p)
        return remote(part, part, tok_s.at[f, dx], tok_r.at[f, dx], to)

    def spread(f, to):
        part = feats[f].at[rows(bat(nx - far_dx, 0) * tl + p * piece, piece)]
        return remote(part, part, spr_s.at[f], spr_r.at[f], to)

    def spread_all(f):
        part = feats[f].at[0 : tl - piece]
        return remote(part, part, spr_s.at[f], spr_r.at[f], sibling)

    def forward(f, dx):
        block = feats[f].at[rows(bat(nx - dx, 0) * tl, tl)]
        return remote(block, block, fwd_s.at[f, dx], fwd_r.at[f, dx], sibling)

    near = (1, nx - 1)

    def tokens_send(f):
        token_copy(f, far_dx).start()
        token_copy(f, 0).start()
        for h in range(2):
            for dx in near:
                near_copy(f, dx, h).start()

    def spread_start(f):
        token_copy(f, far_dx).wait_recv()
        for _, to in proto_peers:
            spread(f, to).start()

    def spread_end(f):
        spread_all(f).wait_recv()
        forward(f, far_dx).start()

    def near_part(f, h):
        for dx in near:
            near_copy(f, dx, h).wait_recv()
            near_forward(f, dx, h).start()

    def tokens_drain(f):
        token_copy(f, far_dx).wait_send()
        token_copy(f, 0).wait_send()
        forward(f, far_dx).wait_send()
        for h in range(2):
            for dx in near:
                if f:
                    near_copy(f, dx, h).wait_send()
                near_forward(f, dx, h).wait_send()
        spread_all(f).wait_send()

    tokens_send(0)
    loads[2].wait()
    norm_into(anchor, anchor, 0, pl_rows)

    def exp_block(left, right, out, block, width, factor, accumulate, first):
        cols = pl.ds(pl.multiple_of(block * tl, width), width)

        def body(i):
            sl = rows(i * 256, 256)
            value = jnp.exp2(nt(left[sl, :], right[cols, :]) * factor)
            out[sl, cols] = value.astype(BF)
            accumulate(value, sl, cols, width, first)

        loop(pl_rows // 256, body)

    def col_acc(value, sl, cols, width, first):
        acc = value[:, 0:128]
        for q in range(1, width // 128):
            acc = acc + value[:, q * 128 : (q + 1) * 128]
        if first:
            cs[sl, :] = acc
        else:
            cs[sl, :] += acc

    def row_acc(value, sl, cols, width, first):
        tot[:, cols] += jnp.sum(value.reshape(32, 8, width), axis=0)

    def chip_block(dx):
        return lax.rem(x + nx - dx, nx) * 2

    def teacher_block(block, width, first=False):
        exp_block(anchor, t_all, e, block, width, LOG2E / teacher_temp, col_acc, first)

    def student_plane(dx):
        if dx == far_dx:
            forward(1, dx).wait_recv()
        elif dx:
            for h in range(2):
                near_forward(1, dx, h).wait_recv()
        else:
            token_copy(1, 0).wait_recv()
        exp_block(
            pu, s_all, s, chip_block(dx), plane, LOG2E / student_temp, row_acc, False
        )

    loads[1].wait()
    norm_into(sf, s_all, b * tl, tl)
    token_copy(0, 0).wait_recv()
    teacher_block(chip_block(0), plane, True)
    spread_start(0)
    loads[3].wait()

    def norm_protos(i):
        sl = rows(i * 128, 128)
        unit, _ = unit_rows(sp[sl, :])
        pu[sl, :] = unit.astype(BF)
        put[:, sl] = unit.T.astype(BF)

    loop(pl_rows // 128, norm_protos)
    tot[...] = jnp.zeros_like(tot)
    for h in range(2):
        for dx in near:
            near_copy(0, dx, h).wait_send()
    tokens_send(1)
    spread_end(0)
    near_part(0, 0)
    forward(0, far_dx).wait_recv()
    teacher_block(chip_block(far_dx), plane)
    near_part(0, 1)
    for dx in near:
        teacher_block(chip_block(dx) + c, tl)
    for dx in near:
        for h in range(2):
            near_forward(0, dx, h).wait_recv()
        teacher_block(chip_block(dx) + 1 - c, tl)
    half = lax.broadcasted_iota(jnp.int32, (16, 128), 0) < 8

    def split_into(dst, j, row):
        high = row.astype(BF).astype(F32)
        dst[:, j * 128 : (j + 1) * 128] = jnp.where(half, high, row - high).astype(BF)

    def first_step(n, slot, to):
        return remote(w_src.at[n], w_g1.at[n, slot], a1_s.at[n], a1_r.at[n], to)

    def second_step(n, slot, to):
        return remote(w_mid.at[n], w_g2.at[n, slot], a2_s.at[n], a2_r.at[n], to)

    def first_all(n):
        return remote(w_g1.at[n], w_g1.at[n], a1_s.at[n], a1_r.at[n], sibling)

    def second_all(n):
        return remote(w_g2.at[n], w_g2.at[n], a2_s.at[n], a2_r.at[n], sibling)

    def reduce_start(n):
        for slot, to in batch_peers:
            first_step(n, slot, to).start()

    def reduce_middle(n):
        first_all(n).wait_recv()
        value = w_src[n]
        for j in range(nb - 1):
            value = value + w_g1[n, j]
        w_mid[n] = value.astype(BF)
        for slot, to in proto_peers:
            second_step(n, slot, to).start()

    def reduce_end(n):
        second_all(n).wait_recv()
        value = w_mid[n].astype(F32)
        for j in range(nq - 1):
            value = value + w_g2[n, j].astype(F32)
        return value

    def spread_rows(k, weights):
        for j in range(wide):
            w_row[k, :, j * 128 : (j + 1) * 128] = jnp.broadcast_to(
                weights[j : j + 1, :], (8, 128)
            )

    def row_pass(n):
        out = nn(c16[...], e[...])
        line = out[0:1, :] + out[8:9, :]
        for j in range(wide):
            w_src[n, j : j + 1, :] = line[:, j * 128 : (j + 1) * 128]

    def col_pass(weights):
        for j in range(wide):
            split_into(r16, j, weights[j : j + 1, :])
        out = nt(r16[...], e[...])
        line = 1.0 / (protos * (out[0:1, :] + out[8:9, :]))
        return [line[:, j * 128 : (j + 1) * 128] for j in range(pl_rows // 128)]

    def feat_copy(buf, to, ss, rs, xx):
        return remote(buf.at[xx], to.at[xx], ss.at[xx], rs.at[xx], sibling)

    def feat_out(left, right, buf, to, ss, rs):
        def body(xx):
            cols = rows((xx * 2 + 1 - c) * tl, tl)
            buf[xx] = nn(left[...], right[:, cols]).astype(BF)
            feat_copy(buf, to, ss, rs, xx).start()

        loop(nx, body)

    def feat_own(left, right, out):
        def body(xx):
            cols = rows((xx * 2 + c) * tl, tl)
            out[xx] = nn(left[...], right[:, cols])

        loop(nx, body)

    for j in range(pl_rows // 128):
        sums = jnp.sum(cs[j * 128 : (j + 1) * 128, :].T, axis=0, keepdims=True)
        split_into(c16, j, 1.0 / (protos * sums))
    row_pass(0)
    reduce_start(0)
    spread_start(1)
    student_plane(0)
    reduce_middle(0)
    near_part(1, 0)
    near_part(1, 1)
    spread_end(1)
    student_plane(near[0])
    student_plane(near[1])
    student_plane(far_dx)
    tokens_drain(0)
    weights = 1.0 / (tokens * reduce_end(0))
    for j, line in enumerate(col_pass(weights)):
        split_into(c16, j, line)
    row_pass(1)
    reduce_start(1)
    feat_out(put, s, oa, ra, ra_s, ra_r)
    reduce_middle(1)
    line = jnp.sum(tot[...], axis=0, keepdims=True)
    for j in range(wide):
        w_src[ITERS, j : j + 1, :] = line[:, j * 128 : (j + 1) * 128]
    reduce_start(ITERS)
    feat_own(put, s, fa)
    weights = 1.0 / (tokens * reduce_end(1))
    lines = col_pass(weights)
    for j, line in enumerate(lines):
        split_into(c16, j, line)
    row_pass(2)
    reduce_start(2)
    reduce_middle(ITERS)
    for j, line in enumerate(lines):
        sl = slice(j * 128, (j + 1) * 128)
        anct[:, sl] = (put[:, sl].astype(F32) * line).astype(BF)
    feat_out(anct, e, ob, rb, rb_s, rb_r)
    reduce_middle(2)
    feat_own(anct, e, fb)
    spread_rows(1, 1.0 / (student_temp * tokens * reduce_end(ITERS)))
    for j, line in enumerate(lines):
        ccol[j * 128 : (j + 1) * 128, :] = jnp.broadcast_to(line, (128, 128)).T


    tokens_drain(1)
    for xx in range(nx):
        feat_copy(oa, ra, ra_s, ra_r, xx).wait()
        feat_copy(ob, rb, rb_s, rb_r, xx).wait()
    spread_rows(0, (1.0 / student_temp) / (tokens * reduce_end(2)))

    group = tl // 128

    def combine(i):
        xx, g = i // group, lax.rem(i, group)
        sl = rows(g * 128, 128)
        at = rows(((xx * 2 + c) * group + g) * 128, 128)
        value = (fa[xx, :, sl] + ra[xx, :, sl].astype(F32)) * w_row[1, 0:1, at]
        value = value - (fb[xx, :, sl] + rb[xx, :, sl].astype(F32)) * w_row[0, 0:1, at]
        cx[xx, g] = value.T.astype(BF).reshape(nz, piece, depth)

    loop(nx * group, combine)
    def feat_send(src, dst, ss, rs, to):
        remote(src, dst, ss, rs, to).start()

    def whole(buf, ss, rs):
        return remote(buf, buf, ss.at[0], rs.at[0], sibling)

    first = [whole(b1y, y1_s, y1_r), whole(b1z, z1_s, z1_r)]
    second = [whole(b2y, z2_s, z2_r), whole(b2z, y2_s, y2_r)]
    third = whole(xr, xr_s, xr_r)
    final = remote(
        gs_out.at[0 : tl - piece], gs_out.at[0 : tl - piece],
        gs_s.at[0], gs_r.at[0], sibling,
    )

    def along_y(d):
        return lax.rem(y + d, ny)

    def along_z(d):
        return lax.rem(z + d, nz)

    for d in range(1, ny):
        feat_send(cx.at[0:hx, along_y(d)], b1y.at[d - 1], y1_s.at[0],
                  y1_r.at[0], (b, along_y(d) * nz + z))
    for d in range(1, nz):
        feat_send(cx.at[hx:nx, :, along_z(d)], b1z.at[d - 1], z1_s.at[0],
                  z1_r.at[0], (b, y * nz + along_z(d)))

    def feat_middle():
        for d in first:
            d.wait_recv()
        for h in range(hx):
            value = cx[h, y].astype(F32)
            for d in range(ny - 1):
                value = value + b1y[d, h].astype(F32)
            c2y[h] = value.astype(BF)
            value = cx[hx + h, :, z].astype(F32)
            for d in range(nz - 1):
                value = value + b1z[d, h].astype(F32)
            c2z[h] = value.astype(BF)
        for d in range(1, nz):
            feat_send(c2y.at[:, along_z(d)], b2y.at[d - 1], z2_s.at[0],
                      z2_r.at[0], (b, y * nz + along_z(d)))
        for d in range(1, ny):
            feat_send(c2z.at[:, along_y(d)], b2z.at[d - 1], y2_s.at[0],
                      y2_r.at[0], (b, along_y(d) * nz + z))

    def feat_x():
        for d in second:
            d.wait_recv()
        value = c2y[:, z].astype(F32)
        for d in range(nz - 1):
            value = value + b2y[d].astype(F32)
        sumf[0:hx] = value
        xs[0:hx] = value.astype(BF)
        value = c2z[:, y].astype(F32)
        for d in range(ny - 1):
            value = value + b2z[d].astype(F32)
        sumf[hx:nx] = value
        xs[hx:nx] = value.astype(BF)
        for dx in range(1, nx):
            feat_send(xs.at[lax.rem(x + dx, nx)], xr.at[dx - 1],
                      xr_s.at[0], xr_r.at[0], (bat(dx, 0), p))

    def feat_last():
        third.wait_recv()
        value = sumf[x]
        for dx in range(nx - 1):
            value = value + xr[dx].astype(F32)
        own = rows(p * piece, piece)
        unit, scale = unit_rows(sf[own, :])
        gs_out[own, :] = back_norm(value, unit, scale).astype(BF)
        part = gs_out.at[own]
        for _, to in proto_peers:
            feat_send(part, part, gs_s.at[0], gs_r.at[0], to)

    span = 2 * CH
    groups = pl_rows // span

    def chunk_send(q, k):
        to = (bat(1, 0), p) if k == 0 else (bat(nx - 1, 0), p)
        part = gp_out.at[rows(b * pl_rows + q * CH, CH)]
        return remote(part, part, out_s.at[0], g_r.at[k, q], to)

    def group_forward(g, k):
        block = bat(nx - 1, 0) if k == 0 else bat(1, 0)
        to = (bat(1, 0), p) if k == 0 else (bat(nx - 1, 0), p)
        part = gp_out.at[rows(block * pl_rows + g * span + k * CH, CH)]
        return remote(part, part, out_s.at[0], f_r.at[k, g], to)

    def group_sibling(g, k):
        block = bat((nx - 1, 1, 2)[k], 0)
        part = gp_out.at[rows(block * pl_rows + g * span, span)]
        return remote(part, part, out_s.at[0], sib_r.at[0], sibling)

    def own_sibling():
        part = gp_out.at[rows(b * pl_rows, pl_rows)]
        return remote(part, part, out_s.at[0], sib_r.at[0], sibling)

    def chunk_compute(q):
        sl = rows(q * CH, CH)
        weight = ccol[sl, 0:1]
        for j in range(tokens // 512):
            js = slice(j * 512, (j + 1) * 512)
            value = s[sl, js].astype(F32) * w_row[1, 0:1, js]
            value = value - e[sl, js].astype(F32) * (w_row[0, 0:1, js] * weight)
            delta[:, js] = value.astype(BF)
        back = nn(delta[...], s_all[...])
        unit, scale = unit_rows(sp[sl, :])
        value = back_norm(back, unit, scale).astype(BF)
        gp_out[rows(b * pl_rows + q * CH, CH), :] = value
        chunk_send(q, 0).start()
        chunk_send(q, 1).start()

    def group_recv(g):
        for k in range(2):
            chunk_send(2 * g, k).wait_recv()
            chunk_send(2 * g + 1, k).wait_recv()
            group_forward(g, k).start()
            group_sibling(g, k).start()

    def group_last(g):
        for k in range(2):
            group_forward(g, k).wait_recv()
        group_sibling(g, 2).start()

    loop(chunks, chunk_compute)
    own_sibling().start()
    feat_middle()
    feat_x()
    loop(groups - 1, group_recv)
    feat_last()
    group_recv(groups - 1)
    loop(groups, group_last)

    for n in range(ITERS + 1):
        first_all(n).wait_send()
        second_all(n).wait_send()
    for d in first + second + [third, final]:
        d.wait_send()
    sent = gp_out.at[0 : pl_rows * (nx + 3)]
    remote(sent, sent, out_s.at[0], sib_r.at[0], sibling).wait_send()
    held = gp_out.at[0 : pl_rows * nx]
    remote(held, held, out_s.at[0], sib_r.at[0], sibling).wait_recv()
    final.wait_recv()


def on_device(nb, nq, student_feats, teacher_feats, student_protos, teacher_protos):
    tl, depth = student_feats.shape
    pl_rows = student_protos.shape[0] // nb
    tokens = tl * nb
    chunks = pl_rows // CH
    wide = tokens // 128
    nx = nb // 2
    piece = tl // nq
    vm = pltpu.VMEM
    dma = pltpu.SemaphoreType.DMA
    hx, nz = nx // 2, NZ
    ny = nq // nz
    scratch = [
        vm((tl, depth), BF),
        vm((tl, depth), BF),
        vm((tokens, depth), BF),
        vm((tokens, depth), BF),
        vm((pl_rows, depth), BF),
        vm((pl_rows, depth), BF),
        vm((pl_rows, depth), BF),
        vm((pl_rows, tokens), BF),
        vm((pl_rows, tokens), BF),
        vm((pl_rows, 128), F32),
        vm((8, tokens), F32),
        vm((nx, depth, tl), F32),
        vm((nx, depth, tl), F32),
        vm((nx, depth, tl), BF),
        vm((nx, depth, tl), BF),
        vm((nx, depth, tl), BF),
        vm((nx, depth, tl), BF),
        vm((depth, pl_rows), BF),
        vm((depth, pl_rows), BF),
        vm((pl_rows, 128), F32),
        vm((16, tokens), BF),
        vm((16, pl_rows), BF),
        vm((ITERS + 1, wide, 128), F32),
        vm((ITERS + 1, wide, 128), BF),
        vm((ITERS + 1, nb - 1, wide, 128), F32),
        vm((ITERS + 1, nq - 1, wide, 128), BF),
        vm((2, 8, tokens), F32),
        vm((CH, tokens), BF),
        vm((nx, ny, nz, piece, depth), BF),
        vm((ny - 1, hx, nz, piece, depth), BF),
        vm((nz - 1, hx, ny, piece, depth), BF),
        vm((hx, nz, piece, depth), BF),
        vm((hx, ny, piece, depth), BF),
        vm((nz - 1, hx, piece, depth), BF),
        vm((ny - 1, hx, piece, depth), BF),
        vm((nx, piece, depth), F32),
        vm((nx, piece, depth), BF),
        vm((nx - 1, piece, depth), BF),
        dma((4,)),
        dma((2, nx, 2)), dma((2, nx, 2)), dma((2, nx, 2)), dma((2, nx, 2)),
        dma((2, nx)), dma((2, nx)), dma((2, nx)), dma((2, nx)),
        dma((2,)), dma((2,)),
        dma((ITERS + 1,)), dma((ITERS + 1,)),
        dma((ITERS + 1,)), dma((ITERS + 1,)),
        dma((1,)), dma((2, chunks)), dma((2, chunks // 2)), dma((1,)),
        dma((nx,)), dma((nx,)), dma((nx,)), dma((nx,)),
        dma((1,)), dma((1,)), dma((1,)), dma((1,)), dma((1,)), dma((1,)),
        dma((1,)), dma((1,)), dma((1,)), dma((1,)), dma((1,)), dma((1,)),
    ]
    in_vmem = pl.BlockSpec(memory_space=pltpu.VMEM)
    anywhere = pl.BlockSpec(memory_space=pl.ANY)
    return pl.pallas_call(
        functools.partial(kernel, nb, nq),
        out_shape=[
            pltpu.VMEM(student_protos.shape, BF),
            pltpu.VMEM(student_feats.shape, BF),
        ],
        in_specs=[anywhere] * 4,
        out_specs=[in_vmem, in_vmem],
        scratch_shapes=scratch,
        compiler_params=pltpu.CompilerParams(
            collective_id=0, has_side_effects=True, vmem_limit_bytes=54 << 20
        ),
        name="prototype_head",
    )(student_feats, teacher_feats, student_protos, teacher_protos)


def solution(mesh):
    nb, nq = mesh.shape["batch"], mesh.shape["proto"]
    in_specs = (P("batch", None), P("batch", None), P("proto", None), P("proto", None))
    out_specs = (P("proto", None), P("batch", None))
    return jax.shard_map(
        functools.partial(on_device, nb, nq),
        mesh=mesh, in_specs=in_specs, out_specs=out_specs, check_vma=False,
    )
```

```python
import functools

import jax
import jax.numpy as jnp
from jax import lax
from jax.experimental import pallas as pl
from jax.experimental.pallas import tpu as pltpu
from jax.sharding import PartitionSpec as P

ITERS = 3
eps = 1e-06
teacher_temp = 0.04
student_temp = 0.1
LOG2E = 1.4426950408889634
F32 = jnp.float32
BF = jnp.bfloat16
MESH = pl.DeviceIdType.MESH
CH = 128
NZ = 4


def nt(left, right):
    return lax.dot_general(
        left, right, (((1,), (1,)), ((), ())), preferred_element_type=F32
    )


def nn(left, right):
    return jnp.dot(left, right, preferred_element_type=F32)


def tn(left, right):
    return lax.dot_general(
        left, right, (((0,), (0,)), ((), ())), preferred_element_type=F32
    )


def loop(count, body):
    def step(i, carry):
        body(i)
        return carry

    lax.fori_loop(0, count, step, 0)


def rows(start, size):
    return pl.ds(pl.multiple_of(start, size), size)


def unit_rows(values):
    values = values.astype(F32)
    scale = lax.rsqrt(jnp.sum(values * values, axis=1, keepdims=True) + eps)
    return values * scale, scale


def back_norm(grad, unit, scale):
    return scale * (grad - unit * jnp.sum(grad * unit, axis=1, keepdims=True))


def kernel(
    nb, nq,
    sf_hbm, tf_hbm, sp_hbm, tp_hbm,
    gp_out, gs_out,
    sf, tf, t_all, s_all, sp, anchor, pu, e, s, cs, tot, fa, fb, ra, rb, oa, ob, put, anct, ccol,
    r16, c16, w_src, w_mid, w_g1, w_g2, w_row, delta, cx, b1y, b1z, c2y, c2z, b2y, b2z, sumf, xs, xr,
    lsem, near_s, near_r, nfwd_s, nfwd_r, tok_s, tok_r, fwd_s, fwd_r, spr_s, spr_r,
    a1_s, a1_r, a2_s, a2_r, out_s, g_r, f_r, sib_r,
    ra_s, ra_r, rb_s, rb_r, y1_s, y1_r, z1_s, z1_r, y2_s, y2_r, z2_s, z2_r, xr_s, xr_r, gs_s, gs_r,
):
    nx = nb // 2
    far_dx = nx // 2
    hx = nx // 2
    nz = NZ
    ny = nq // nz
    tl, depth = sf.shape
    tokens = tl * nb
    pl_rows = sp.shape[0]
    protos = pl_rows * nb * nq
    chunks = pl_rows // CH
    wide = tokens // 128
    piece = tl // nq
    plane = 2 * tl
    b, p = lax.axis_index("batch"), lax.axis_index("proto")
    x, c = b // 2, lax.rem(b, 2)
    y, z = p // nz, lax.rem(p, nz)

    def bat(dx, dc):
        return lax.rem(x + dx, nx) * 2 + lax.rem(c + dc, 2)

    def hops(d, n):
        return min(d, n - d)

    ys = [lax.rem(y + d, ny) for d in range(ny)]
    zs = [lax.rem(z + d, nz) for d in range(nz)]
    steps = [(dy, dz) for dy in range(ny) for dz in range(nz) if dy or dz]
    steps.sort(key=lambda d: -hops(d[0], ny) - hops(d[1], nz))
    proto_peers = [(dy * nz + dz - 1, (b, ys[dy] * nz + zs[dz])) for dy, dz in steps]
    steps = [(dx, dc) for dx in range(nx) for dc in range(2) if dx or dc]
    steps.sort(key=lambda d: -2 * hops(d[0], nx) - d[1])
    batch_peers = [(dx * 2 + dc - 1, (bat(dx, dc), p)) for dx, dc in steps]

    def remote(src, dst, ss, rs, to):
        return pltpu.make_async_remote_copy(
            src, dst, ss, rs, device_id=to, device_id_type=MESH
        )

    sibling = (bat(0, 1), p)

    barrier = pltpu.get_barrier_semaphore()
    for _, to in proto_peers + batch_peers:
        pl.semaphore_signal(barrier, inc=1, device_id=to, device_id_type=MESH)
    mine = rows(b * pl_rows, pl_rows)
    loads = [
        pltpu.make_async_copy(tf_hbm, tf, lsem.at[0]),
        pltpu.make_async_copy(sf_hbm, sf, lsem.at[1]),
        pltpu.make_async_copy(tp_hbm.at[mine], anchor, lsem.at[2]),
        pltpu.make_async_copy(sp_hbm.at[mine], sp, lsem.at[3]),
    ]
    for d in loads:
        d.start()

    def norm_into(src, dst, start, count):
        def body(i):
            unit, _ = unit_rows(src[rows(i * 128, 128), :])
            dst[rows(start + i * 128, 128), :] = unit.astype(BF)

        loop(count // 128, body)

    loads[0].wait()
    norm_into(tf, t_all, b * tl, tl)
    pl.semaphore_wait(barrier, nb + nq - 2)

    feats = (t_all, s_all)

    def near_copy(f, dx, h):
        part = feats[f].at[rows(b * tl + h * (tl // 2), tl // 2)]
        return remote(
            part, part, near_s.at[f, dx, h], near_r.at[f, dx, h], (bat(dx, 0), p)
        )

    def near_forward(f, dx, h):
        part = feats[f].at[rows(bat(nx - dx, 0) * tl + h * (tl // 2), tl // 2)]
        return remote(
            part, part, nfwd_s.at[f, dx, h], nfwd_r.at[f, dx, h], sibling
        )

    def token_copy(f, dx):
        start, size = b * tl, tl
        if dx == far_dx:
            start, size = b * tl + p * piece, piece
        part = feats[f].at[rows(start, size)]
        to = sibling if dx == 0 else (bat(dx, 0), p)
        return remote(part, part, tok_s.at[f, dx], tok_r.at[f, dx], to)

    def spread(f, to):
        part = feats[f].at[rows(bat(nx - far_dx, 0) * tl + p * piece, piece)]
        return remote(part, part, spr_s.at[f], spr_r.at[f], to)

    def spread_all(f):
        part = feats[f].at[0 : tl - piece]
        return remote(part, part, spr_s.at[f], spr_r.at[f], sibling)

    def forward(f, dx):
        block = feats[f].at[rows(bat(nx - dx, 0) * tl, tl)]
        return remote(block, block, fwd_s.at[f, dx], fwd_r.at[f, dx], sibling)

    near = (1, nx - 1)

    def tokens_send(f):
        token_copy(f, far_dx).start()
        token_copy(f, 0).start()
        for h in range(2):
            for dx in near:
                near_copy(f, dx, h).start()

    def spread_start(f):
        token_copy(f, far_dx).wait_recv()
        for _, to in proto_peers:
            spread(f, to).start()

    def spread_end(f):
        spread_all(f).wait_recv()
        forward(f, far_dx).start()

    def near_part(f, h):
        for dx in near:
            near_copy(f, dx, h).wait_recv()
            near_forward(f, dx, h).start()

    def tokens_drain(f):
        token_copy(f, far_dx).wait_send()
        token_copy(f, 0).wait_send()
        forward(f, far_dx).wait_send()
        for h in range(2):
            for dx in near:
                if f:
                    near_copy(f, dx, h).wait_send()
                near_forward(f, dx, h).wait_send()
        spread_all(f).wait_send()

    tokens_send(0)
    loads[2].wait()
    norm_into(anchor, anchor, 0, pl_rows)

    def exp_block(left, right, out, block, width, factor, accumulate, first):
        cols = pl.ds(pl.multiple_of(block * tl, width), width)

        def body(i):
            sl = rows(i * 256, 256)
            value = jnp.exp2(nt(left[sl, :], right[cols, :]) * factor)
            out[sl, cols] = value.astype(BF)
            accumulate(value, sl, cols, width, first)

        loop(pl_rows // 256, body)

    def col_acc(value, sl, cols, width, first):
        acc = value[:, 0:128]
        for q in range(1, width // 128):
            acc = acc + value[:, q * 128 : (q + 1) * 128]
        if first:
            cs[sl, :] = acc
        else:
            cs[sl, :] += acc

    def row_acc(value, sl, cols, width, first):
        tot[:, cols] += jnp.sum(value.reshape(32, 8, width), axis=0)

    def chip_block(dx):
        return lax.rem(x + nx - dx, nx) * 2

    def teacher_block(block, width, first=False):
        exp_block(anchor, t_all, e, block, width, LOG2E / teacher_temp, col_acc, first)

    def student_plane(dx):
        if dx == far_dx:
            forward(1, dx).wait_recv()
        elif dx:
            for h in range(2):
                near_forward(1, dx, h).wait_recv()
        else:
            token_copy(1, 0).wait_recv()
        exp_block(
            pu, s_all, s, chip_block(dx), plane, LOG2E / student_temp, row_acc, False
        )

    loads[1].wait()
    norm_into(sf, s_all, b * tl, tl)
    spread_start(0)
    token_copy(0, 0).wait_recv()
    teacher_block(chip_block(0), plane, True)
    loads[3].wait()

    def norm_protos(i):
        sl = rows(i * 128, 128)
        unit, _ = unit_rows(sp[sl, :])
        pu[sl, :] = unit.astype(BF)
        put[:, sl] = unit.T.astype(BF)

    near_part(0, 0)
    loop(pl_rows // 128, norm_protos)
    tot[...] = jnp.zeros_like(tot)
    for h in range(2):
        for dx in near:
            near_copy(0, dx, h).wait_send()
    tokens_send(1)
    spread_end(0)
    near_part(0, 1)
    for dx in near:
        teacher_block(chip_block(dx) + c, tl)
    forward(0, far_dx).wait_recv()
    teacher_block(chip_block(far_dx), plane)
    for dx in near:
        for h in range(2):
            near_forward(0, dx, h).wait_recv()
        teacher_block(chip_block(dx) + 1 - c, tl)
    half = lax.broadcasted_iota(jnp.int32, (16, 128), 0) < 8

    def split_into(dst, j, row):
        high = row.astype(BF).astype(F32)
        dst[:, j * 128 : (j + 1) * 128] = jnp.where(half, high, row - high).astype(BF)

    def first_step(n, slot, to):
        return remote(w_src.at[n], w_g1.at[n, slot], a1_s.at[n], a1_r.at[n], to)

    def second_step(n, slot, to):
        return remote(w_mid.at[n], w_g2.at[n, slot], a2_s.at[n], a2_r.at[n], to)

    def first_all(n):
        return remote(w_g1.at[n], w_g1.at[n], a1_s.at[n], a1_r.at[n], sibling)

    def second_all(n):
        return remote(w_g2.at[n], w_g2.at[n], a2_s.at[n], a2_r.at[n], sibling)

    def reduce_start(n):
        for slot, to in batch_peers:
            first_step(n, slot, to).start()

    def reduce_middle(n):
        first_all(n).wait_recv()
        value = w_src[n]
        for j in range(nb - 1):
            value = value + w_g1[n, j]
        w_mid[n] = value.astype(BF)
        for slot, to in proto_peers:
            second_step(n, slot, to).start()

    def reduce_end(n):
        second_all(n).wait_recv()
        value = w_mid[n].astype(F32)
        for j in range(nq - 1):
            value = value + w_g2[n, j].astype(F32)
        return value

    def spread_rows(k, weights):
        for j in range(wide):
            w_row[k, :, j * 128 : (j + 1) * 128] = jnp.broadcast_to(
                weights[j : j + 1, :], (8, 128)
            )

    def row_pass(n):
        out = nn(c16[...], e[...])
        line = out[0:1, :] + out[8:9, :]
        for j in range(wide):
            w_src[n, j : j + 1, :] = line[:, j * 128 : (j + 1) * 128]

    def col_pass(weights):
        for j in range(wide):
            split_into(r16, j, weights[j : j + 1, :])
        out = nt(r16[...], e[...])
        line = 1.0 / (protos * (out[0:1, :] + out[8:9, :]))
        return [line[:, j * 128 : (j + 1) * 128] for j in range(pl_rows // 128)]

    def feat_copy(buf, to, ss, rs, xx):
        return remote(buf.at[xx], to.at[xx], ss.at[xx], rs.at[xx], sibling)

    def feat_out(left, right, buf, to, ss, rs):
        def body(xx):
            cols = rows((xx * 2 + 1 - c) * tl, tl)
            buf[xx] = nn(left[...], right[:, cols]).astype(BF)
            feat_copy(buf, to, ss, rs, xx).start()

        loop(nx, body)

    def feat_own(left, right, out):
        def body(xx):
            cols = rows((xx * 2 + c) * tl, tl)
            out[xx] = nn(left[...], right[:, cols])

        loop(nx, body)

    for j in range(pl_rows // 128):
        sums = jnp.sum(cs[j * 128 : (j + 1) * 128, :].T, axis=0, keepdims=True)
        split_into(c16, j, 1.0 / (protos * sums))
    row_pass(0)
    reduce_start(0)
    spread_start(1)
    student_plane(0)
    reduce_middle(0)
    near_part(1, 0)
    near_part(1, 1)
    spread_end(1)
    student_plane(near[0])
    student_plane(near[1])
    student_plane(far_dx)
    tokens_drain(0)
    weights = 1.0 / (tokens * reduce_end(0))
    for j, line in enumerate(col_pass(weights)):
        split_into(c16, j, line)
    row_pass(1)
    reduce_start(1)
    feat_out(put, s, oa, ra, ra_s, ra_r)
    reduce_middle(1)
    line = jnp.sum(tot[...], axis=0, keepdims=True)
    for j in range(wide):
        w_src[ITERS, j : j + 1, :] = line[:, j * 128 : (j + 1) * 128]
    reduce_start(ITERS)
    feat_own(put, s, fa)
    weights = 1.0 / (tokens * reduce_end(1))
    lines = col_pass(weights)
    for j, line in enumerate(lines):
        split_into(c16, j, line)
    row_pass(2)
    reduce_start(2)
    reduce_middle(ITERS)
    for j, line in enumerate(lines):
        sl = slice(j * 128, (j + 1) * 128)
        anct[:, sl] = (put[:, sl].astype(F32) * line).astype(BF)
    feat_out(anct, e, ob, rb, rb_s, rb_r)
    reduce_middle(2)
    feat_own(anct, e, fb)
    spread_rows(1, 1.0 / (student_temp * tokens * reduce_end(ITERS)))
    for j, line in enumerate(lines):
        ccol[j * 128 : (j + 1) * 128, :] = jnp.broadcast_to(line, (128, 128)).T


    tokens_drain(1)
    for xx in range(nx):
        feat_copy(oa, ra, ra_s, ra_r, xx).wait()
        feat_copy(ob, rb, rb_s, rb_r, xx).wait()
    spread_rows(0, (1.0 / student_temp) / (tokens * reduce_end(2)))

    span = 2 * CH
    groups = pl_rows // span

    def chunk_send(q, k):
        to = (bat(1, 0), p) if k == 0 else (bat(nx - 1, 0), p)
        part = gp_out.at[rows(b * pl_rows + q * CH, CH)]
        return remote(part, part, out_s.at[0], g_r.at[k, q], to)

    def group_forward(g, k):
        block = bat(nx - 1, 0) if k == 0 else bat(1, 0)
        to = (bat(1, 0), p) if k == 0 else (bat(nx - 1, 0), p)
        part = gp_out.at[rows(block * pl_rows + g * span + k * CH, CH)]
        return remote(part, part, out_s.at[0], f_r.at[k, g], to)

    def group_sibling(g, k):
        block = bat((nx - 1, 1, 2)[k], 0)
        part = gp_out.at[rows(block * pl_rows + g * span, span)]
        return remote(part, part, out_s.at[0], sib_r.at[0], sibling)

    def own_sibling():
        part = gp_out.at[rows(b * pl_rows, pl_rows)]
        return remote(part, part, out_s.at[0], sib_r.at[0], sibling)

    def chunk_compute(q):
        sl = rows(q * CH, CH)
        weight = ccol[sl, 0:1]
        for j in range(tokens // 512):
            js = slice(j * 512, (j + 1) * 512)
            value = s[sl, js].astype(F32) * w_row[1, 0:1, js]
            value = value - e[sl, js].astype(F32) * (w_row[0, 0:1, js] * weight)
            delta[:, js] = value.astype(BF)
        back = nn(delta[...], s_all[...])
        unit, scale = unit_rows(sp[sl, :])
        value = back_norm(back, unit, scale).astype(BF)
        gp_out[rows(b * pl_rows + q * CH, CH), :] = value
        chunk_send(q, 0).start()
        chunk_send(q, 1).start()

    def group_recv(g):
        for k in range(2):
            chunk_send(2 * g, k).wait_recv()
            chunk_send(2 * g + 1, k).wait_recv()
            group_forward(g, k).start()
            group_sibling(g, k).start()

    def group_last(g):
        for k in range(2):
            group_forward(g, k).wait_recv()
        group_sibling(g, 2).start()

    chunk_compute(0)

    group = tl // 128

    def combine(i):
        xx, g = i // group, lax.rem(i, group)
        sl = rows(g * 128, 128)
        at = rows(((xx * 2 + c) * group + g) * 128, 128)
        value = (fa[xx, :, sl] + ra[xx, :, sl].astype(F32)) * w_row[1, 0:1, at]
        value = value - (fb[xx, :, sl] + rb[xx, :, sl].astype(F32)) * w_row[0, 0:1, at]
        cx[xx, g] = value.T.astype(BF).reshape(nz, piece, depth)

    loop(nx * group, combine)
    def feat_send(src, dst, ss, rs, to):
        remote(src, dst, ss, rs, to).start()

    def whole(buf, ss, rs):
        return remote(buf, buf, ss.at[0], rs.at[0], sibling)

    first = [whole(b1y, y1_s, y1_r), whole(b1z, z1_s, z1_r)]
    second = [whole(b2y, z2_s, z2_r), whole(b2z, y2_s, y2_r)]
    third = whole(xr, xr_s, xr_r)
    final = remote(
        gs_out.at[0 : tl - piece], gs_out.at[0 : tl - piece],
        gs_s.at[0], gs_r.at[0], sibling,
    )

    def along_y(d):
        return lax.rem(y + d, ny)

    def along_z(d):
        return lax.rem(z + d, nz)

    for d in range(1, ny):
        feat_send(cx.at[0:hx, along_y(d)], b1y.at[d - 1], y1_s.at[0],
                  y1_r.at[0], (b, along_y(d) * nz + z))
    for d in range(1, nz):
        feat_send(cx.at[hx:nx, :, along_z(d)], b1z.at[d - 1], z1_s.at[0],
                  z1_r.at[0], (b, y * nz + along_z(d)))

    def feat_middle():
        for d in first:
            d.wait_recv()
        for h in range(hx):
            value = cx[h, y].astype(F32)
            for d in range(ny - 1):
                value = value + b1y[d, h].astype(F32)
            c2y[h] = value.astype(BF)
            value = cx[hx + h, :, z].astype(F32)
            for d in range(nz - 1):
                value = value + b1z[d, h].astype(F32)
            c2z[h] = value.astype(BF)
        for d in range(1, nz):
            feat_send(c2y.at[:, along_z(d)], b2y.at[d - 1], z2_s.at[0],
                      z2_r.at[0], (b, y * nz + along_z(d)))
        for d in range(1, ny):
            feat_send(c2z.at[:, along_y(d)], b2z.at[d - 1], y2_s.at[0],
                      y2_r.at[0], (b, along_y(d) * nz + z))

    def feat_x():
        for d in second:
            d.wait_recv()
        value = c2y[:, z].astype(F32)
        for d in range(nz - 1):
            value = value + b2y[d].astype(F32)
        sumf[0:hx] = value
        xs[0:hx] = value.astype(BF)
        value = c2z[:, y].astype(F32)
        for d in range(ny - 1):
            value = value + b2z[d].astype(F32)
        sumf[hx:nx] = value
        xs[hx:nx] = value.astype(BF)
        for dx in range(1, nx):
            feat_send(xs.at[lax.rem(x + dx, nx)], xr.at[dx - 1],
                      xr_s.at[0], xr_r.at[0], (bat(dx, 0), p))

    def feat_last():
        third.wait_recv()
        value = sumf[x]
        for dx in range(nx - 1):
            value = value + xr[dx].astype(F32)
        own = rows(p * piece, piece)
        unit, scale = unit_rows(sf[own, :])
        gs_out[own, :] = back_norm(value, unit, scale).astype(BF)
        part = gs_out.at[own]
        for _, to in proto_peers:
            feat_send(part, part, gs_s.at[0], gs_r.at[0], to)

    loop(chunks - 1, lambda q: chunk_compute(q + 1))
    own_sibling().start()
    feat_middle()
    feat_x()
    loop(groups - 1, group_recv)
    feat_last()
    group_recv(groups - 1)
    loop(groups, group_last)

    for n in range(ITERS + 1):
        first_all(n).wait_send()
        second_all(n).wait_send()
    for d in first + second + [third, final]:
        d.wait_send()
    sent = gp_out.at[0 : pl_rows * (nx + 3)]
    remote(sent, sent, out_s.at[0], sib_r.at[0], sibling).wait_send()
    held = gp_out.at[0 : pl_rows * nx]
    remote(held, held, out_s.at[0], sib_r.at[0], sibling).wait_recv()
    final.wait_recv()


def on_device(nb, nq, student_feats, teacher_feats, student_protos, teacher_protos):
    tl, depth = student_feats.shape
    pl_rows = student_protos.shape[0] // nb
    tokens = tl * nb
    chunks = pl_rows // CH
    wide = tokens // 128
    nx = nb // 2
    piece = tl // nq
    vm = pltpu.VMEM
    dma = pltpu.SemaphoreType.DMA
    hx, nz = nx // 2, NZ
    ny = nq // nz
    scratch = [
        vm((tl, depth), BF),
        vm((tl, depth), BF),
        vm((tokens, depth), BF),
        vm((tokens, depth), BF),
        vm((pl_rows, depth), BF),
        vm((pl_rows, depth), BF),
        vm((pl_rows, depth), BF),
        vm((pl_rows, tokens), BF),
        vm((pl_rows, tokens), BF),
        vm((pl_rows, 128), F32),
        vm((8, tokens), F32),
        vm((nx, depth, tl), F32),
        vm((nx, depth, tl), F32),
        vm((nx, depth, tl), BF),
        vm((nx, depth, tl), BF),
        vm((nx, depth, tl), BF),
        vm((nx, depth, tl), BF),
        vm((depth, pl_rows), BF),
        vm((depth, pl_rows), BF),
        vm((pl_rows, 128), F32),
        vm((16, tokens), BF),
        vm((16, pl_rows), BF),
        vm((ITERS + 1, wide, 128), F32),
        vm((ITERS + 1, wide, 128), BF),
        vm((ITERS + 1, nb - 1, wide, 128), F32),
        vm((ITERS + 1, nq - 1, wide, 128), BF),
        vm((2, 8, tokens), F32),
        vm((CH, tokens), BF),
        vm((nx, ny, nz, piece, depth), BF),
        vm((ny - 1, hx, nz, piece, depth), BF),
        vm((nz - 1, hx, ny, piece, depth), BF),
        vm((hx, nz, piece, depth), BF),
        vm((hx, ny, piece, depth), BF),
        vm((nz - 1, hx, piece, depth), BF),
        vm((ny - 1, hx, piece, depth), BF),
        vm((nx, piece, depth), F32),
        vm((nx, piece, depth), BF),
        vm((nx - 1, piece, depth), BF),
        dma((4,)),
        dma((2, nx, 2)), dma((2, nx, 2)), dma((2, nx, 2)), dma((2, nx, 2)),
        dma((2, nx)), dma((2, nx)), dma((2, nx)), dma((2, nx)),
        dma((2,)), dma((2,)),
        dma((ITERS + 1,)), dma((ITERS + 1,)),
        dma((ITERS + 1,)), dma((ITERS + 1,)),
        dma((1,)), dma((2, chunks)), dma((2, chunks // 2)), dma((1,)),
        dma((nx,)), dma((nx,)), dma((nx,)), dma((nx,)),
        dma((1,)), dma((1,)), dma((1,)), dma((1,)), dma((1,)), dma((1,)),
        dma((1,)), dma((1,)), dma((1,)), dma((1,)), dma((1,)), dma((1,)),
    ]
    in_vmem = pl.BlockSpec(memory_space=pltpu.VMEM)
    anywhere = pl.BlockSpec(memory_space=pl.ANY)
    return pl.pallas_call(
        functools.partial(kernel, nb, nq),
        out_shape=[
            pltpu.VMEM(student_protos.shape, BF),
            pltpu.VMEM(student_feats.shape, BF),
        ],
        in_specs=[anywhere] * 4,
        out_specs=[in_vmem, in_vmem],
        scratch_shapes=scratch,
        compiler_params=pltpu.CompilerParams(
            collective_id=0, has_side_effects=True, vmem_limit_bytes=54 << 20
        ),
        name="prototype_head",
    )(student_feats, teacher_feats, student_protos, teacher_protos)


def solution(mesh):
    nb, nq = mesh.shape["batch"], mesh.shape["proto"]
    in_specs = (P("batch", None), P("batch", None), P("proto", None), P("proto", None))
    out_specs = (P("proto", None), P("batch", None))
    return jax.shard_map(
        functools.partial(on_device, nb, nq),
        mesh=mesh, in_specs=in_specs, out_specs=out_specs, check_vma=False,
    )
```

```python
import functools

import jax
import jax.numpy as jnp
from jax import lax
from jax.experimental import pallas as pl
from jax.experimental.pallas import tpu as pltpu
from jax.sharding import PartitionSpec as P

ITERS = 3
eps = 1e-06
teacher_temp = 0.04
student_temp = 0.1
LOG2E = 1.4426950408889634
F32 = jnp.float32
BF = jnp.bfloat16
MESH = pl.DeviceIdType.MESH
CH = 128
NZ = 4


def nt(left, right):
    return lax.dot_general(
        left, right, (((1,), (1,)), ((), ())), preferred_element_type=F32
    )


def nn(left, right):
    return jnp.dot(left, right, preferred_element_type=F32)


def tn(left, right):
    return lax.dot_general(
        left, right, (((0,), (0,)), ((), ())), preferred_element_type=F32
    )


def loop(count, body):
    def step(i, carry):
        body(i)
        return carry

    lax.fori_loop(0, count, step, 0)


def rows(start, size):
    return pl.ds(pl.multiple_of(start, size), size)


def unit_rows(values):
    values = values.astype(F32)
    scale = lax.rsqrt(jnp.sum(values * values, axis=1, keepdims=True) + eps)
    return values * scale, scale


def back_norm(grad, unit, scale):
    return scale * (grad - unit * jnp.sum(grad * unit, axis=1, keepdims=True))


def kernel(
    nb, nq,
    sf_hbm, tf_hbm, sp_hbm, tp_hbm,
    gp_out, gs_out,
    sf, tf, t_all, s_all, sp, anchor, pu, e, s, cs, tot, fa, fb, ra, rb, oa, ob, put, anct, ccol,
    r16, c16, w_src, w_mid, w_g1, w_g2, w_row, delta, cx, b1y, b1z, c2y, c2z, b2y, b2z, sumf, xs, xr,
    lsem, near_s, near_r, nfwd_s, nfwd_r, tok_s, tok_r, fwd_s, fwd_r, spr_s, spr_r,
    a1_s, a1_r, a2_s, a2_r, out_s, g_r, f_r, sib_r,
    ra_s, ra_r, rb_s, rb_r, y1_s, y1_r, z1_s, z1_r, y2_s, y2_r, z2_s, z2_r, xr_s, xr_r, gs_s, gs_r,
):
    nx = nb // 2
    far_dx = nx // 2
    hx = nx // 2
    nz = NZ
    ny = nq // nz
    tl, depth = sf.shape
    tokens = tl * nb
    pl_rows = sp.shape[0]
    protos = pl_rows * nb * nq
    chunks = pl_rows // CH
    wide = tokens // 128
    piece = tl // nq
    plane = 2 * tl
    b, p = lax.axis_index("batch"), lax.axis_index("proto")
    x, c = b // 2, lax.rem(b, 2)
    y, z = p // nz, lax.rem(p, nz)

    def bat(dx, dc):
        return lax.rem(x + dx, nx) * 2 + lax.rem(c + dc, 2)

    def hops(d, n):
        return min(d, n - d)

    ys = [lax.rem(y + d, ny) for d in range(ny)]
    zs = [lax.rem(z + d, nz) for d in range(nz)]
    steps = [(dy, dz) for dy in range(ny) for dz in range(nz) if dy or dz]
    steps.sort(key=lambda d: -hops(d[0], ny) - hops(d[1], nz))
    proto_peers = [(dy * nz + dz - 1, (b, ys[dy] * nz + zs[dz])) for dy, dz in steps]
    steps = [(dx, dc) for dx in range(nx) for dc in range(2) if dx or dc]
    steps.sort(key=lambda d: -2 * hops(d[0], nx) - d[1])
    batch_peers = [(dx * 2 + dc - 1, (bat(dx, dc), p)) for dx, dc in steps]

    def remote(src, dst, ss, rs, to):
        return pltpu.make_async_remote_copy(
            src, dst, ss, rs, device_id=to, device_id_type=MESH
        )

    sibling = (bat(0, 1), p)

    barrier = pltpu.get_barrier_semaphore()
    for _, to in proto_peers + batch_peers:
        pl.semaphore_signal(barrier, inc=1, device_id=to, device_id_type=MESH)
    mine = rows(b * pl_rows, pl_rows)
    loads = [
        pltpu.make_async_copy(tf_hbm, tf, lsem.at[0]),
        pltpu.make_async_copy(sf_hbm, sf, lsem.at[1]),
        pltpu.make_async_copy(tp_hbm.at[mine], anchor, lsem.at[2]),
        pltpu.make_async_copy(sp_hbm.at[mine], sp, lsem.at[3]),
    ]
    for d in loads:
        d.start()

    def norm_into(src, dst, start, count):
        def body(i):
            unit, _ = unit_rows(src[rows(i * 128, 128), :])
            dst[rows(start + i * 128, 128), :] = unit.astype(BF)

        loop(count // 128, body)

    loads[0].wait()
    norm_into(tf, t_all, b * tl, tl)
    pl.semaphore_wait(barrier, nb + nq - 2)

    feats = (t_all, s_all)

    def near_copy(f, dx, h):
        part = feats[f].at[rows(b * tl + h * (tl // 2), tl // 2)]
        return remote(
            part, part, near_s.at[f, dx, h], near_r.at[f, dx, h], (bat(dx, 0), p)
        )

    def near_forward(f, dx, h):
        part = feats[f].at[rows(bat(nx - dx, 0) * tl + h * (tl // 2), tl // 2)]
        return remote(
            part, part, nfwd_s.at[f, dx, h], nfwd_r.at[f, dx, h], sibling
        )

    def token_copy(f, dx):
        start, size = b * tl, tl
        if dx == far_dx:
            start, size = b * tl + p * piece, piece
        part = feats[f].at[rows(start, size)]
        to = sibling if dx == 0 else (bat(dx, 0), p)
        return remote(part, part, tok_s.at[f, dx], tok_r.at[f, dx], to)

    def spread(f, to):
        part = feats[f].at[rows(bat(nx - far_dx, 0) * tl + p * piece, piece)]
        return remote(part, part, spr_s.at[f], spr_r.at[f], to)

    def spread_all(f):
        part = feats[f].at[0 : tl - piece]
        return remote(part, part, spr_s.at[f], spr_r.at[f], sibling)

    def forward(f, dx):
        block = feats[f].at[rows(bat(nx - dx, 0) * tl, tl)]
        return remote(block, block, fwd_s.at[f, dx], fwd_r.at[f, dx], sibling)

    near = (1, nx - 1)

    def tokens_send(f):
        token_copy(f, far_dx).start()
        token_copy(f, 0).start()
        for h in range(2):
            for dx in near:
                near_copy(f, dx, h).start()

    def spread_start(f):
        token_copy(f, far_dx).wait_recv()
        for _, to in proto_peers:
            spread(f, to).start()

    def spread_end(f):
        spread_all(f).wait_recv()
        forward(f, far_dx).start()

    def near_part(f, h):
        for dx in near:
            near_copy(f, dx, h).wait_recv()
            near_forward(f, dx, h).start()

    def tokens_drain(f):
        token_copy(f, far_dx).wait_send()
        token_copy(f, 0).wait_send()
        forward(f, far_dx).wait_send()
        for h in range(2):
            for dx in near:
                if f:
                    near_copy(f, dx, h).wait_send()
                near_forward(f, dx, h).wait_send()
        spread_all(f).wait_send()

    tokens_send(0)
    loads[2].wait()
    norm_into(anchor, anchor, 0, pl_rows)

    def exp_block(left, right, out, block, width, factor, accumulate, first):
        cols = pl.ds(pl.multiple_of(block * tl, width), width)

        def body(i):
            sl = rows(i * 256, 256)
            value = jnp.exp2(nt(left[sl, :], right[cols, :]) * factor)
            out[sl, cols] = value.astype(BF)
            accumulate(value, sl, cols, width, first)

        loop(pl_rows // 256, body)

    def col_acc(value, sl, cols, width, first):
        acc = value[:, 0:128]
        for q in range(1, width // 128):
            acc = acc + value[:, q * 128 : (q + 1) * 128]
        if first:
            cs[sl, :] = acc
        else:
            cs[sl, :] += acc

    def row_acc(value, sl, cols, width, first):
        tot[:, cols] += jnp.sum(value.reshape(32, 8, width), axis=0)

    def chip_block(dx):
        return lax.rem(x + nx - dx, nx) * 2

    def teacher_block(block, width, first=False):
        exp_block(anchor, t_all, e, block, width, LOG2E / teacher_temp, col_acc, first)

    def student_block(block, width):
        exp_block(pu, s_all, s, block, width, LOG2E / student_temp, row_acc, False)

    def student_plane(dx):
        if dx == far_dx:
            forward(1, dx).wait_recv()
        elif dx:
            for h in range(2):
                near_forward(1, dx, h).wait_recv()
        else:
            token_copy(1, 0).wait_recv()
        exp_block(
            pu, s_all, s, chip_block(dx), plane, LOG2E / student_temp, row_acc, False
        )

    loads[1].wait()
    norm_into(sf, s_all, b * tl, tl)
    spread_start(0)
    token_copy(0, 0).wait_recv()
    teacher_block(chip_block(0), plane, True)
    loads[3].wait()

    def norm_protos(i):
        sl = rows(i * 128, 128)
        unit, _ = unit_rows(sp[sl, :])
        pu[sl, :] = unit.astype(BF)
        put[:, sl] = unit.T.astype(BF)

    near_part(0, 0)
    loop(pl_rows // 128, norm_protos)
    tot[...] = jnp.zeros_like(tot)
    for h in range(2):
        for dx in near:
            near_copy(0, dx, h).wait_send()
    tokens_send(1)
    spread_end(0)
    near_part(0, 1)
    for dx in near:
        teacher_block(chip_block(dx) + c, tl)
    forward(0, far_dx).wait_recv()
    teacher_block(chip_block(far_dx), plane)
    for dx in near:
        for h in range(2):
            near_forward(0, dx, h).wait_recv()
        teacher_block(chip_block(dx) + 1 - c, tl)
    half = lax.broadcasted_iota(jnp.int32, (16, 128), 0) < 8

    def split_into(dst, j, row):
        high = row.astype(BF).astype(F32)
        dst[:, j * 128 : (j + 1) * 128] = jnp.where(half, high, row - high).astype(BF)

    def first_step(n, slot, to):
        return remote(w_src.at[n], w_g1.at[n, slot], a1_s.at[n], a1_r.at[n], to)

    def second_step(n, slot, to):
        return remote(w_mid.at[n], w_g2.at[n, slot], a2_s.at[n], a2_r.at[n], to)

    def first_all(n):
        return remote(w_g1.at[n], w_g1.at[n], a1_s.at[n], a1_r.at[n], sibling)

    def second_all(n):
        return remote(w_g2.at[n], w_g2.at[n], a2_s.at[n], a2_r.at[n], sibling)

    def reduce_start(n):
        for slot, to in batch_peers:
            first_step(n, slot, to).start()

    def reduce_middle(n):
        first_all(n).wait_recv()
        value = w_src[n]
        for j in range(nb - 1):
            value = value + w_g1[n, j]
        w_mid[n] = value.astype(BF)
        for slot, to in proto_peers:
            second_step(n, slot, to).start()

    def reduce_end(n):
        second_all(n).wait_recv()
        value = w_mid[n].astype(F32)
        for j in range(nq - 1):
            value = value + w_g2[n, j].astype(F32)
        return value

    def spread_rows(k, weights):
        for j in range(wide):
            w_row[k, :, j * 128 : (j + 1) * 128] = jnp.broadcast_to(
                weights[j : j + 1, :], (8, 128)
            )

    def row_pass(n):
        out = nn(c16[...], e[...])
        line = out[0:1, :] + out[8:9, :]
        for j in range(wide):
            w_src[n, j : j + 1, :] = line[:, j * 128 : (j + 1) * 128]

    def col_pass(weights):
        for j in range(wide):
            split_into(r16, j, weights[j : j + 1, :])
        out = nt(r16[...], e[...])
        line = 1.0 / (protos * (out[0:1, :] + out[8:9, :]))
        return [line[:, j * 128 : (j + 1) * 128] for j in range(pl_rows // 128)]

    def feat_copy(buf, to, ss, rs, xx):
        return remote(buf.at[xx], to.at[xx], ss.at[xx], rs.at[xx], sibling)

    def feat_out(left, right, buf, to, ss, rs):
        def body(xx):
            cols = rows((xx * 2 + 1 - c) * tl, tl)
            buf[xx] = nn(left[...], right[:, cols]).astype(BF)
            feat_copy(buf, to, ss, rs, xx).start()

        loop(nx, body)

    def feat_own(left, right, out):
        def body(xx):
            cols = rows((xx * 2 + c) * tl, tl)
            out[xx] = nn(left[...], right[:, cols])

        loop(nx, body)

    for j in range(pl_rows // 128):
        sums = jnp.sum(cs[j * 128 : (j + 1) * 128, :].T, axis=0, keepdims=True)
        split_into(c16, j, 1.0 / (protos * sums))
    row_pass(0)
    reduce_start(0)
    spread_start(1)
    student_plane(0)
    near_part(1, 0)
    reduce_middle(0)
    near_part(1, 1)
    for dx in near:
        student_block(chip_block(dx) + c, tl)
    spread_end(1)
    for dx in near:
        for h in range(2):
            near_forward(1, dx, h).wait_recv()
        student_block(chip_block(dx) + 1 - c, tl)
    student_plane(far_dx)
    tokens_drain(0)
    weights = 1.0 / (tokens * reduce_end(0))
    for j, line in enumerate(col_pass(weights)):
        split_into(c16, j, line)
    row_pass(1)
    reduce_start(1)
    feat_out(put, s, oa, ra, ra_s, ra_r)
    reduce_middle(1)
    line = jnp.sum(tot[...], axis=0, keepdims=True)
    for j in range(wide):
        w_src[ITERS, j : j + 1, :] = line[:, j * 128 : (j + 1) * 128]
    reduce_start(ITERS)
    feat_own(put, s, fa)
    weights = 1.0 / (tokens * reduce_end(1))
    lines = col_pass(weights)
    for j, line in enumerate(lines):
        split_into(c16, j, line)
    row_pass(2)
    reduce_start(2)
    reduce_middle(ITERS)
    for j, line in enumerate(lines):
        sl = slice(j * 128, (j + 1) * 128)
        anct[:, sl] = (put[:, sl].astype(F32) * line).astype(BF)
    feat_out(anct, e, ob, rb, rb_s, rb_r)
    reduce_middle(2)
    feat_own(anct, e, fb)
    spread_rows(1, 1.0 / (student_temp * tokens * reduce_end(ITERS)))
    for j, line in enumerate(lines):
        ccol[j * 128 : (j + 1) * 128, :] = jnp.broadcast_to(line, (128, 128)).T


    tokens_drain(1)
    for xx in range(nx):
        feat_copy(oa, ra, ra_s, ra_r, xx).wait()
        feat_copy(ob, rb, rb_s, rb_r, xx).wait()
    spread_rows(0, (1.0 / student_temp) / (tokens * reduce_end(2)))

    span = 2 * CH
    groups = pl_rows // span

    def chunk_send(q, k):
        to = (bat(1, 0), p) if k == 0 else (bat(nx - 1, 0), p)
        part = gp_out.at[rows(b * pl_rows + q * CH, CH)]
        return remote(part, part, out_s.at[0], g_r.at[k, q], to)

    def group_forward(g, k):
        block = bat(nx - 1, 0) if k == 0 else bat(1, 0)
        to = (bat(1, 0), p) if k == 0 else (bat(nx - 1, 0), p)
        part = gp_out.at[rows(block * pl_rows + g * span + k * CH, CH)]
        return remote(part, part, out_s.at[0], f_r.at[k, g], to)

    def group_sibling(g, k):
        block = bat((nx - 1, 1, 2)[k], 0)
        part = gp_out.at[rows(block * pl_rows + g * span, span)]
        return remote(part, part, out_s.at[0], sib_r.at[0], sibling)

    def own_sibling():
        part = gp_out.at[rows(b * pl_rows, pl_rows)]
        return remote(part, part, out_s.at[0], sib_r.at[0], sibling)

    def chunk_compute(q):
        sl = rows(q * CH, CH)
        weight = ccol[sl, 0:1]
        for j in range(tokens // 512):
            js = slice(j * 512, (j + 1) * 512)
            value = s[sl, js].astype(F32) * w_row[1, 0:1, js]
            value = value - e[sl, js].astype(F32) * (w_row[0, 0:1, js] * weight)
            delta[:, js] = value.astype(BF)
        back = nn(delta[...], s_all[...])
        unit, scale = unit_rows(sp[sl, :])
        value = back_norm(back, unit, scale).astype(BF)
        gp_out[rows(b * pl_rows + q * CH, CH), :] = value
        chunk_send(q, 0).start()
        chunk_send(q, 1).start()

    def group_recv(g):
        for k in range(2):
            chunk_send(2 * g, k).wait_recv()
            chunk_send(2 * g + 1, k).wait_recv()
            group_forward(g, k).start()
            group_sibling(g, k).start()

    def group_last(g):
        for k in range(2):
            group_forward(g, k).wait_recv()
        group_sibling(g, 2).start()

    loop(2, chunk_compute)

    group = tl // 128

    def combine(i):
        xx, g = i // group, lax.rem(i, group)
        sl = rows(g * 128, 128)
        at = rows(((xx * 2 + c) * group + g) * 128, 128)
        value = (fa[xx, :, sl] + ra[xx, :, sl].astype(F32)) * w_row[1, 0:1, at]
        value = value - (fb[xx, :, sl] + rb[xx, :, sl].astype(F32)) * w_row[0, 0:1, at]
        cx[xx, g] = value.T.astype(BF).reshape(nz, piece, depth)

    loop(nx * group, combine)
    def feat_send(src, dst, ss, rs, to):
        remote(src, dst, ss, rs, to).start()

    def whole(buf, ss, rs):
        return remote(buf, buf, ss.at[0], rs.at[0], sibling)

    first = [whole(b1y, y1_s, y1_r), whole(b1z, z1_s, z1_r)]
    second = [whole(b2y, z2_s, z2_r), whole(b2z, y2_s, y2_r)]
    third = whole(xr, xr_s, xr_r)
    final = remote(
        gs_out.at[0 : tl - piece], gs_out.at[0 : tl - piece],
        gs_s.at[0], gs_r.at[0], sibling,
    )

    def along_y(d):
        return lax.rem(y + d, ny)

    def along_z(d):
        return lax.rem(z + d, nz)

    for d in range(1, ny):
        feat_send(cx.at[0:hx, along_y(d)], b1y.at[d - 1], y1_s.at[0],
                  y1_r.at[0], (b, along_y(d) * nz + z))
    for d in range(1, nz):
        feat_send(cx.at[hx:nx, :, along_z(d)], b1z.at[d - 1], z1_s.at[0],
                  z1_r.at[0], (b, y * nz + along_z(d)))

    def feat_middle():
        for d in first:
            d.wait_recv()
        for h in range(hx):
            value = cx[h, y].astype(F32)
            for d in range(ny - 1):
                value = value + b1y[d, h].astype(F32)
            c2y[h] = value.astype(BF)
            value = cx[hx + h, :, z].astype(F32)
            for d in range(nz - 1):
                value = value + b1z[d, h].astype(F32)
            c2z[h] = value.astype(BF)
        for d in range(1, nz):
            feat_send(c2y.at[:, along_z(d)], b2y.at[d - 1], z2_s.at[0],
                      z2_r.at[0], (b, y * nz + along_z(d)))
        for d in range(1, ny):
            feat_send(c2z.at[:, along_y(d)], b2z.at[d - 1], y2_s.at[0],
                      y2_r.at[0], (b, along_y(d) * nz + z))

    def feat_x():
        for d in second:
            d.wait_recv()
        value = c2y[:, z].astype(F32)
        for d in range(nz - 1):
            value = value + b2y[d].astype(F32)
        sumf[0:hx] = value
        xs[0:hx] = value.astype(BF)
        value = c2z[:, y].astype(F32)
        for d in range(ny - 1):
            value = value + b2z[d].astype(F32)
        sumf[hx:nx] = value
        xs[hx:nx] = value.astype(BF)
        for dx in range(1, nx):
            feat_send(xs.at[lax.rem(x + dx, nx)], xr.at[dx - 1],
                      xr_s.at[0], xr_r.at[0], (bat(dx, 0), p))

    def feat_last():
        third.wait_recv()
        value = sumf[x]
        for dx in range(nx - 1):
            value = value + xr[dx].astype(F32)
        own = rows(p * piece, piece)
        unit, scale = unit_rows(sf[own, :])
        gs_out[own, :] = back_norm(value, unit, scale).astype(BF)
        part = gs_out.at[own]
        for _, to in proto_peers:
            feat_send(part, part, gs_s.at[0], gs_r.at[0], to)

    loop(chunks - 2, lambda q: chunk_compute(q + 2))
    own_sibling().start()
    feat_middle()
    feat_x()
    loop(groups - 1, group_recv)
    feat_last()
    group_recv(groups - 1)
    loop(groups, group_last)

    for n in range(ITERS + 1):
        first_all(n).wait_send()
        second_all(n).wait_send()
    for d in first + second + [third, final]:
        d.wait_send()
    sent = gp_out.at[0 : pl_rows * (nx + 3)]
    remote(sent, sent, out_s.at[0], sib_r.at[0], sibling).wait_send()
    held = gp_out.at[0 : pl_rows * nx]
    remote(held, held, out_s.at[0], sib_r.at[0], sibling).wait_recv()
    final.wait_recv()


def on_device(nb, nq, student_feats, teacher_feats, student_protos, teacher_protos):
    tl, depth = student_feats.shape
    pl_rows = student_protos.shape[0] // nb
    tokens = tl * nb
    chunks = pl_rows // CH
    wide = tokens // 128
    nx = nb // 2
    piece = tl // nq
    vm = pltpu.VMEM
    dma = pltpu.SemaphoreType.DMA
    hx, nz = nx // 2, NZ
    ny = nq // nz
    scratch = [
        vm((tl, depth), BF),
        vm((tl, depth), BF),
        vm((tokens, depth), BF),
        vm((tokens, depth), BF),
        vm((pl_rows, depth), BF),
        vm((pl_rows, depth), BF),
        vm((pl_rows, depth), BF),
        vm((pl_rows, tokens), BF),
        vm((pl_rows, tokens), BF),
        vm((pl_rows, 128), F32),
        vm((8, tokens), F32),
        vm((nx, depth, tl), F32),
        vm((nx, depth, tl), F32),
        vm((nx, depth, tl), BF),
        vm((nx, depth, tl), BF),
        vm((nx, depth, tl), BF),
        vm((nx, depth, tl), BF),
        vm((depth, pl_rows), BF),
        vm((depth, pl_rows), BF),
        vm((pl_rows, 128), F32),
        vm((16, tokens), BF),
        vm((16, pl_rows), BF),
        vm((ITERS + 1, wide, 128), F32),
        vm((ITERS + 1, wide, 128), BF),
        vm((ITERS + 1, nb - 1, wide, 128), F32),
        vm((ITERS + 1, nq - 1, wide, 128), BF),
        vm((2, 8, tokens), F32),
        vm((CH, tokens), BF),
        vm((nx, ny, nz, piece, depth), BF),
        vm((ny - 1, hx, nz, piece, depth), BF),
        vm((nz - 1, hx, ny, piece, depth), BF),
        vm((hx, nz, piece, depth), BF),
        vm((hx, ny, piece, depth), BF),
        vm((nz - 1, hx, piece, depth), BF),
        vm((ny - 1, hx, piece, depth), BF),
        vm((nx, piece, depth), F32),
        vm((nx, piece, depth), BF),
        vm((nx - 1, piece, depth), BF),
        dma((4,)),
        dma((2, nx, 2)), dma((2, nx, 2)), dma((2, nx, 2)), dma((2, nx, 2)),
        dma((2, nx)), dma((2, nx)), dma((2, nx)), dma((2, nx)),
        dma((2,)), dma((2,)),
        dma((ITERS + 1,)), dma((ITERS + 1,)),
        dma((ITERS + 1,)), dma((ITERS + 1,)),
        dma((1,)), dma((2, chunks)), dma((2, chunks // 2)), dma((1,)),
        dma((nx,)), dma((nx,)), dma((nx,)), dma((nx,)),
        dma((1,)), dma((1,)), dma((1,)), dma((1,)), dma((1,)), dma((1,)),
        dma((1,)), dma((1,)), dma((1,)), dma((1,)), dma((1,)), dma((1,)),
    ]
    in_vmem = pl.BlockSpec(memory_space=pltpu.VMEM)
    anywhere = pl.BlockSpec(memory_space=pl.ANY)
    return pl.pallas_call(
        functools.partial(kernel, nb, nq),
        out_shape=[
            pltpu.VMEM(student_protos.shape, BF),
            pltpu.VMEM(student_feats.shape, BF),
        ],
        in_specs=[anywhere] * 4,
        out_specs=[in_vmem, in_vmem],
        scratch_shapes=scratch,
        compiler_params=pltpu.CompilerParams(
            collective_id=0, has_side_effects=True, vmem_limit_bytes=54 << 20
        ),
        name="prototype_head",
    )(student_feats, teacher_feats, student_protos, teacher_protos)


def solution(mesh):
    nb, nq = mesh.shape["batch"], mesh.shape["proto"]
    in_specs = (P("batch", None), P("batch", None), P("proto", None), P("proto", None))
    out_specs = (P("proto", None), P("batch", None))
    return jax.shard_map(
        functools.partial(on_device, nb, nq),
        mesh=mesh, in_specs=in_specs, out_specs=out_specs, check_vma=False,
    )
```
